32 devices in a mesh: dp: 8 (over z, y), expert: 4 (over x, core).
Axes of the slice: x: 2, y: 2, z: 4, core: 2. Of those that a mesh axis runs over, the one named last changes fastest.
Arguments:
- source: bfloat16 [8, 1024, 512], P('dp', 'expert'), may hold values from -6 to 6
- target: bfloat16 [8, 1024, 512], P('dp', 'expert'), may hold values from -6 to 6
- attention_in: bfloat16 [3, 512, 1536], replicated, may hold values from -0.25 to 0.25
- attention_out: bfloat16 [3, 512, 512], replicated, may hold values from -3 to 3
- norm_gains: float32 [6, 512], replicated, may hold values from 0.5 to 1.5
- encoder_up: bfloat16 [16, 2048, 512], P('expert'), may hold values from -0.25 to 0.25
- encoder_down: bfloat16 [16, 2048, 512], P('expert'), may hold values from -0.1875 to 0.1875
- decoder_up: bfloat16 [16, 2048, 512], P('expert'), may hold values from -0.25 to 0.25
- decoder_down: bfloat16 [16, 2048, 512], P('expert'), may hold values from -0.1875 to 0.1875
- encoder_route: int32 [2, 8, 1024], P(None, 'dp', 'expert'), may hold values from 0 to 15, as said below
- encoder_slot: int32 [2, 8, 1024], P(None, 'dp', 'expert'), may hold values from 0 to 31, as said below
- decoder_route: int32 [2, 8, 1024], P(None, 'dp', 'expert'), may hold values from 0 to 15, as said below
- decoder_slot: int32 [2, 8, 1024], P(None, 'dp', 'expert'), may hold values from 0 to 31, as said below
- output_grad: float32 [2, 8, 1024, 512], P(None, 'dp', 'expert'), may hold values from -6 to 6
Outputs:
- decoder_output: bfloat16 [2, 8, 1024, 512], P(None, 'dp', 'expert')
- source_grad: float32 [8, 1024, 512], P('dp', 'expert')
- target_grad: float32 [8, 1024, 512], P('dp', 'expert')
- attention_in_grad: float32 [3, 512, 1536], replicated
- attention_out_grad: float32 [3, 512, 512], replicated
- norm_gains_grad: float32 [6, 512], replicated
- encoder_up_grad: float32 [16, 2048, 512], P('expert', 'dp')
- encoder_down_grad: float32 [16, 2048, 512], P('expert', 'dp')
- decoder_up_grad: float32 [16, 2048, 512], P('expert', 'dp')
- decoder_down_grad: float32 [16, 2048, 512], P('expert', 'dp')
- expert_counts: int32 [2, 2, 16], replicated
The draws below stay inside these ranges and needn't reach their ends.
Inputs may be any that keep to these rules, and one draw needn't show every extreme that they name: `encoder_route`: in each pass, among the tokens of one device (the 1 pairs of a dp index, the 256 positions of an expert index), no expert is named more than 32 times; in each pass one expert is named exactly 32 times by the tokens of every device. `encoder_slot`: in each pass, tokens of one device that name the same expert in encoder_route carry different slots. `decoder_route`: in each pass, among the tokens of one device (the 1 pairs of a dp index, the 256 positions of an expert index), no expert is named more than 32 times; in each pass one expert is named exactly 32 times by the tokens of every device. `decoder_slot`: in each pass, tokens of one device that name the same expert in decoder_route carry different slots.
All inputs are finite; a program needn't handle non-finite values.
Results may differ from the reference program's by a relative error of at most 0.024.
Values may be sent and summed in bfloat16 or wider, within the bound.
A program may use at most 256 MiB of HBM per device.

```python
from functools import partial
import jax
import jax.numpy as jnp
from jax import lax

D = 512
HEADS = 8
HEAD_DIM = 64
FF = 2048
EXPERTS = 16
LEN = 1024
PAIRS = 1
ROWS = 256
SEQS = 8
CAP = 32
N_DP = 8
N_EXPERT = 4


def route_table(key, layer):
    key = jax.random.fold_in(key, 40 + layer)
    groups = SEQS // PAIRS
    pieces = LEN // ROWS
    block_rows = PAIRS * ROWS
    blocks = 2 * groups * pieces
    spares = (EXPERTS - 1) * CAP
    hottest = jax.random.randint(jax.random.fold_in(key, 1), (2,), 0, EXPERTS)
    block_hot = jnp.repeat(hottest, groups * pieces)
    block_keys = jax.random.split(jax.random.fold_in(key, 2), blocks)

    def one_block(block_key, hot_one):
        pick_key = jax.random.fold_in(block_key, 5)
        order_key = jax.random.fold_in(block_key, 6)
        chosen = jax.random.permutation(pick_key, spares)[:block_rows - CAP]
        others = (chosen // CAP).astype(jnp.int32)
        others = others + (others >= hot_one).astype(jnp.int32)
        experts = jnp.concatenate([jnp.full((CAP,), hot_one, jnp.int32), others])
        slot_ids = jnp.concatenate([jnp.arange(CAP, dtype=jnp.int32), (chosen % CAP).astype(jnp.int32)])
        shuffle = jax.random.permutation(order_key, block_rows)
        return (experts[shuffle], slot_ids[shuffle])
    experts, slot_ids = jax.vmap(one_block)(block_keys, block_hot)
    layout = (2, groups, pieces, PAIRS, ROWS)
    experts = experts.reshape(layout).transpose(0, 1, 3, 2, 4).reshape(2, SEQS, LEN)
    slot_ids = slot_ids.reshape(layout).transpose(0, 1, 3, 2, 4).reshape(2, SEQS, LEN)
    return (experts, slot_ids)


def draw_encoder_route(key, part):
    experts, slot_ids = route_table(key, 0)
    return experts


def draw_encoder_slot(key, part):
    experts, slot_ids = route_table(key, 0)
    return slot_ids


def draw_decoder_route(key, part):
    experts, slot_ids = route_table(key, 1)
    return experts


def draw_decoder_slot(key, part):
    experts, slot_ids = route_table(key, 1)
    return slot_ids


def levels(key, shape, cuts, low, largest):
    level = 1.0
    for dim, blocks in cuts:
        draws = jax.random.uniform(jax.random.fold_in(jax.random.fold_in(key, 6), dim), (blocks,), jnp.float32, low / len(cuts), largest / len(cuts))
        level = level * jnp.repeat(jnp.exp(draws), shape[dim] // blocks).reshape((-1,) + (1,) * (len(shape) - 1 - dim))
    return level


def centred(rng, shape, deviation, limit, cuts=(), kind=jnp.bfloat16):
    values = jax.random.normal(rng, shape, jnp.float32) * deviation
    if len(cuts) > 0:
        values = levels(rng, shape, cuts, -0.22, 0.18) * values
    return jnp.clip(values, min=-limit, max=limit).astype(kind)


def setup_inputs(seed: int = 0) -> dict:
    key_list = jax.random.split(jax.random.key(seed), 15)
    return {
        "source": centred(key_list[0], (SEQS, LEN, D), 1.0, 6.0, ((0, 8), (1, 4))),
        "target": centred(key_list[1], (SEQS, LEN, D), 1.0, 6.0, ((0, 8), (1, 4))),
        "attention_in": centred(key_list[2], (3, D, 3 * D), D ** -0.5, 0.25),
        "attention_out": centred(key_list[3], (3, D, D), (max(D // 128, 1)) ** -0.5, 3.0),
        "norm_gains": jnp.clip(1.0 + 0.1 * jax.random.normal(key_list[4], (6, D), jnp.float32), 0.5, 1.5),
        "encoder_up": centred(key_list[5], (EXPERTS, FF, D), D ** -0.5, 0.25, ((0, 4),)),
        "encoder_down": centred(key_list[6], (EXPERTS, FF, D), (FF // 2) ** -0.5, 0.1875, ((0, 4),)),
        "decoder_up": centred(key_list[7], (EXPERTS, FF, D), D ** -0.5, 0.25, ((0, 4),)),
        "decoder_down": centred(key_list[8], (EXPERTS, FF, D), (FF // 2) ** -0.5, 0.1875, ((0, 4),)),
        "encoder_route": draw_encoder_route(jax.random.fold_in(key_list[14], 71), 0),
        "encoder_slot": draw_encoder_slot(jax.random.fold_in(key_list[14], 71), 0),
        "decoder_route": draw_decoder_route(jax.random.fold_in(key_list[14], 71), 0),
        "decoder_slot": draw_decoder_slot(jax.random.fold_in(key_list[14], 71), 0),
        "output_grad": centred(key_list[13], (2, SEQS, LEN, D), 1.0, 6.0, ((1, 8), (2, 4)), jnp.float32),
    }


NORM_EPSILON = 1e-05
HIGHEST = lax.Precision.HIGHEST

@jax.custom_vjp
def low(v):
    return lax.optimization_barrier(v.astype(jnp.bfloat16)).astype(jnp.float32)

@jax.custom_vjp
def low_back(v):
    return v

def low_keep(v):
    return (low(v), None)

def low_pass(kept, grad):
    return (grad,)

def back_keep(v):
    return (v, None)

def back_low(kept, grad):
    return (low(grad),)
low.defvjp(low_keep, low_pass)
low_back.defvjp(back_keep, back_low)

def layer_norm(values, gain):
    centered = values - lax.optimization_barrier(jnp.mean(values, axis=-1, keepdims=True))
    spread = lax.optimization_barrier(jnp.mean(centered * centered, axis=-1, keepdims=True))
    return centered * lax.rsqrt(spread + NORM_EPSILON) * gain

def activate(values):
    return jax.nn.gelu(values, approximate=True)

def project(values, weight):
    return jnp.einsum('...d,dk->...k', values, weight, precision=HIGHEST)

def split_heads(values):
    return values.reshape(values.shape[:-1] + (HEADS, HEAD_DIM))

def join_heads(values):
    return values.reshape(values.shape[:-2] + (HEADS * HEAD_DIM,))

def attention_core(queries, key_rows, value_rows, causal):
    scores = jnp.einsum('qhd,khd->hqk', queries, key_rows, precision=HIGHEST) * HEAD_DIM ** (-0.5)
    scores = low_back(scores)
    if causal:
        positions = jnp.arange(LEN, dtype=jnp.int32)
        scores = jnp.where(positions[:, None] >= positions[None, :], scores, -1e+30)
    weights = jax.nn.softmax(scores, axis=-1)
    return jnp.einsum('hqk,khd->qhd', low(weights), value_rows, precision=HIGHEST)

def attend_all(queries, key_rows, value_rows, causal):
    checkpointed = jax.checkpoint(partial(attention_core, causal=causal))
    return lax.map(lambda members: checkpointed(members[0], members[1], members[2]), (queries, key_rows, value_rows))

def self_attention(residual, gain, inward, outward, causal):
    feature = residual.shape[-1]
    normed = low(layer_norm(residual, gain))
    packed = low_back(low(project(normed, inward)))
    blended = attend_all(split_heads(packed[..., :feature]), split_heads(packed[..., feature:2 * feature]), split_heads(packed[..., 2 * feature:]), causal)
    blended = low_back(low(join_heads(blended)))
    return residual + low_back(project(blended, outward))

def to_blocks(values):
    trailing = values.shape[3:]
    shaped = values.reshape((2, N_DP, PAIRS, N_EXPERT, ROWS) + trailing)
    shaped = jnp.swapaxes(shaped, 2, 3)
    return shaped.reshape((2, N_DP, N_EXPERT, PAIRS * ROWS) + trailing)

def from_blocks(values):
    trailing = values.shape[4:]
    shaped = values.reshape((2, N_DP, N_EXPERT, PAIRS, ROWS) + trailing)
    shaped = jnp.swapaxes(shaped, 2, 3)
    return shaped.reshape((2, SEQS, LEN) + trailing)

def expert_work(rows_in, weight_up, weight_down):
    hidden = low_back(jnp.einsum('pabecd,efd->pabecf', rows_in, weight_up, precision=HIGHEST))
    active = low(activate(hidden))
    return low_back(low(jnp.einsum('pabecf,efd->pabecd', active, weight_down, precision=HIGHEST)))

def mixture(tokens, route, slot, weight_up, weight_down):
    columns = to_blocks(route * CAP + slot)
    dispatch_table = (columns[..., None] == jnp.arange(EXPERTS * CAP, dtype=jnp.int32)).astype(tokens.dtype)
    buffer = jnp.einsum('pabts,pabtd->pabsd', dispatch_table, to_blocks(tokens), precision=HIGHEST)
    buffer = buffer.reshape(buffer.shape[:3] + (EXPERTS, CAP, buffer.shape[-1]))
    outcome = jax.checkpoint(expert_work)(buffer, weight_up, weight_down)
    outcome = outcome.reshape(outcome.shape[:3] + (EXPERTS * CAP, outcome.shape[-1]))
    return from_blocks(jnp.einsum('pabts,pabsd->pabtd', dispatch_table, outcome, precision=HIGHEST))

def merge_passes(values):
    return values.reshape((2 * SEQS,) + values.shape[2:])

def forward(source, target, attention_in, attention_out, norm_gains, encoder_up, encoder_down, decoder_up, decoder_down, encoder_route, encoder_slot, decoder_route, decoder_slot):
    feature = source.shape[-1]
    encoder_attended = self_attention(source, norm_gains[0], attention_in[0], attention_out[0], False)
    moe_input = low(layer_norm(encoder_attended, norm_gains[1]))
    moe_input = low_back(jnp.broadcast_to(moe_input[None], (2,) + moe_input.shape))
    encoder_final = encoder_attended[None] + mixture(moe_input, encoder_route, encoder_slot, encoder_up, encoder_down)
    memory = low(layer_norm(encoder_final, norm_gains[2]))
    decoder_attended = self_attention(target, norm_gains[3], attention_in[1], attention_out[1], True)
    cross_input = low(layer_norm(decoder_attended, norm_gains[4]))
    queries = low(project(cross_input, attention_in[2][:, :feature]))
    queries = low_back(jnp.broadcast_to(queries[None], (2,) + queries.shape))
    key_value = low_back(low(project(memory, attention_in[2][:, feature:])))
    blended = attend_all(split_heads(merge_passes(queries)), split_heads(merge_passes(key_value[..., :feature])), split_heads(merge_passes(key_value[..., feature:])), False)
    blended = low_back(low(join_heads(blended))).reshape((2,) + decoder_attended.shape)
    decoder_crossed = decoder_attended[None] + low_back(project(blended, attention_out[2]))
    moe_rows = low_back(low(layer_norm(decoder_crossed, norm_gains[5])))
    return decoder_crossed + mixture(moe_rows, decoder_route, decoder_slot, decoder_up, decoder_down)

def tally_route(route):
    experts_range = jnp.arange(EXPERTS, dtype=jnp.int32)
    return lax.optimization_barrier(jnp.sum((route[..., None] == experts_range).astype(jnp.int32), axis=(1, 2)))

def reference(source, target, attention_in, attention_out, norm_gains, encoder_up, encoder_down, decoder_up, decoder_down, encoder_route, encoder_slot, decoder_route, decoder_slot, output_grad):
    operands = [operand.astype(jnp.float32) for operand in (source, target, attention_in, attention_out, norm_gains, encoder_up, encoder_down, decoder_up, decoder_down)]

    def closed(*weights):
        return forward(*weights, encoder_route, encoder_slot, decoder_route, decoder_slot)
    output, pullback = jax.vjp(closed, *operands)
    gradients = pullback(output_grad.astype(jnp.float32))
    counts = jnp.stack([tally_route(encoder_route), tally_route(decoder_route)])
    return (output.astype(jnp.bfloat16), gradients[0], gradients[1], gradients[2], gradients[3], gradients[4], gradients[5], gradients[6], gradients[7], gradients[8], counts)
```

```python
import functools

import jax
import jax.numpy as jnp
from jax import lax
from jax.experimental import pallas as pl
from jax.experimental.pallas import tpu as pltpu
from jax.sharding import PartitionSpec as P

HEAD_DIM = 64
EXPERTS = 16
NORM_EPSILON = 1e-05
MASKED = -1e30
F32 = jnp.float32
BF16 = jnp.bfloat16
VMEM_LIMIT = 58 << 20


def nn(a, b):
    return jnp.dot(a, b, preferred_element_type=F32)


def nt(a, b):
    return lax.dot_general(a, b, (((1,), (1,)), ((), ())), preferred_element_type=F32)


def tn(a, b):
    return lax.dot_general(a, b, (((0,), (0,)), ((), ())), preferred_element_type=F32)


def tt(a, b):
    return lax.dot_general(a, b, (((0,), (1,)), ((), ())), preferred_element_type=F32)


def norm_parts(x):
    mean = jnp.mean(x, axis=-1, keepdims=True)
    centered = x - mean
    spread = jnp.mean(centered * centered, axis=-1, keepdims=True)
    scale = lax.rsqrt(spread + NORM_EPSILON)
    return centered * scale, scale


def norm(x, gain):
    return norm_parts(x)[0] * gain


def norm_back(x, gain, grad):
    hat, scale = norm_parts(x)
    inner = grad * gain
    dx = scale * (
        inner
        - jnp.mean(inner, axis=-1, keepdims=True)
        - hat * jnp.mean(inner * hat, axis=-1, keepdims=True)
    )
    return dx, jnp.sum(grad * hat, axis=0, keepdims=True)


GELU_A = 0.7978845608028654
GELU_B = 0.044715


def gelu(x):
    return 0.5 * x * (1.0 + jnp.tanh(GELU_A * (x + GELU_B * (x * x * x))))


def gelu_both(x):
    sq = x * x
    th = jnp.tanh(x * (GELU_A + (GELU_A * GELU_B) * sq))
    half = 0.5 * (1.0 + th)
    slope = half + (0.5 * x) * (1.0 - th * th) * (GELU_A + (3.0 * GELU_A * GELU_B) * sq)
    return x * half, slope


def whole(shape):
    return pl.BlockSpec(shape, lambda *_: (0,) * len(shape))


def call(body, ins, outs, name, grid=None, in_specs=None, out_specs=None, scratch=(), scalars=(), flops=0):
    if in_specs is None:
        in_specs = [None] * len(ins)
    if out_specs is None:
        out_specs = [None] * len(outs)
    in_specs = [whole(a.shape) if s is None else s for a, s in zip(ins, in_specs)]
    out_specs = [whole(o[0]) if s is None else s for o, s in zip(outs, out_specs)]
    moved = sum(a.size * a.dtype.itemsize for a in ins) + sum(
        functools.reduce(lambda x, y: x * y, o[0], 1) * jnp.dtype(o[1]).itemsize for o in outs
    )
    spec = pltpu.PrefetchScalarGridSpec(
        num_scalar_prefetch=len(scalars),
        grid=(1,) if grid is None else grid,
        in_specs=in_specs,
        out_specs=out_specs,
        scratch_shapes=list(scratch),
    )
    return pl.pallas_call(
        body,
        out_shape=[jax.ShapeDtypeStruct(s, d) for s, d in outs],
        grid_spec=spec,
        name=name,
        compiler_params=pltpu.CompilerParams(vmem_limit_bytes=VMEM_LIMIT),
        cost_estimate=pl.CostEstimate(flops=flops, bytes_accessed=moved, transcendentals=0),
    )(*scalars, *ins)


def head_rows(values, h):
    rows = values[h * HEAD_DIM : (h + 1) * HEAD_DIM]
    zero = jnp.zeros_like(rows)
    return jnp.concatenate([rows, zero] if h % 2 == 0 else [zero, rows], axis=0)


def head_lanes(values, h):
    pair = values[:, (h // 2) * 128 : (h // 2 + 1) * 128]
    lane = lax.broadcasted_iota(jnp.int32, pair.shape, 1)
    keep = lane < HEAD_DIM if h % 2 == 0 else lane >= HEAD_DIM
    return jnp.where(keep, pair, jnp.zeros_like(pair))


def causal_allow(me, ids, rows):
    parts = []
    for r in ids:
        key = (me ^ r) * rows + lax.broadcasted_iota(jnp.int32, (rows, rows), 0)
        query = me * rows + lax.broadcasted_iota(jnp.int32, (rows, rows), 1)
        parts.append(key <= query)
    return jnp.concatenate([p.astype(F32) for p in parts], axis=0) > 0.5


def attend_forward(q_t, k, v_t, allow, o_t, lse):
    heads = q_t.shape[0] // HEAD_DIM
    for h in range(heads):
        pair = slice((h // 2) * 128, (h // 2 + 1) * 128)
        scores = nn(k[:, pair], head_rows(q_t, h))
        if allow is not None:
            scores = jnp.where(allow, scores, MASKED)
        top = jnp.max(scores, axis=0, keepdims=True)
        lifted = jnp.exp(scores - top)
        total = jnp.sum(lifted, axis=0, keepdims=True)
        rows = slice(h * HEAD_DIM, (h + 1) * HEAD_DIM)
        blended = nn(v_t[rows, :], lifted.astype(BF16)) * (1.0 / total)
        o_t[rows, :] = blended.astype(BF16)
        lse[h : h + 1, :] = top + jnp.log(total)


def attend_backward(q, k, v, k_t, do, lse, allow, dk, dv, dq_t):
    heads = q.shape[1] // HEAD_DIM
    q_t = q.astype(F32).T.astype(BF16)
    do_t = do.astype(F32).T.astype(BF16)
    for h2 in range(heads // 2):
        pair = slice(h2 * 128, (h2 + 1) * 128)
        dk_pair = None
        for h in (2 * h2, 2 * h2 + 1):
            rows = slice(h * HEAD_DIM, (h + 1) * HEAD_DIM)
            scores = nn(k[:, pair], head_rows(q_t, h))
            weights = jnp.exp(scores - lse[h : h + 1, :])
            if allow is not None:
                weights = jnp.where(allow, weights, 0.0)
            weights_grad = nn(v[:, pair], head_rows(do_t, h))
            centre = jnp.sum(weights * weights_grad, axis=0, keepdims=True)
            scores_grad = (weights * (weights_grad - centre)).astype(BF16)
            dv_part = nn(weights.astype(BF16), head_lanes(do, h))
            dk_part = nn(scores_grad, head_lanes(q, h))
            dq_t[rows, :] = (nn(k_t[rows, :], scores_grad) * HEAD_DIM ** (-0.5)).astype(BF16)
            if dk_pair is None:
                dk_pair, dv_pair = dk_part, dv_part
            else:
                dk_pair, dv_pair = dk_pair + dk_part, dv_pair + dv_part
        dk[:, pair] = dk_pair.astype(BF16)
        dv[:, pair] = dv_pair.astype(BF16)


def piece_blocks(pieces):
    return [(ref, i) for ref in pieces for i in range(ref.shape[0])]


def self_forward(pieces, ids, me, gain, gain_next, inward, outward, causal):
    rows, feature = pieces[0].shape[1:]
    length = len(ids) * rows
    heads = feature // HEAD_DIM
    count = len(pieces)

    def body(me_ref, *refs):
        parts = refs[:count]
        g, gn, win, wout, out, nxt, hm, k, k_t, v, q, o_t, lse, v_t = refs[count:]
        for b, (ref, i) in enumerate(piece_blocks(parts)):
            hm[b * rows : (b + 1) * rows, :] = norm(ref[i].astype(F32), g[...]).astype(BF16)
        hm_all = hm[...]
        k[...] = nn(hm_all, win[:, feature : 2 * feature]).astype(BF16)
        v[...] = nn(hm_all, win[:, 2 * feature :]).astype(BF16)
        k_t[...] = tt(win[:, feature : 2 * feature], hm_all).astype(BF16)
        v_t[...] = tt(win[:, 2 * feature :], hm_all).astype(BF16)
        q_scaled = nn(hm[0:rows, :], win[:, :feature]).astype(BF16).astype(F32) * HEAD_DIM ** (-0.5)
        q[...] = q_scaled.astype(BF16)
        allow = causal_allow(me_ref[0], ids, rows) if causal else None
        attend_forward(q_scaled.T.astype(BF16), k, v_t, allow, o_t, lse)
        merged = o_t[...].astype(F32).T.astype(BF16)
        after = parts[0][0].astype(F32) + nn(merged, wout[...])
        out[...] = after
        nxt[...] = norm(after, gn[...]).astype(BF16)

    return call(
        body,
        [*pieces, gain, gain_next, inward, outward],
        [
            ((rows, feature), F32),
            ((rows, feature), BF16),
            ((length, feature), BF16),
            ((length, feature), BF16),
            ((feature, length), BF16),
            ((length, feature), BF16),
            ((rows, feature), BF16),
            ((feature, rows), BF16),
            ((heads, rows), F32),
        ],
        "self_forward",
        scratch=[pltpu.VMEM((feature, length), BF16)],
        scalars=[me],
        flops=2 * length * feature * (4 * feature + 4 * rows),
    )


def weight_grad_store(dw, feature, hq, hm, dq, dk, dv, o_t, d_branch):
    dw[:, :feature] = tn(hq, dq).astype(BF16)
    dw[:, feature : 2 * feature] = tn(hm, dk).astype(BF16)
    dw[:, 2 * feature : 3 * feature] = tn(hm, dv).astype(BF16)
    dw[:, 3 * feature :] = nn(o_t, d_branch).astype(BF16)


def store_blocks(outs, values, rows):
    for b, (ref, i) in enumerate(piece_blocks(outs)):
        ref[i] = values[b * rows : (b + 1) * rows].astype(BF16)


def self_backward_core(me_ref, ids, causal, d_branch, saved, win, wout, outs, dw, scratch):
    hm, k, k_t, v, q, o_t, lse = saved
    dk, dv, dq_t = scratch
    rows, feature = q.shape
    do = nt(d_branch, wout[...]).astype(BF16)
    allow = causal_allow(me_ref[0], ids, rows) if causal else None
    attend_backward(q[...], k, v, k_t, do, lse, allow, dk, dv, dq_t)
    dq = dq_t[...].astype(F32).T.astype(BF16)
    for b, (ref, i) in enumerate(piece_blocks(outs)):
        span = slice(b * rows, (b + 1) * rows)
        part = nt(dk[span, :], win[:, feature : 2 * feature]) + nt(dv[span, :], win[:, 2 * feature :])
        if b == 0:
            part = part + nt(dq, win[:, :feature])
        ref[i] = part.astype(BF16)
    weight_grad_store(dw, feature, hm[0:rows, :], hm[...], dq, dk[...], dv[...], o_t[...], d_branch)


def self_backward(upstream, ids, sizes, me, saved, inward, outward, causal):
    rows, feature = upstream.shape
    length = len(ids) * rows
    count = len(sizes)

    def body(me_ref, up, hm, k, k_t, v, q, o_t, lse, win, wout, *refs):
        outs, dw, scratch = refs[:count], refs[count], refs[count + 1 :]
        self_backward_core(
            me_ref, ids, causal, up[...].astype(BF16), (hm, k, k_t, v, q, o_t, lse), win, wout, outs, dw, scratch
        )

    return call(
        body,
        [upstream, *saved, inward, outward],
        [((n, rows, feature), BF16) for n in sizes] + [((feature, 4 * feature), BF16)],
        "self_backward",
        scratch=[
            pltpu.VMEM((length, feature), BF16),
            pltpu.VMEM((length, feature), BF16),
            pltpu.VMEM((feature, rows), BF16),
        ],
        scalars=[me],
        flops=2 * length * feature * (4 * feature + 10 * rows),
    )


def gather_rows(me, experts, cap, col, returned):
    total = None
    slots = experts * cap
    for r, rows in returned:
        local = col - (me ^ r) * slots
        hot = (local == lax.broadcasted_iota(jnp.int32, (col.shape[0], slots), 1)).astype(BF16)
        part = nn(hot, rows.reshape(slots, rows.shape[-1]))
        total = part if total is None else total + part
    return total


def spread_rows(me, experts, cap, col, tokens):
    slots = experts * cap
    local = col - me * slots
    hot = (local == lax.broadcasted_iota(jnp.int32, (slots, col.shape[1]), 0)).astype(BF16)
    return nn(hot, tokens).astype(BF16)


def fill_buffers(me, experts, cap, cols, token_of, sources, dest):
    for s in range(sources):
        for p in range(2):
            rows = spread_rows(me, experts, cap, cols[2 * s + p], token_of(s, p))
            at = (2 * s + p) * cap
            for j in range(experts):
                dest[j, at : at + cap, :] = rows[j * cap : (j + 1) * cap]


def expert_forward(pieces, cols, me, weight_up, weight_down, ids):
    experts, hidden, feature = weight_up.shape
    rows = pieces[0].shape[1]
    cap = 2 * rows // EXPERTS
    count = len(pieces)
    sources = len(ids)
    length = sources * 2 * cap

    def body(me_ref, *refs):
        parts = refs[:count]
        col, up, down = refs[count : count + 3]
        outs = refs[count + 3 : count + 3 + sources]
        buf = refs[-1]
        j = pl.program_id(0)

        @pl.when(j == 0)
        def _():
            blocks = piece_blocks(parts)
            fill_buffers(me_ref[0], experts, cap, col, lambda s, p: blocks[s][0][blocks[s][1]], sources, buf)

        x = buf[j]
        act = gelu(nt(x, up[0])).astype(BF16)
        res = nn(act, down[0]).astype(BF16)
        for s in range(sources):
            for p in range(2):
                at = (2 * s + p) * cap
                outs[s][0, p] = res[at : at + cap]

    weight = pl.BlockSpec((1, hidden, feature), lambda j, *_: (j, 0, 0))
    return call(
        body,
        [*pieces, cols, weight_up, weight_down],
        [((experts, 2, cap, feature), BF16)] * sources,
        "expert_forward",
        grid=(experts,),
        in_specs=[None] * (count + 1) + [weight, weight],
        out_specs=[pl.BlockSpec((1, 2, cap, feature), lambda j, *_: (j, 0, 0, 0))] * sources,
        scratch=[pltpu.VMEM((experts, length, feature), BF16)],
        scalars=[me],
        flops=4 * experts * length * hidden * feature,
    )


def expert_backward(pieces, grads, cols, me, weight_up, weight_down, ids, with_result):
    experts, hidden, feature = weight_up.shape
    rows = grads[0].shape[2]
    cap = 2 * rows // EXPERTS
    count = len(pieces)
    sources = len(ids)
    length = sources * 2 * cap
    both = pieces[0].ndim == 4
    kinds = 2 if with_result else 1

    def body(me_ref, *refs):
        parts = refs[:count]
        gparts = refs[count : 2 * count]
        col, up, down = refs[2 * count : 2 * count + 3]
        outs = refs[2 * count + 3 : 2 * count + 3 + kinds * sources]
        buf, gbuf = refs[-2:]
        j = pl.program_id(0)

        @pl.when(j == 0)
        def _():
            blocks = piece_blocks(parts)
            gblocks = piece_blocks(gparts)
            pick = lambda s, p: blocks[s][0][blocks[s][1], p] if both else blocks[s][0][blocks[s][1]]
            fill_buffers(me_ref[0], experts, cap, col, pick, sources, buf)
            gpick = lambda s, p: gblocks[s][0][gblocks[s][1], p]
            fill_buffers(me_ref[0], experts, cap, col, gpick, sources, gbuf)

        value, slope = gelu_both(nt(buf[j], up[0]))
        hidden_grad = (slope * nt(gbuf[j], down[0])).astype(BF16)
        dx = nn(hidden_grad, up[0]).astype(BF16)
        results = [dx]
        if with_result:
            results.append(nn(value.astype(BF16), down[0]).astype(BF16))
        for n, res in enumerate(results):
            for s in range(sources):
                for p in range(2):
                    at = (2 * s + p) * cap
                    outs[n * sources + s][0, p] = res[at : at + cap]

    weight = pl.BlockSpec((1, hidden, feature), lambda j, *_: (j, 0, 0))
    outs = call(
        body,
        [*pieces, *grads, cols, weight_up, weight_down],
        [((experts, 2, cap, feature), BF16)] * (kinds * sources),
        "expert_backward",
        grid=(experts,),
        in_specs=[None] * (2 * count + 1) + [weight, weight],
        out_specs=[pl.BlockSpec((1, 2, cap, feature), lambda j, *_: (j, 0, 0, 0))] * (kinds * sources),
        scratch=[pltpu.VMEM((experts, length, feature), BF16)] * 2,
        scalars=[me],
        flops=(8 if with_result else 6) * experts * length * hidden * feature,
    )
    return outs[:sources], outs[sources:]


def expert_weights(pieces, grads, cols, place, weight_up, weight_down, sources, ny, nz):
    experts, hidden, feature = weight_up.shape
    rows = grads[0].shape[2]
    cap = 2 * rows // EXPERTS
    count, gcount = len(pieces), len(grads)
    length = sources * 2 * cap
    both = pieces[0].ndim == 4
    span = hidden // (ny * nz)

    def body(place_ref, *refs):
        parts = refs[:count]
        gparts = refs[count : count + gcount]
        col, up, down = refs[count + gcount : count + gcount + 3]
        up_out, down_out, buf, gbuf = refs[count + gcount + 3 :]
        j = pl.program_id(0)

        @pl.when((j == 0) & (pl.program_id(1) == 0))
        def _():
            blocks = piece_blocks(parts)
            gblocks = piece_blocks(gparts)
            pick = lambda s, p: blocks[s][0][blocks[s][1], p] if both else blocks[s][0][blocks[s][1]]
            fill_buffers(place_ref[0], experts, cap, col, pick, sources, buf)
            gpick = lambda s, p: gblocks[s][0][gblocks[s][1], p]
            fill_buffers(place_ref[0], experts, cap, col, gpick, sources, gbuf)

        x, g = buf[j], gbuf[j]
        value, slope = gelu_both(nt(up[0], x))
        hidden_grad = (slope * nt(down[0], g)).astype(BF16)
        up_out[0, 0] = nn(hidden_grad, x).astype(BF16)
        down_out[0, 0] = nn(value.astype(BF16), g).astype(BF16)

    weight = pl.BlockSpec((1, span, feature), lambda j, r, place_ref: (j, place_ref[1] * ny + (place_ref[2] ^ r), 0))
    out = pl.BlockSpec((1, 1, span, feature), lambda j, r, *_: (r, j, 0, 0))
    return call(
        body,
        [*pieces, *grads, cols, weight_up, weight_down],
        [((ny, experts, span, feature), BF16)] * 2,
        "expert_weights",
        grid=(experts, ny),
        in_specs=[None] * (count + gcount + 1) + [weight, weight],
        out_specs=[out, out],
        scratch=[pltpu.VMEM((experts, length, feature), BF16)] * 2,
        scalars=[place],
        flops=8 * experts * length * (hidden // nz) * feature,
    )


def combine_norm(returned, ids, col, me, residual, gain):
    experts, _, cap, feature = returned[0].shape
    rows = residual.shape[-2]
    count = len(ids)

    def body(me_ref, *refs):
        ret = refs[:count]
        c, res, g, out, nxt = refs[count:]
        for p in range(2):
            mixed = gather_rows(me_ref[0], experts, cap, c[p], [(r, ref[:, p]) for r, ref in zip(ids, ret)])
            after = res[...] + mixed
            out[p] = after
            nxt[p] = norm(after, g[...]).astype(BF16)

    return call(
        body,
        [*returned, col, residual, gain],
        [((2, rows, feature), F32), ((2, rows, feature), BF16)],
        "combine_norm",
        scalars=[me],
        flops=4 * rows * EXPERTS * cap * feature,
    )


def combine_output(returned, ids, col, me, residual):
    experts, _, cap, feature = returned[0].shape
    rows = residual.shape[-2]
    count = len(ids)

    def body(me_ref, *refs):
        ret = refs[:count]
        c, res, out = refs[count:]
        for p in range(2):
            mixed = gather_rows(me_ref[0], experts, cap, c[p], [(r, ref[:, p]) for r, ref in zip(ids, ret)])
            out[p] = (res[p] + mixed).astype(BF16)

    return call(
        body,
        [*returned, col, residual],
        [((2, rows, feature), BF16)],
        "combine_output",
        scalars=[me],
        flops=4 * rows * EXPERTS * cap * feature,
    )[0]


def cross_forward(hc, pieces, ids, mid, gain, inward, outward):
    rows, feature = hc.shape
    length = len(ids) * rows
    heads = feature // HEAD_DIM
    count = len(pieces)

    def body(*refs):
        h, *parts = refs[: count + 1]
        res, g, win, wout, out, nxt, hm, k, k_t, v, q, o_t, lse, v_t = refs[count + 1 :]
        for b, (ref, i) in enumerate(piece_blocks(parts)):
            hm[0, b * rows : (b + 1) * rows, :] = ref[i, 0]
        hm_all = hm[0]
        k[0] = nn(hm_all, win[:, feature : 2 * feature]).astype(BF16)
        v[0] = nn(hm_all, win[:, 2 * feature :]).astype(BF16)
        k_t[0] = tt(win[:, feature : 2 * feature], hm_all).astype(BF16)
        v_t[...] = tt(win[:, 2 * feature :], hm_all).astype(BF16)
        q_scaled = nn(h[...], win[:, :feature]).astype(BF16).astype(F32) * HEAD_DIM ** (-0.5)
        q[...] = q_scaled.astype(BF16)
        attend_forward(q_scaled.T.astype(BF16), k.at[0], v_t, None, o_t.at[0], lse.at[0])
        merged = o_t[0].astype(F32).T.astype(BF16)
        after = res[...] + nn(merged, wout[...])
        out[0] = after
        nxt[0] = norm(after, g[...]).astype(BF16)

    per = lambda *shape: pl.BlockSpec((1,) + shape, lambda p, *_: (p,) + (0,) * len(shape))
    return call(
        body,
        [hc, *pieces, mid, gain, inward, outward],
        [
            ((2, rows, feature), F32),
            ((2, rows, feature), BF16),
            ((2, length, feature), BF16),
            ((2, length, feature), BF16),
            ((2, feature, length), BF16),
            ((2, length, feature), BF16),
            ((rows, feature), BF16),
            ((2, feature, rows), BF16),
            ((2, heads, rows), F32),
        ],
        "cross_forward",
        grid=(2,),
        in_specs=[None]
        + [pl.BlockSpec((a.shape[0], 1, rows, feature), lambda p, *_: (0, p, 0, 0)) for a in pieces]
        + [None] * 4,
        out_specs=[
            per(rows, feature),
            per(rows, feature),
            per(length, feature),
            per(length, feature),
            per(feature, length),
            per(length, feature),
            None,
            per(feature, rows),
            per(heads, rows),
        ],
        scratch=[pltpu.VMEM((feature, length), BF16)],
        flops=4 * length * feature * (4 * feature + 4 * rows),
    )


def cross_backward(returned, ids, sizes, col, me, crossed, gain_w, out_grad, saved, hc, mid, gain_c, inward, outward):
    experts, _, cap, feature = returned[0].shape
    rows = mid.shape[0]
    length = len(ids) * rows
    heads = feature // HEAD_DIM
    count = len(ids)
    npieces = len(sizes)

    def body(me_ref, *refs):
        ret = refs[:count]
        c, t2, gw, og, hm, k, k_t, v, q, o_t, lse, h, t1, gc, win, wout = refs[count : count + 16]
        rest = refs[count + 16 :]
        outs = rest[:npieces]
        dw, dt1, dgw, dgc = rest[npieces : npieces + 4]
        dk, dv, dq_t, dw_acc, dh_acc = rest[npieces + 4 :]
        p = pl.program_id(0)
        dwr = gather_rows(me_ref[0], experts, cap, c[0], [(r, ref[:, 0]) for r, ref in zip(ids, ret)])
        dx, dg = norm_back(t2[0], gw[...], dwr)
        upstream = og[0] + dx
        d_branch = upstream.astype(BF16)
        do = nt(d_branch, wout[...]).astype(BF16)
        attend_backward(q[...], k.at[0], v.at[0], k_t.at[0], do, lse.at[0], None, dk, dv, dq_t)
        dq = dq_t[...].astype(F32).T.astype(BF16)
        for b, (ref, i) in enumerate(piece_blocks(outs)):
            span = slice(b * rows, (b + 1) * rows)
            part = nt(dk[span, :], win[:, feature : 2 * feature]) + nt(dv[span, :], win[:, 2 * feature :])
            ref[i, 0] = part.astype(BF16)
        dh = nt(dq, win[:, :feature])
        grads = [
            tn(h[...], dq),
            tn(hm[0], dk[...]),
            tn(hm[0], dv[...]),
            nn(o_t[0], d_branch),
        ]

        @pl.when(p == 0)
        def _():
            for n, value in enumerate(grads):
                dw_acc[:, n * feature : (n + 1) * feature] = value
            dh_acc[...] = dh
            dt1[...] = upstream
            dgw[...] = dg

        @pl.when(p == 1)
        def _():
            for n, value in enumerate(grads):
                at = slice(n * feature, (n + 1) * feature)
                dw[:, at] = (dw_acc[:, at] + value).astype(BF16)
            back, dg_c = norm_back(t1[...], gc[...], dh_acc[...] + dh)
            dt1[...] = dt1[...] + upstream + back
            dgw[...] = dgw[...] + dg
            dgc[...] = dg_c

    per = lambda *shape: pl.BlockSpec((1,) + shape, lambda p, *_: (p,) + (0,) * len(shape))
    return call(
        body,
        [*returned, col, crossed, gain_w, out_grad, *saved, hc, mid, gain_c, inward, outward],
        [((n, 2, rows, feature), BF16) for n in sizes]
        + [((feature, 4 * feature), BF16), ((rows, feature), F32), ((1, feature), F32), ((1, feature), F32)],
        "cross_backward",
        grid=(2,),
        in_specs=[pl.BlockSpec((experts, 1, cap, feature), lambda p, *_: (0, p, 0, 0))] * count
        + [
            per(rows, 1),
            per(rows, feature),
            None,
            per(rows, feature),
            per(length, feature),
            per(length, feature),
            per(feature, length),
            per(length, feature),
            None,
            per(feature, rows),
            per(heads, rows),
            None,
            None,
            None,
            None,
            None,
        ],
        out_specs=[pl.BlockSpec((n, 1, rows, feature), lambda p, *_: (0, p, 0, 0)) for n in sizes] + [None] * 4,
        scratch=[
            pltpu.VMEM((length, feature), BF16),
            pltpu.VMEM((length, feature), BF16),
            pltpu.VMEM((feature, rows), BF16),
            pltpu.VMEM((feature, 4 * feature), F32),
            pltpu.VMEM((rows, feature), F32),
        ],
        scalars=[me],
        flops=4 * length * feature * (4 * feature + 10 * rows),
    )


def memory_backward(parts, final, gain):
    _, rows, feature = final.shape
    count = len(parts)

    def body(*refs):
        p = refs[:count]
        x, g, out, low, dg = refs[count:]
        total = None
        for n in range(2):
            grad = p[0][n].astype(F32)
            for other in p[1:]:
                grad = grad + other[n].astype(F32)
            dx, dgain = norm_back(x[n], g[...], grad)
            out[n] = dx
            low[n] = dx.astype(BF16)
            total = dgain if total is None else total + dgain
        dg[...] = total

    return call(
        body,
        [*parts, final, gain],
        [((2, rows, feature), F32), ((2, rows, feature), BF16), ((1, feature), F32)],
        "memory_backward",
    )


def encoder_backward(returned, ids, sizes, col, me, attended, gain, final_grad, saved, inward, outward):
    experts, _, cap, feature = returned[0].shape
    rows = attended.shape[0]
    length = len(ids) * rows
    count = len(ids)
    npieces = len(sizes)

    def body(me_ref, *refs):
        ret = refs[:count]
        c, e1, g, fg, hm, k, k_t, v, q, o_t, lse, win, wout = refs[count : count + 13]
        rest = refs[count + 13 :]
        outs = rest[:npieces]
        dw, de1, dg = rest[npieces : npieces + 3]
        scratch = rest[npieces + 3 :]
        du = None
        for p in range(2):
            part = gather_rows(me_ref[0], experts, cap, c[p], [(r, ref[:, p]) for r, ref in zip(ids, ret)])
            du = part if du is None else du + part
        dx, dgain = norm_back(e1[...], g[...], du)
        upstream = fg[0] + fg[1] + dx
        de1[...] = upstream
        dg[...] = dgain
        self_backward_core(
            me_ref, ids, False, upstream.astype(BF16), (hm, k, k_t, v, q, o_t, lse), win, wout, outs, dw, scratch
        )

    return call(
        body,
        [*returned, col, attended, gain, final_grad, *saved, inward, outward],
        [((n, rows, feature), BF16) for n in sizes]
        + [((feature, 4 * feature), BF16), ((rows, feature), F32), ((1, feature), F32)],
        "encoder_backward",
        scratch=[
            pltpu.VMEM((length, feature), BF16),
            pltpu.VMEM((length, feature), BF16),
            pltpu.VMEM((feature, rows), BF16),
        ],
        scalars=[me],
        flops=2 * length * feature * (4 * feature + 10 * rows),
    )


def input_backward(parts, values, gain, upstream):
    rows, feature = upstream.shape
    count = len(parts)

    def body(*refs):
        p = refs[:count]
        x, g, up, out, dg = refs[count:]
        grad = p[0][...].reshape(rows, feature).astype(F32)
        for other in p[1:]:
            grad = grad + other[...].reshape(rows, feature).astype(F32)
        dx, dgain = norm_back(x[...].astype(F32), g[...], grad)
        out[...] = up[...] + dx
        dg[...] = dgain

    return call(
        body,
        [*parts, values, gain, upstream],
        [((rows, feature), F32), ((1, feature), F32)],
        "input_backward",
    )


AXES = ("dp", "expert")


def flip(value, n_dp, n_expert, dp_bits, expert_bits):
    pairs = []
    for d in range(n_dp):
        for e in range(n_expert):
            pairs.append((d * n_expert + e, (d ^ dp_bits) * n_expert + (e ^ expert_bits)))
    return lax.ppermute(value, AXES, pairs)


def bits_down(n):
    out, b = [], n // 2
    while b >= 1:
        out.append(b)
        b //= 2
    return out


def local(
    n_dp,
    n_expert,
    source,
    target,
    attention_in,
    attention_out,
    norm_gains,
    encoder_up,
    encoder_down,
    decoder_up,
    decoder_down,
    encoder_route,
    encoder_slot,
    decoder_route,
    decoder_slot,
    output_grad,
):
    _, rows, feature = source.shape
    cap = 2 * rows // EXPERTS
    ny = 2 if n_dp <= 8 else 4
    nz = n_dp // ny
    me = lax.axis_index("expert").astype(jnp.int32)
    dp = lax.axis_index("dp").astype(jnp.int32)
    place = jnp.stack([me, dp // ny, dp % ny])
    me1 = me[None]
    swap = lambda v, d, e: flip(v, n_dp, n_expert, d, e)

    ids, sizes = [0], [1]
    for b in bits_down(n_expert):
        sizes.append(len(ids))
        ids = ids + [i ^ b for i in ids]

    def gather_expert(value):
        pieces = [value]
        for b in bits_down(n_expert):
            joined = pieces[0] if len(pieces) == 1 else jnp.concatenate(pieces, axis=0)
            pieces.append(swap(joined, 0, b))
        return pieces

    def scatter_expert(pieces):
        pieces = list(pieces)
        bits = bits_down(n_expert)
        for b in reversed(bits):
            got = swap(pieces.pop(), 0, b)
            if len(pieces) == 1:
                return [pieces[0], got]
            at, fresh = 0, []
            for piece in pieces:
                n = piece.shape[0]
                fresh.append((piece.astype(F32) + got[at : at + n].astype(F32)).astype(BF16))
                at += n
            pieces = fresh

    def gather_far(value, keep):
        mine = [value]
        for b in bits_down(nz):
            joined = mine[0] if len(mine) == 1 else jnp.concatenate(mine, axis=0)
            mine.append(swap(joined, b * ny, 0))
        far = jnp.concatenate(mine[1:], axis=0)
        pieces = [far]
        for b in bits_down(n_expert):
            joined = pieces[0] if len(pieces) == 1 else jnp.concatenate(pieces, axis=0)
            pieces.append(swap(joined, 0, b))
        return list(keep) + pieces

    def give_back(blocks):
        return [b if r == 0 else swap(b, 0, r) for r, b in zip(ids, blocks)]

    def finish_weights(grads):
        blocks = [grads[i] for i in range(ny)]
        half = ny // 2
        while half >= 1:
            got = swap(jnp.concatenate([b[None] for b in blocks[half:]], axis=0), half, 0)
            if half > 1:
                blocks = [
                    (blocks[i].astype(F32) + got[i].astype(F32)).astype(BF16) for i in range(half)
                ]
            else:
                return blocks[0].astype(F32) + got[0].astype(F32)
            half //= 2

    columns = jnp.stack(
        [encoder_route * cap + encoder_slot, decoder_route * cap + decoder_slot]
    ).reshape(2, 2, rows)
    near = gather_expert(columns[None])
    all_columns = gather_far(columns[None], near)
    near = jnp.concatenate(near, axis=0)
    all_columns = jnp.concatenate(all_columns, axis=0)
    near_cols = [near[:, l].reshape(-1, 1, rows) for l in range(2)]
    far_cols = [all_columns[:, l].reshape(-1, 1, rows) for l in range(2)]
    own_cols = [columns[l].reshape(2, rows, 1) for l in range(2)]
    sources = n_expert * nz

    gains = [norm_gains[i : i + 1] for i in range(6)]
    source_pieces = gather_expert(source)
    target_pieces = gather_expert(target)
    out_grad = output_grad.reshape(2, rows, feature)
    og = out_grad.astype(BF16)[None]
    og_near = gather_expert(og)
    og_all = gather_far(og, og_near)

    e1, u, *enc_saved = self_forward(
        source_pieces, ids, me1, gains[0], gains[1], attention_in[0], attention_out[0], False
    )
    u_near = gather_expert(u[None])
    u_all = gather_far(u[None], u_near)
    t1, hc, *dec_saved = self_forward(
        target_pieces, ids, me1, gains[3], gains[4], attention_in[1], attention_out[1], True
    )
    returned = give_back(expert_forward(u_near, near_cols[0], me1, encoder_up, encoder_down, ids))
    e2, memory = combine_norm(returned, ids, own_cols[0], me1, e1, gains[2])
    memory_near = gather_expert(memory[None])
    t2, w, *cross_saved = cross_forward(
        hc, memory_near, ids, t1, gains[5], attention_in[2], attention_out[2]
    )
    w_near = gather_expert(w[None])
    w_all = gather_far(w[None], w_near)
    dx_blocks, res_blocks = expert_backward(
        w_near, og_near, near_cols[1], me1, decoder_up, decoder_down, ids, True
    )

    dx_back = give_back(dx_blocks)
    res_back = give_back(res_blocks)
    *dmem, cross_dw, dt1, dg5, dg4 = cross_backward(
        dx_back,
        ids,
        sizes,
        own_cols[1],
        me1,
        t2,
        gains[5],
        out_grad,
        cross_saved,
        hc,
        t1,
        gains[4],
        attention_in[2],
        attention_out[2],
    )
    decoder_output = combine_output(res_back, ids, own_cols[1], me1, t2)
    dmem_parts = scatter_expert(dmem)
    fg, fg_low, dg2 = memory_backward(
        [d.reshape(2, rows, feature) for d in dmem_parts], e2, gains[2]
    )
    fg_near = gather_expert(fg_low[None])
    fg_all = gather_far(fg_low[None], fg_near)
    du_blocks, _ = expert_backward(
        u_near, fg_near, near_cols[0], me1, encoder_up, encoder_down, ids, False
    )
    du_back = give_back(du_blocks)
    *dht, dec_dw = self_backward(
        dt1, ids, sizes, me1, dec_saved, attention_in[1], attention_out[1], True
    )
    target_grad, dg3 = input_backward(scatter_expert(dht), target[0], gains[3], dt1)
    dec_up_g, dec_down_g = expert_weights(
        w_all, og_all, far_cols[1], place, decoder_up, decoder_down, sources, ny, nz
    )
    *dhs, enc_dw, de1, dg1 = encoder_backward(
        du_back,
        ids,
        sizes,
        own_cols[0],
        me1,
        e1,
        gains[1],
        fg,
        enc_saved,
        attention_in[0],
        attention_out[0],
    )
    source_grad, dg0 = input_backward(scatter_expert(dhs), source[0], gains[0], de1)
    enc_up_g, enc_down_g = expert_weights(
        u_all, fg_all, far_cols[0], place, encoder_up, encoder_down, sources, ny, nz
    )

    counts = jnp.sum(
        (
            jnp.stack([encoder_route, decoder_route]).reshape(2, 2, rows, 1)
            == jnp.arange(EXPERTS, dtype=jnp.int32)
        ).astype(F32),
        axis=2,
    )
    gain_grads = jnp.concatenate([dg0, dg1, dg2, dg3, dg4, dg5], axis=0)
    dw = jnp.stack([enc_dw, dec_dw, cross_dw])
    dw = lax.psum(dw, AXES).astype(F32)
    gain_grads, counts = lax.psum((gain_grads, counts), AXES)

    return (
        decoder_output.reshape(2, 1, rows, feature),
        source_grad[None],
        target_grad[None],
        dw[..., : 3 * feature],
        dw[..., 3 * feature :],
        gain_grads,
        finish_weights(enc_up_g),
        finish_weights(enc_down_g),
        finish_weights(dec_up_g),
        finish_weights(dec_down_g),
        counts.astype(jnp.int32),
    )


def solution(mesh):
    n_dp, n_expert = mesh.shape["dp"], mesh.shape["expert"]
    in_specs = (
        P("dp", "expert", None),
        P("dp", "expert", None),
        P(),
        P(),
        P(),
        P("expert", None, None),
        P("expert", None, None),
        P("expert", None, None),
        P("expert", None, None),
        P(None, "dp", "expert"),
        P(None, "dp", "expert"),
        P(None, "dp", "expert"),
        P(None, "dp", "expert"),
        P(None, "dp", "expert", None),
    )
    out_specs = (
        P(None, "dp", "expert", None),
        P("dp", "expert", None),
        P("dp", "expert", None),
        P(),
        P(),
        P(),
        P("expert", "dp", None),
        P("expert", "dp", None),
        P("expert", "dp", None),
        P("expert", "dp", None),
        P(),
    )
    return jax.shard_map(
        functools.partial(local, n_dp, n_expert),
        mesh=mesh,
        in_specs=in_specs,
        out_specs=out_specs,
        check_vma=False,
    )
```

```python
import functools

import jax
import jax.numpy as jnp
from jax import lax
from jax.experimental import pallas as pl
from jax.experimental.pallas import tpu as pltpu
from jax.sharding import PartitionSpec as P

HEAD_DIM = 64
EXPERTS = 16
NORM_EPSILON = 1e-05
MASKED = -1e30
F32 = jnp.float32
BF16 = jnp.bfloat16
VMEM_LIMIT = 58 << 20
MEASURED_US = {'self_forward': 12.4, 'self_backward': 14.5, 'expert_forward': 10.6, 'expert_backward': 14.5, 'expert_weights': 21, 'combine_norm': 3.4, 'combine_output': 3.4, 'cross_forward': 21, 'cross_backward': 28, 'memory_backward': 3.4, 'encoder_backward': 16, 'input_backward': 2.5}


def nn(a, b):
    return jnp.dot(a, b, preferred_element_type=F32)


def nt(a, b):
    return lax.dot_general(a, b, (((1,), (1,)), ((), ())), preferred_element_type=F32)


def tn(a, b):
    return lax.dot_general(a, b, (((0,), (0,)), ((), ())), preferred_element_type=F32)


def tt(a, b):
    return lax.dot_general(a, b, (((0,), (1,)), ((), ())), preferred_element_type=F32)


def norm_parts(x):
    mean = jnp.mean(x, axis=-1, keepdims=True)
    centered = x - mean
    spread = jnp.mean(centered * centered, axis=-1, keepdims=True)
    scale = lax.rsqrt(spread + NORM_EPSILON)
    return centered * scale, scale


def norm(x, gain):
    return norm_parts(x)[0] * gain


def norm_back(x, gain, grad):
    hat, scale = norm_parts(x)
    inner = grad * gain
    dx = scale * (
        inner
        - jnp.mean(inner, axis=-1, keepdims=True)
        - hat * jnp.mean(inner * hat, axis=-1, keepdims=True)
    )
    return dx, jnp.sum(grad * hat, axis=0, keepdims=True)


GELU_A = 0.7978845608028654
GELU_B = 0.044715


def gelu(x):
    return 0.5 * x * (1.0 + jnp.tanh(GELU_A * (x + GELU_B * (x * x * x))))


def gelu_both(x):
    sq = x * x
    th = jnp.tanh(x * (GELU_A + (GELU_A * GELU_B) * sq))
    half = 0.5 * (1.0 + th)
    slope = half + (0.5 * x) * (1.0 - th * th) * (GELU_A + (3.0 * GELU_A * GELU_B) * sq)
    return x * half, slope


def whole(shape):
    return pl.BlockSpec(shape, lambda *_: (0,) * len(shape))


def call(body, ins, outs, name, grid=None, in_specs=None, out_specs=None, scratch=(), scalars=(), flops=0, collective_id=None):
    if in_specs is None:
        in_specs = [None] * len(ins)
    if out_specs is None:
        out_specs = [None] * len(outs)
    in_specs = [whole(a.shape) if s is None else s for a, s in zip(ins, in_specs)]
    out_specs = [whole(o[0]) if s is None else s for o, s in zip(outs, out_specs)]
    moved = sum(a.size * a.dtype.itemsize for a in ins) + sum(
        functools.reduce(lambda x, y: x * y, o[0], 1) * jnp.dtype(o[1]).itemsize for o in outs
    )
    spec = pltpu.PrefetchScalarGridSpec(
        num_scalar_prefetch=len(scalars),
        grid=(1,) if grid is None else grid,
        in_specs=in_specs,
        out_specs=out_specs,
        scratch_shapes=list(scratch),
    )
    return pl.pallas_call(
        body,
        out_shape=[jax.ShapeDtypeStruct(s, d) for s, d in outs],
        grid_spec=spec,
        name=name,
        compiler_params=pltpu.CompilerParams(
            vmem_limit_bytes=VMEM_LIMIT, collective_id=collective_id, has_side_effects=collective_id is not None
        ),
        cost_estimate=pl.CostEstimate(flops=int(MEASURED_US[name] * 1.15e9), bytes_accessed=moved, transcendentals=0),
    )(*scalars, *ins)


MESH = pl.DeviceIdType.MESH


def xor(value, bits):
    b = 1
    while b <= bits:
        if bits & b:
            value = value + b * (1 - 2 * lax.rem(lax.div(value, b), 2))
        b *= 2
    return value


def peer(dp_bits, expert_bits):
    return (xor(lax.axis_index("dp"), dp_bits), xor(lax.axis_index("expert"), expert_bits))


def greet(peers):
    barrier = pltpu.get_barrier_semaphore()
    for p in peers:
        pl.semaphore_signal(barrier, inc=1, device_id=peer(*p), device_id_type=MESH)
    pl.semaphore_wait(barrier, len(peers))


def send(src, dst, send_sem, recv_sem, to):
    return pltpu.make_async_remote_copy(
        src_ref=src, dst_ref=dst, send_sem=send_sem, recv_sem=recv_sem, device_id=peer(*to), device_id_type=MESH
    )


class Gather:
    def __init__(self, ids, own, near, send_sems, recv_sems):
        self.pos = {r: i for i, r in enumerate(ids)}
        self.far = [r for r in ids if r % 2 == 0 and r > 0]
        self.own, self.near, self.sems = own, near, (send_sems, recv_sems)

    def copy(self, r, src, to):
        at = self.pos[r]
        return send(src, self.near.at[at], self.sems[0].at[at], self.sems[1].at[at], (0, to))

    def first(self, r):
        return self.copy(r, self.own, r)

    def second(self, r):
        return self.copy(r ^ 1, self.near.at[self.pos[r]], 1)

    def start(self):
        for r in self.far:
            self.first(r).start()
        self.first(1).start()

    def forward(self):
        for r in self.far:
            self.first(r).wait_recv()
            self.second(r).start()

    def finish(self):
        for r in self.far:
            self.second(r).wait_recv()
        self.first(1).wait_recv()
        for r in self.far:
            self.first(r).wait_send()
            self.second(r).wait_send()
        self.first(1).wait_send()


def head_rows(values, h):
    rows = values[h * HEAD_DIM : (h + 1) * HEAD_DIM]
    zero = jnp.zeros_like(rows)
    return jnp.concatenate([rows, zero] if h % 2 == 0 else [zero, rows], axis=0)


def head_lanes(values, h):
    pair = values[:, (h // 2) * 128 : (h // 2 + 1) * 128]
    lane = lax.broadcasted_iota(jnp.int32, pair.shape, 1)
    keep = lane < HEAD_DIM if h % 2 == 0 else lane >= HEAD_DIM
    return jnp.where(keep, pair, jnp.zeros_like(pair))


def causal_allow(me, ids, rows):
    parts = []
    for r in ids:
        key = (me ^ r) * rows + lax.broadcasted_iota(jnp.int32, (rows, rows), 0)
        query = me * rows + lax.broadcasted_iota(jnp.int32, (rows, rows), 1)
        parts.append(key <= query)
    return jnp.concatenate([p.astype(F32) for p in parts], axis=0) > 0.5


def attend_forward(q_t, k, v_t, allow, o_t, lse):
    heads = q_t.shape[0] // HEAD_DIM
    for h in range(heads):
        pair = slice((h // 2) * 128, (h // 2 + 1) * 128)
        scores = nn(k[:, pair], head_rows(q_t, h))
        if allow is not None:
            scores = jnp.where(allow, scores, MASKED)
        top = jnp.max(scores, axis=0, keepdims=True)
        lifted = jnp.exp(scores - top)
        total = jnp.sum(lifted, axis=0, keepdims=True)
        rows = slice(h * HEAD_DIM, (h + 1) * HEAD_DIM)
        blended = nn(v_t[rows, :], lifted.astype(BF16)) * (1.0 / total)
        o_t[rows, :] = blended.astype(BF16)
        lse[h : h + 1, :] = top + jnp.log(total)


def attend_backward(q, k, v, k_t, do, lse, allow, dk, dv, dq_t):
    heads = q.shape[1] // HEAD_DIM
    q_t = q.astype(F32).T.astype(BF16)
    do_t = do.astype(F32).T.astype(BF16)
    for h2 in range(heads // 2):
        pair = slice(h2 * 128, (h2 + 1) * 128)
        dk_pair = None
        for h in (2 * h2, 2 * h2 + 1):
            rows = slice(h * HEAD_DIM, (h + 1) * HEAD_DIM)
            scores = nn(k[:, pair], head_rows(q_t, h))
            weights = jnp.exp(scores - lse[h : h + 1, :])
            if allow is not None:
                weights = jnp.where(allow, weights, 0.0)
            weights_grad = nn(v[:, pair], head_rows(do_t, h))
            centre = jnp.sum(weights * weights_grad, axis=0, keepdims=True)
            scores_grad = (weights * (weights_grad - centre)).astype(BF16)
            dv_part = nn(weights.astype(BF16), head_lanes(do, h))
            dk_part = nn(scores_grad, head_lanes(q, h))
            dq_t[rows, :] = (nn(k_t[rows, :], scores_grad) * HEAD_DIM ** (-0.5)).astype(BF16)
            if dk_pair is None:
                dk_pair, dv_pair = dk_part, dv_part
            else:
                dk_pair, dv_pair = dk_pair + dk_part, dv_pair + dv_part
        dk[:, pair] = dk_pair.astype(BF16)
        dv[:, pair] = dv_pair.astype(BF16)


def piece_blocks(pieces):
    return [(ref, i) for ref in pieces for i in range(ref.shape[0])]


def self_forward(pieces, ids, me, gain, gain_next, inward, outward, causal):
    rows, feature = pieces[0].shape[1:]
    length = len(ids) * rows
    heads = feature // HEAD_DIM
    count = len(pieces)

    def body(me_ref, *refs):
        parts = refs[:count]
        g, gn, win, wout, out, nxt, hm, k, k_t, v, q, o_t, lse, v_t = refs[count:]
        for b, (ref, i) in enumerate(piece_blocks(parts)):
            hm[b * rows : (b + 1) * rows, :] = norm(ref[i].astype(F32), g[...]).astype(BF16)
        hm_all = hm[...]
        k[...] = nn(hm_all, win[:, feature : 2 * feature]).astype(BF16)
        v[...] = nn(hm_all, win[:, 2 * feature :]).astype(BF16)
        k_t[...] = tt(win[:, feature : 2 * feature], hm_all).astype(BF16)
        v_t[...] = tt(win[:, 2 * feature :], hm_all).astype(BF16)
        q_scaled = nn(hm[0:rows, :], win[:, :feature]).astype(BF16).astype(F32) * HEAD_DIM ** (-0.5)
        q[...] = q_scaled.astype(BF16)
        allow = causal_allow(me_ref[0], ids, rows) if causal else None
        attend_forward(q_scaled.T.astype(BF16), k, v_t, allow, o_t, lse)
        merged = o_t[...].astype(F32).T.astype(BF16)
        after = parts[0][0].astype(F32) + nn(merged, wout[...])
        out[...] = after
        nxt[...] = norm(after, gn[...]).astype(BF16)

    return call(
        body,
        [*pieces, gain, gain_next, inward, outward],
        [
            ((rows, feature), F32),
            ((rows, feature), BF16),
            ((length, feature), BF16),
            ((length, feature), BF16),
            ((feature, length), BF16),
            ((length, feature), BF16),
            ((rows, feature), BF16),
            ((feature, rows), BF16),
            ((heads, rows), F32),
        ],
        "self_forward",
        scratch=[pltpu.VMEM((feature, length), BF16)],
        scalars=[me],
        flops=2 * length * feature * (4 * feature + 4 * rows),
    )


def weight_grad_store(dw, feature, hq, hm, dq, dk, dv, o_t, d_branch):
    dw[:, :feature] = tn(hq, dq).astype(BF16)
    dw[:, feature : 2 * feature] = tn(hm, dk).astype(BF16)
    dw[:, 2 * feature : 3 * feature] = tn(hm, dv).astype(BF16)
    dw[:, 3 * feature :] = nn(o_t, d_branch).astype(BF16)


def store_blocks(outs, values, rows):
    for b, (ref, i) in enumerate(piece_blocks(outs)):
        ref[i] = values[b * rows : (b + 1) * rows].astype(BF16)


def self_backward_core(me_ref, ids, causal, d_branch, saved, win, wout, outs, dw, scratch):
    hm, k, k_t, v, q, o_t, lse = saved
    dk, dv, dq_t = scratch
    rows, feature = q.shape
    do = nt(d_branch, wout[...]).astype(BF16)
    allow = causal_allow(me_ref[0], ids, rows) if causal else None
    attend_backward(q[...], k, v, k_t, do, lse, allow, dk, dv, dq_t)
    dq = dq_t[...].astype(F32).T.astype(BF16)
    for b, (ref, i) in enumerate(piece_blocks(outs)):
        span = slice(b * rows, (b + 1) * rows)
        part = nt(dk[span, :], win[:, feature : 2 * feature]) + nt(dv[span, :], win[:, 2 * feature :])
        if b == 0:
            part = part + nt(dq, win[:, :feature])
        ref[i] = part.astype(BF16)
    weight_grad_store(dw, feature, hm[0:rows, :], hm[...], dq, dk[...], dv[...], o_t[...], d_branch)


def self_backward(upstream, ids, sizes, me, saved, inward, outward, causal):
    rows, feature = upstream.shape
    length = len(ids) * rows
    count = len(sizes)

    def body(me_ref, up, hm, k, k_t, v, q, o_t, lse, win, wout, *refs):
        outs, dw, scratch = refs[:count], refs[count], refs[count + 1 :]
        self_backward_core(
            me_ref, ids, causal, up[...].astype(BF16), (hm, k, k_t, v, q, o_t, lse), win, wout, outs, dw, scratch
        )

    return call(
        body,
        [upstream, *saved, inward, outward],
        [((n, rows, feature), BF16) for n in sizes] + [((feature, 4 * feature), BF16)],
        "self_backward",
        scratch=[
            pltpu.VMEM((length, feature), BF16),
            pltpu.VMEM((length, feature), BF16),
            pltpu.VMEM((feature, rows), BF16),
        ],
        scalars=[me],
        flops=2 * length * feature * (4 * feature + 10 * rows),
    )


def gather_rows(me, experts, cap, col, returned):
    total = None
    slots = experts * cap
    for r, rows in returned:
        local = col - xor(me, r) * slots
        hot = (local == lax.broadcasted_iota(jnp.int32, (col.shape[0], slots), 1)).astype(BF16)
        part = nn(hot, rows.reshape(slots, rows.shape[-1]))
        total = part if total is None else total + part
    return total


def spread_rows(me, experts, cap, col, tokens):
    slots = experts * cap
    local = col - me * slots
    hot = (local == lax.broadcasted_iota(jnp.int32, (slots, col.shape[1]), 0)).astype(BF16)
    return nn(hot, tokens).astype(BF16)


def fill_buffers(me, experts, cap, cols, token_of, sources, dest):
    for s in range(sources):
        for p in range(2):
            rows = spread_rows(me, experts, cap, cols[2 * s + p], token_of(s, p))
            at = (2 * s + p) * cap
            for j in range(experts):
                dest[j, at : at + cap, :] = rows[j * cap : (j + 1) * cap]


def expert_forward(own, cols, own_col, residual, gain, weight_up, weight_down, ids):
    experts, hidden, feature = weight_up.shape
    rows = own.shape[1]
    cap = 2 * rows // EXPERTS
    sources = len(ids)
    length = sources * 2 * cap

    def body(u, col, mine, res, g, up, down, out, nxt, near_out, near, buf, stage, ret, gs, gr, rs, rr, ls):
        me = lax.axis_index("expert")
        j = pl.program_id(0)
        gather = Gather(ids, near.at[0], near, gs, gr)
        keep = pltpu.make_async_copy(near, near_out, ls)

        def back(s, n):
            return send(stage.at[s, n], ret.at[s, n], rs.at[s, n], rr.at[s, n], (0, ids[s]))

        @pl.when(j == 0)
        def _():
            near[0] = u[0]
            greet([(0, r) for r in ids[1:]])
            gather.start()
            gather.forward()
            gather.finish()
            keep.start()
            fill_buffers(me, experts, cap, col, lambda s, p: near[s], sources, buf)

        act = gelu(nt(buf[j], up[0])).astype(BF16)
        got = nn(act, down[0]).astype(BF16)
        for s in range(sources):
            for p in range(2):
                at = (2 * s + p) * cap
                if s == 0:
                    ret[s, j, p] = got[at : at + cap]
                else:
                    stage[s, j, p] = got[at : at + cap]
        for s in range(1, sources):
            back(s, j).start()

        @pl.when(j == experts - 1)
        def _():
            for s in range(1, sources):
                for n in range(experts):
                    back(s, n).wait()
            for p in range(2):
                mixed = gather_rows(me, experts, cap, mine[p], [(r, ret[i, :, p]) for i, r in enumerate(ids)])
                after = res[...] + mixed
                out[p] = after
                nxt[p] = norm(after, g[...]).astype(BF16)
            keep.wait()

    weight = pl.BlockSpec((1, hidden, feature), lambda j, *_: (j, 0, 0))
    dma = pltpu.SemaphoreType.DMA
    return call(
        body,
        [own, cols, own_col, residual, gain, weight_up, weight_down],
        [((2, rows, feature), F32), ((2, rows, feature), BF16), ((sources, rows, feature), BF16)],
        "expert_forward",
        grid=(experts,),
        in_specs=[None] * 5 + [weight, weight],
        out_specs=[None, None, pl.BlockSpec(memory_space=pl.ANY)],
        scratch=[
            pltpu.VMEM((sources, rows, feature), BF16),
            pltpu.VMEM((experts, length, feature), BF16),
            pltpu.VMEM((sources, experts, 2, cap, feature), BF16),
            pltpu.VMEM((sources, experts, 2, cap, feature), BF16),
            dma((sources,)),
            dma((sources,)),
            dma((sources, experts)),
            dma((sources, experts)),
            dma,
        ],
        flops=4 * experts * length * hidden * feature,
        collective_id=2,
    )


def expert_backward(pieces, grads, cols, me, weight_up, weight_down, ids, with_result):
    experts, hidden, feature = weight_up.shape
    rows = grads[0].shape[2]
    cap = 2 * rows // EXPERTS
    count, gcount = len(pieces), len(grads)
    sources = len(ids)
    length = sources * 2 * cap
    both = pieces[0].ndim == 4
    kinds = 2 if with_result else 1

    def body(me_ref, *refs):
        parts = refs[:count]
        gparts = refs[count : count + gcount]
        col, up, down = refs[count + gcount : count + gcount + 3]
        outs = refs[count + gcount + 3 : count + gcount + 3 + kinds * sources]
        buf, gbuf = refs[-2:]
        j = pl.program_id(0)

        @pl.when(j == 0)
        def _():
            blocks = piece_blocks(parts)
            gblocks = piece_blocks(gparts)
            pick = lambda s, p: blocks[s][0][blocks[s][1], p] if both else blocks[s][0][blocks[s][1]]
            fill_buffers(me_ref[0], experts, cap, col, pick, sources, buf)
            gpick = lambda s, p: gblocks[s][0][gblocks[s][1], p]
            fill_buffers(me_ref[0], experts, cap, col, gpick, sources, gbuf)

        value, slope = gelu_both(nt(buf[j], up[0]))
        hidden_grad = (slope * nt(gbuf[j], down[0])).astype(BF16)
        dx = nn(hidden_grad, up[0]).astype(BF16)
        results = [dx]
        if with_result:
            results.append(nn(value.astype(BF16), down[0]).astype(BF16))
        for n, res in enumerate(results):
            for s in range(sources):
                for p in range(2):
                    at = (2 * s + p) * cap
                    outs[n * sources + s][0, p] = res[at : at + cap]

    weight = pl.BlockSpec((1, hidden, feature), lambda j, *_: (j, 0, 0))
    outs = call(
        body,
        [*pieces, *grads, cols, weight_up, weight_down],
        [((experts, 2, cap, feature), BF16)] * (kinds * sources),
        "expert_backward",
        grid=(experts,),
        in_specs=[None] * (count + gcount + 1) + [weight, weight],
        out_specs=[pl.BlockSpec((1, 2, cap, feature), lambda j, *_: (j, 0, 0, 0))] * (kinds * sources),
        scratch=[pltpu.VMEM((experts, length, feature), BF16)] * 2,
        scalars=[me],
        flops=(8 if with_result else 6) * experts * length * hidden * feature,
    )
    return outs[:sources], outs[sources:]


def expert_weights(pieces, grads, cols, place, weight_up, weight_down, sources, ny, nz):
    experts, hidden, feature = weight_up.shape
    rows = grads[0].shape[2]
    cap = 2 * rows // EXPERTS
    count, gcount = len(pieces), len(grads)
    length = sources * 2 * cap
    both = pieces[0].ndim == 4
    span = hidden // (ny * nz)

    def body(place_ref, *refs):
        parts = refs[:count]
        gparts = refs[count : count + gcount]
        col, up, down = refs[count + gcount : count + gcount + 3]
        up_out, down_out, buf, gbuf = refs[count + gcount + 3 :]
        j = pl.program_id(0)

        @pl.when((j == 0) & (pl.program_id(1) == 0))
        def _():
            blocks = piece_blocks(parts)
            gblocks = piece_blocks(gparts)
            pick = lambda s, p: blocks[s][0][blocks[s][1], p] if both else blocks[s][0][blocks[s][1]]
            fill_buffers(place_ref[0], experts, cap, col, pick, sources, buf)
            gpick = lambda s, p: gblocks[s][0][gblocks[s][1], p]
            fill_buffers(place_ref[0], experts, cap, col, gpick, sources, gbuf)

        x, g = buf[j], gbuf[j]
        value, slope = gelu_both(nt(up[0], x))
        hidden_grad = (slope * nt(down[0], g)).astype(BF16)
        up_out[0, 0] = nn(hidden_grad, x).astype(BF16)
        down_out[0, 0] = nn(value.astype(BF16), g).astype(BF16)

    weight = pl.BlockSpec((1, span, feature), lambda j, r, place_ref: (j, place_ref[1] * ny + (place_ref[2] ^ r), 0))
    out = pl.BlockSpec((1, 1, span, feature), lambda j, r, *_: (r, j, 0, 0))
    return call(
        body,
        [*pieces, *grads, cols, weight_up, weight_down],
        [((ny, experts, span, feature), BF16)] * 2,
        "expert_weights",
        grid=(experts, ny),
        in_specs=[None] * (count + gcount + 1) + [weight, weight],
        out_specs=[out, out],
        scratch=[pltpu.VMEM((experts, length, feature), BF16)] * 2,
        scalars=[place],
        flops=8 * experts * length * (hidden // nz) * feature,
    )


def combine_output(returned, ids, col, me, residual):
    experts, _, cap, feature = returned[0].shape
    rows = residual.shape[-2]
    count = len(ids)

    def body(me_ref, *refs):
        ret = refs[:count]
        c, res, out = refs[count:]
        for p in range(2):
            mixed = gather_rows(me_ref[0], experts, cap, c[p], [(r, ref[:, p]) for r, ref in zip(ids, ret)])
            out[p] = (res[p] + mixed).astype(BF16)

    return call(
        body,
        [*returned, col, residual],
        [((2, rows, feature), BF16)],
        "combine_output",
        scalars=[me],
        flops=4 * rows * EXPERTS * cap * feature,
    )[0]


def cross_forward(hc, pieces, ids, mid, gain, inward, outward):
    rows, feature = hc.shape
    length = len(ids) * rows
    heads = feature // HEAD_DIM
    count = len(pieces)

    def body(*refs):
        h, *parts = refs[: count + 1]
        res, g, win, wout, out, nxt, hm, k, k_t, v, q, o_t, lse, v_t = refs[count + 1 :]
        for b, (ref, i) in enumerate(piece_blocks(parts)):
            hm[0, b * rows : (b + 1) * rows, :] = ref[i, 0]
        hm_all = hm[0]
        k[0] = nn(hm_all, win[:, feature : 2 * feature]).astype(BF16)
        v[0] = nn(hm_all, win[:, 2 * feature :]).astype(BF16)
        k_t[0] = tt(win[:, feature : 2 * feature], hm_all).astype(BF16)
        v_t[...] = tt(win[:, 2 * feature :], hm_all).astype(BF16)
        q_scaled = nn(h[...], win[:, :feature]).astype(BF16).astype(F32) * HEAD_DIM ** (-0.5)
        q[...] = q_scaled.astype(BF16)
        attend_forward(q_scaled.T.astype(BF16), k.at[0], v_t, None, o_t.at[0], lse.at[0])
        merged = o_t[0].astype(F32).T.astype(BF16)
        after = res[...] + nn(merged, wout[...])
        out[0] = after
        nxt[0] = norm(after, g[...]).astype(BF16)

    per = lambda *shape: pl.BlockSpec((1,) + shape, lambda p, *_: (p,) + (0,) * len(shape))
    return call(
        body,
        [hc, *pieces, mid, gain, inward, outward],
        [
            ((2, rows, feature), F32),
            ((2, rows, feature), BF16),
            ((2, length, feature), BF16),
            ((2, length, feature), BF16),
            ((2, feature, length), BF16),
            ((2, length, feature), BF16),
            ((rows, feature), BF16),
            ((2, feature, rows), BF16),
            ((2, heads, rows), F32),
        ],
        "cross_forward",
        grid=(2,),
        in_specs=[None]
        + [pl.BlockSpec((a.shape[0], 1, rows, feature), lambda p, *_: (0, p, 0, 0)) for a in pieces]
        + [None] * 4,
        out_specs=[
            per(rows, feature),
            per(rows, feature),
            per(length, feature),
            per(length, feature),
            per(feature, length),
            per(length, feature),
            None,
            per(feature, rows),
            per(heads, rows),
        ],
        scratch=[pltpu.VMEM((feature, length), BF16)],
        flops=4 * length * feature * (4 * feature + 4 * rows),
    )


def cross_backward(returned, ids, sizes, col, me, crossed, gain_w, out_grad, saved, hc, mid, gain_c, inward, outward):
    experts, _, cap, feature = returned[0].shape
    rows = mid.shape[0]
    length = len(ids) * rows
    heads = feature // HEAD_DIM
    count = len(ids)
    npieces = len(sizes)

    def body(me_ref, *refs):
        ret = refs[:count]
        c, t2, gw, og, hm, k, k_t, v, q, o_t, lse, h, t1, gc, win, wout = refs[count : count + 16]
        rest = refs[count + 16 :]
        outs = rest[:npieces]
        dw, dt1, dgw, dgc = rest[npieces : npieces + 4]
        dk, dv, dq_t, dw_acc, dh_acc = rest[npieces + 4 :]
        p = pl.program_id(0)
        dwr = gather_rows(me_ref[0], experts, cap, c[0], [(r, ref[:, 0]) for r, ref in zip(ids, ret)])
        dx, dg = norm_back(t2[0], gw[...], dwr)
        upstream = og[0] + dx
        d_branch = upstream.astype(BF16)
        do = nt(d_branch, wout[...]).astype(BF16)
        attend_backward(q[...], k.at[0], v.at[0], k_t.at[0], do, lse.at[0], None, dk, dv, dq_t)
        dq = dq_t[...].astype(F32).T.astype(BF16)
        for b, (ref, i) in enumerate(piece_blocks(outs)):
            span = slice(b * rows, (b + 1) * rows)
            part = nt(dk[span, :], win[:, feature : 2 * feature]) + nt(dv[span, :], win[:, 2 * feature :])
            ref[i, 0] = part.astype(BF16)
        dh = nt(dq, win[:, :feature])
        grads = [
            tn(h[...], dq),
            tn(hm[0], dk[...]),
            tn(hm[0], dv[...]),
            nn(o_t[0], d_branch),
        ]

        @pl.when(p == 0)
        def _():
            for n, value in enumerate(grads):
                dw_acc[:, n * feature : (n + 1) * feature] = value
            dh_acc[...] = dh
            dt1[...] = upstream
            dgw[...] = dg

        @pl.when(p == 1)
        def _():
            for n, value in enumerate(grads):
                at = slice(n * feature, (n + 1) * feature)
                dw[:, at] = (dw_acc[:, at] + value).astype(BF16)
            back, dg_c = norm_back(t1[...], gc[...], dh_acc[...] + dh)
            dt1[...] = dt1[...] + upstream + back
            dgw[...] = dgw[...] + dg
            dgc[...] = dg_c

    per = lambda *shape: pl.BlockSpec((1,) + shape, lambda p, *_: (p,) + (0,) * len(shape))
    return call(
        body,
        [*returned, col, crossed, gain_w, out_grad, *saved, hc, mid, gain_c, inward, outward],
        [((n, 2, rows, feature), BF16) for n in sizes]
        + [((feature, 4 * feature), BF16), ((rows, feature), F32), ((1, feature), F32), ((1, feature), F32)],
        "cross_backward",
        grid=(2,),
        in_specs=[pl.BlockSpec((experts, 1, cap, feature), lambda p, *_: (0, p, 0, 0))] * count
        + [
            per(rows, 1),
            per(rows, feature),
            None,
            per(rows, feature),
            per(length, feature),
            per(length, feature),
            per(feature, length),
            per(length, feature),
            None,
            per(feature, rows),
            per(heads, rows),
            None,
            None,
            None,
            None,
            None,
        ],
        out_specs=[pl.BlockSpec((n, 1, rows, feature), lambda p, *_: (0, p, 0, 0)) for n in sizes] + [None] * 4,
        scratch=[
            pltpu.VMEM((length, feature), BF16),
            pltpu.VMEM((length, feature), BF16),
            pltpu.VMEM((feature, rows), BF16),
            pltpu.VMEM((feature, 4 * feature), F32),
            pltpu.VMEM((rows, feature), F32),
        ],
        scalars=[me],
        flops=4 * length * feature * (4 * feature + 10 * rows),
    )


def memory_backward(parts, final, gain):
    _, rows, feature = final.shape
    count = len(parts)

    def body(*refs):
        p = refs[:count]
        x, g, out, low, dg = refs[count:]
        total = None
        for n in range(2):
            grad = p[0][n].astype(F32)
            for other in p[1:]:
                grad = grad + other[n].astype(F32)
            dx, dgain = norm_back(x[n], g[...], grad)
            out[n] = dx
            low[n] = dx.astype(BF16)
            total = dgain if total is None else total + dgain
        dg[...] = total

    return call(
        body,
        [*parts, final, gain],
        [((2, rows, feature), F32), ((2, rows, feature), BF16), ((1, feature), F32)],
        "memory_backward",
    )


def encoder_backward(returned, ids, sizes, col, me, attended, gain, final_grad, saved, inward, outward):
    experts, _, cap, feature = returned[0].shape
    rows = attended.shape[0]
    length = len(ids) * rows
    count = len(ids)
    npieces = len(sizes)

    def body(me_ref, *refs):
        ret = refs[:count]
        c, e1, g, fg, hm, k, k_t, v, q, o_t, lse, win, wout = refs[count : count + 13]
        rest = refs[count + 13 :]
        outs = rest[:npieces]
        dw, de1, dg = rest[npieces : npieces + 3]
        scratch = rest[npieces + 3 :]
        du = None
        for p in range(2):
            part = gather_rows(me_ref[0], experts, cap, c[p], [(r, ref[:, p]) for r, ref in zip(ids, ret)])
            du = part if du is None else du + part
        dx, dgain = norm_back(e1[...], g[...], du)
        upstream = fg[0] + fg[1] + dx
        de1[...] = upstream
        dg[...] = dgain
        self_backward_core(
            me_ref, ids, False, upstream.astype(BF16), (hm, k, k_t, v, q, o_t, lse), win, wout, outs, dw, scratch
        )

    return call(
        body,
        [*returned, col, attended, gain, final_grad, *saved, inward, outward],
        [((n, rows, feature), BF16) for n in sizes]
        + [((feature, 4 * feature), BF16), ((rows, feature), F32), ((1, feature), F32)],
        "encoder_backward",
        scratch=[
            pltpu.VMEM((length, feature), BF16),
            pltpu.VMEM((length, feature), BF16),
            pltpu.VMEM((feature, rows), BF16),
        ],
        scalars=[me],
        flops=2 * length * feature * (4 * feature + 10 * rows),
    )


def input_backward(parts, values, gain, upstream):
    rows, feature = upstream.shape
    count = len(parts)

    def body(*refs):
        p = refs[:count]
        x, g, up, out, dg = refs[count:]
        grad = p[0][...].reshape(rows, feature).astype(F32)
        for other in p[1:]:
            grad = grad + other[...].reshape(rows, feature).astype(F32)
        dx, dgain = norm_back(x[...].astype(F32), g[...], grad)
        out[...] = up[...] + dx
        dg[...] = dgain

    return call(
        body,
        [*parts, values, gain, upstream],
        [((rows, feature), F32), ((1, feature), F32)],
        "input_backward",
    )


AXES = ("dp", "expert")


def flip(value, n_dp, n_expert, dp_bits, expert_bits):
    pairs = []
    for d in range(n_dp):
        for e in range(n_expert):
            pairs.append((d * n_expert + e, (d ^ dp_bits) * n_expert + (e ^ expert_bits)))
    return lax.ppermute(value, AXES, pairs)


def bits_down(n):
    out, b = [], n // 2
    while b >= 1:
        out.append(b)
        b //= 2
    return out


def local(
    n_dp,
    n_expert,
    source,
    target,
    attention_in,
    attention_out,
    norm_gains,
    encoder_up,
    encoder_down,
    decoder_up,
    decoder_down,
    encoder_route,
    encoder_slot,
    decoder_route,
    decoder_slot,
    output_grad,
):
    _, rows, feature = source.shape
    cap = 2 * rows // EXPERTS
    ny = 2 if n_dp <= 8 else 4
    nz = n_dp // ny
    me = lax.axis_index("expert").astype(jnp.int32)
    dp = lax.axis_index("dp").astype(jnp.int32)
    place = jnp.stack([me, dp // ny, dp % ny])
    me1 = me[None]
    swap = lambda v, d, e: flip(v, n_dp, n_expert, d, e)

    ids, sizes = [0], [1]
    for b in bits_down(n_expert):
        sizes.append(len(ids))
        ids = ids + [i ^ b for i in ids]

    def gather_expert(value):
        pieces = [value]
        for b in bits_down(n_expert):
            joined = pieces[0] if len(pieces) == 1 else jnp.concatenate(pieces, axis=0)
            pieces.append(swap(joined, 0, b))
        return pieces

    def scatter_expert(pieces):
        pieces = list(pieces)
        bits = bits_down(n_expert)
        for b in reversed(bits):
            got = swap(pieces.pop(), 0, b)
            if len(pieces) == 1:
                return [pieces[0], got]
            at, fresh = 0, []
            for piece in pieces:
                n = piece.shape[0]
                fresh.append((piece.astype(F32) + got[at : at + n].astype(F32)).astype(BF16))
                at += n
            pieces = fresh

    def gather_far(value, keep):
        mine = [value]
        for b in bits_down(nz):
            joined = mine[0] if len(mine) == 1 else jnp.concatenate(mine, axis=0)
            mine.append(swap(joined, b * ny, 0))
        far = jnp.concatenate(mine[1:], axis=0)
        pieces = [far]
        for b in bits_down(n_expert):
            joined = pieces[0] if len(pieces) == 1 else jnp.concatenate(pieces, axis=0)
            pieces.append(swap(joined, 0, b))
        return list(keep) + pieces

    def give_back(blocks):
        return [b if r == 0 else swap(b, 0, r) for r, b in zip(ids, blocks)]

    def finish_weights(grads):
        blocks = [grads[i] for i in range(ny)]
        half = ny // 2
        while half >= 1:
            got = swap(jnp.concatenate([b[None] for b in blocks[half:]], axis=0), half, 0)
            if half > 1:
                blocks = [
                    (blocks[i].astype(F32) + got[i].astype(F32)).astype(BF16) for i in range(half)
                ]
            else:
                return blocks[0].astype(F32) + got[0].astype(F32)
            half //= 2

    columns = jnp.stack(
        [encoder_route * cap + encoder_slot, decoder_route * cap + decoder_slot]
    ).reshape(2, 2, rows)
    near = gather_expert(columns[None])
    all_columns = gather_far(columns[None], near)
    near = jnp.concatenate(near, axis=0)
    all_columns = jnp.concatenate(all_columns, axis=0)
    near_cols = [near[:, l].reshape(-1, 1, rows) for l in range(2)]
    far_cols = [all_columns[:, l].reshape(-1, 1, rows) for l in range(2)]
    own_cols = [columns[l].reshape(2, rows, 1) for l in range(2)]
    sources = n_expert * nz

    gains = [norm_gains[i : i + 1] for i in range(6)]
    source_pieces = gather_expert(source)
    target_pieces = gather_expert(target)
    out_grad = output_grad.reshape(2, rows, feature)
    og = out_grad.astype(BF16)[None]
    og_near = gather_expert(og)
    og_all = gather_far(og, og_near)

    e1, u, *enc_saved = self_forward(
        source_pieces, ids, me1, gains[0], gains[1], attention_in[0], attention_out[0], False
    )
    t1, hc, *dec_saved = self_forward(
        target_pieces, ids, me1, gains[3], gains[4], attention_in[1], attention_out[1], True
    )
    e2, memory, u_near = expert_forward(
        u[None], near_cols[0], own_cols[0], e1, gains[2], encoder_up, encoder_down, ids
    )
    u_near = [u_near]
    u_all = gather_far(u[None], u_near)
    memory_near = gather_expert(memory[None])
    t2, w, *cross_saved = cross_forward(
        hc, memory_near, ids, t1, gains[5], attention_in[2], attention_out[2]
    )
    w_near = gather_expert(w[None])
    w_all = gather_far(w[None], w_near)
    dx_blocks, res_blocks = expert_backward(
        w_near, og_near, near_cols[1], me1, decoder_up, decoder_down, ids, True
    )

    dx_back = give_back(dx_blocks)
    res_back = give_back(res_blocks)
    *dmem, cross_dw, dt1, dg5, dg4 = cross_backward(
        dx_back,
        ids,
        sizes,
        own_cols[1],
        me1,
        t2,
        gains[5],
        out_grad,
        cross_saved,
        hc,
        t1,
        gains[4],
        attention_in[2],
        attention_out[2],
    )
    decoder_output = combine_output(res_back, ids, own_cols[1], me1, t2)
    dmem_parts = scatter_expert(dmem)
    fg, fg_low, dg2 = memory_backward(
        [d.reshape(2, rows, feature) for d in dmem_parts], e2, gains[2]
    )
    fg_near = gather_expert(fg_low[None])
    fg_all = gather_far(fg_low[None], fg_near)
    du_blocks, _ = expert_backward(
        u_near, fg_near, near_cols[0], me1, encoder_up, encoder_down, ids, False
    )
    du_back = give_back(du_blocks)
    *dht, dec_dw = self_backward(
        dt1, ids, sizes, me1, dec_saved, attention_in[1], attention_out[1], True
    )
    target_grad, dg3 = input_backward(scatter_expert(dht), target[0], gains[3], dt1)
    dec_up_g, dec_down_g = expert_weights(
        w_all, og_all, far_cols[1], place, decoder_up, decoder_down, sources, ny, nz
    )
    *dhs, enc_dw, de1, dg1 = encoder_backward(
        du_back,
        ids,
        sizes,
        own_cols[0],
        me1,
        e1,
        gains[1],
        fg,
        enc_saved,
        attention_in[0],
        attention_out[0],
    )
    source_grad, dg0 = input_backward(scatter_expert(dhs), source[0], gains[0], de1)
    enc_up_g, enc_down_g = expert_weights(
        u_all, fg_all, far_cols[0], place, encoder_up, encoder_down, sources, ny, nz
    )

    counts = jnp.sum(
        (
            jnp.stack([encoder_route, decoder_route]).reshape(2, 2, rows, 1)
            == jnp.arange(EXPERTS, dtype=jnp.int32)
        ).astype(F32),
        axis=2,
    )
    gain_grads = jnp.concatenate([dg0, dg1, dg2, dg3, dg4, dg5], axis=0)
    dw = jnp.stack([enc_dw, dec_dw, cross_dw])
    dw = lax.psum(dw, AXES).astype(F32)
    gain_grads, counts = lax.psum((gain_grads, counts), AXES)

    return (
        decoder_output.reshape(2, 1, rows, feature),
        source_grad[None],
        target_grad[None],
        dw[..., : 3 * feature],
        dw[..., 3 * feature :],
        gain_grads,
        finish_weights(enc_up_g),
        finish_weights(enc_down_g),
        finish_weights(dec_up_g),
        finish_weights(dec_down_g),
        counts.astype(jnp.int32),
    )


def solution(mesh):
    n_dp, n_expert = mesh.shape["dp"], mesh.shape["expert"]
    in_specs = (
        P("dp", "expert", None),
        P("dp", "expert", None),
        P(),
        P(),
        P(),
        P("expert", None, None),
        P("expert", None, None),
        P("expert", None, None),
        P("expert", None, None),
        P(None, "dp", "expert"),
        P(None, "dp", "expert"),
        P(None, "dp", "expert"),
        P(None, "dp", "expert"),
        P(None, "dp", "expert", None),
    )
    out_specs = (
        P(None, "dp", "expert", None),
        P("dp", "expert", None),
        P("dp", "expert", None),
        P(),
        P(),
        P(),
        P("expert", "dp", None),
        P("expert", "dp", None),
        P("expert", "dp", None),
        P("expert", "dp", None),
        P(),
    )
    return jax.shard_map(
        functools.partial(local, n_dp, n_expert),
        mesh=mesh,
        in_specs=in_specs,
        out_specs=out_specs,
        check_vma=False,
    )
```

```python
import functools

import jax
import jax.numpy as jnp
from jax import lax
from jax.experimental import pallas as pl
from jax.experimental.pallas import tpu as pltpu
from jax.sharding import PartitionSpec as P

HEAD_DIM = 64
EXPERTS = 16
NORM_EPSILON = 1e-05
MASKED = -1e30
F32 = jnp.float32
BF16 = jnp.bfloat16
VMEM_LIMIT = 60 << 20
MESH = pl.DeviceIdType.MESH
DMA = pltpu.SemaphoreType.DMA


def nn(a, b):
    return jnp.dot(a, b, preferred_element_type=F32)


def nt(a, b):
    return lax.dot_general(a, b, (((1,), (1,)), ((), ())), preferred_element_type=F32)


def tn(a, b):
    return lax.dot_general(a, b, (((0,), (0,)), ((), ())), preferred_element_type=F32)


def tt(a, b):
    return lax.dot_general(a, b, (((0,), (1,)), ((), ())), preferred_element_type=F32)


def norm_parts(x):
    mean = jnp.mean(x, axis=-1, keepdims=True)
    centered = x - mean
    spread = jnp.mean(centered * centered, axis=-1, keepdims=True)
    scale = lax.rsqrt(spread + NORM_EPSILON)
    return centered * scale, scale


def norm(x, gain):
    return norm_parts(x)[0] * gain


def norm_back(x, gain, grad):
    hat, scale = norm_parts(x)
    inner = grad * gain
    dx = scale * (
        inner
        - jnp.mean(inner, axis=-1, keepdims=True)
        - hat * jnp.mean(inner * hat, axis=-1, keepdims=True)
    )
    return dx, jnp.sum(grad * hat, axis=0, keepdims=True)


GELU_A = 0.7978845608028654
GELU_B = 0.044715


def gelu(x):
    return 0.5 * x * (1.0 + jnp.tanh(x * (GELU_A + (GELU_A * GELU_B) * (x * x))))


def gelu_both(x):
    sq = x * x
    th = jnp.tanh(x * (GELU_A + (GELU_A * GELU_B) * sq))
    half = 0.5 * (1.0 + th)
    slope = half + (0.5 * x) * (1.0 - th * th) * (GELU_A + (3.0 * GELU_A * GELU_B) * sq)
    return x * half, slope


def xor(value, bits):
    b = 1
    while b <= bits:
        if bits & b:
            value = value + b * (1 - 2 * lax.rem(lax.div(value, b), 2))
        b *= 2
    return value


def peer(to):
    return (xor(lax.axis_index("dp"), to[0]), xor(lax.axis_index("expert"), to[1]))


def send(src, dst, send_sem, recv_sem, to):
    return pltpu.make_async_remote_copy(
        src_ref=src, dst_ref=dst, send_sem=send_sem, recv_sem=recv_sem, device_id=peer(to), device_id_type=MESH
    )


def expert_peers(ids):
    return [(0, r) for r in ids[1:]]


class Gather:
    def __init__(self, ids, near, send_sems, recv_sems):
        self.pos = {r: i for i, r in enumerate(ids)}
        self.far = [r for r in ids if r % 2 == 0 and r > 0]
        self.near, self.sems = near, (send_sems, recv_sems)

    def copy(self, r, src, to):
        at = self.pos[r]
        return send(src, self.near.at[at], self.sems[0].at[at], self.sems[1].at[at], (0, to))

    def first(self, r):
        return self.copy(r, self.near.at[0], r)

    def second(self, r):
        return self.copy(r ^ 1, self.near.at[self.pos[r]], 1)

    def start(self):
        for r in self.far:
            self.first(r).start()
        self.first(1).start()

    def forward(self):
        for r in self.far:
            self.first(r).wait_recv()
            self.second(r).start()

    def finish(self):
        for r in self.far:
            self.second(r).wait_recv()
        self.first(1).wait_recv()
        for r in self.far:
            self.first(r).wait_send()
            self.second(r).wait_send()
        self.first(1).wait_send()


class Scatter:
    def __init__(self, ids, parts, got, send_sems, recv_sems):
        self.pos = {r: i for i, r in enumerate(ids)}
        self.odd = [r for r in ids if r % 2]
        self.even = [r for r in ids if r % 2 == 0]
        self.parts, self.got, self.sems = parts, got, (send_sems, recv_sems)

    def copy(self, r, to):
        at = self.pos[r]
        return send(
            self.parts.at[at], self.got.at[self.pos[r ^ 1]], self.sems[0].at[at], self.sems[1].at[at], (0, to)
        )

    def start(self):
        for r in self.odd:
            self.copy(r, 1).start()

    def middle(self):
        for r in self.odd:
            self.copy(r, 1).wait_recv()
        for r in self.even[1:]:
            at = self.pos[r]
            self.parts[at] = (self.parts[at].astype(F32) + self.got[at].astype(F32)).astype(BF16)
            self.copy(r, r).start()

    def finish(self):
        total = self.parts[0].astype(F32) + self.got[0].astype(F32)
        for r in self.even[1:]:
            self.copy(r, r).wait_recv()
            total = total + self.got[self.pos[r ^ 1]].astype(F32)
        for r in self.odd:
            self.copy(r, 1).wait_send()
        for r in self.even[1:]:
            self.copy(r, r).wait_send()
        return total


class Job:
    def __init__(self, own, far, z=(), x=(), c=()):
        self.own, self.far, self.z, self.x, self.c = own, far, list(z), list(x), list(c)


class Plan:
    def __init__(self, n_dp, n_expert):
        self.n_dp, self.n_expert = n_dp, n_expert
        self.ny = 2 if n_dp <= 8 else 4
        self.nz = n_dp // self.ny
        ids, bit = [0], n_expert // 2
        while bit >= 1:
            ids = ids + [i ^ bit for i in ids]
            bit //= 2
        self.ids = ids
        self.zr = list(range(1, self.nz))


class Background:
    def __init__(self, plan, jobs, owns, fars, send_sems, recv_sems, peers):
        self.plan, self.jobs, self.peers = plan, jobs, peers
        self.owns, self.fars, self.sems = owns, fars, (send_sems, recv_sems)

    def copies(self):
        plan = self.plan
        pos = {r: i for i, r in enumerate(plan.ids)}
        across = [r for r in plan.ids if r % 2 == 0 and r > 0]
        n = 0
        for job, own, far in zip(self.jobs, self.owns, self.fars):
            moves = []
            for zr in job.z:
                moves.append((own, far.at[zr - 1, 0], (zr * plan.ny, 0)))
            for zr in job.x:
                for r in across:
                    moves.append((far.at[zr - 1, 0], far.at[zr - 1, pos[r]], (0, r)))
            for zr in job.c:
                for r in [0] + across:
                    moves.append((far.at[zr - 1, pos[r]], far.at[zr - 1, pos[r ^ 1]], (0, 1)))
            for src, dst, to in moves:
                yield send(src, dst, self.sems[0].at[n], self.sems[1].at[n], to)
                n += 1

    def greet(self):
        barrier = pltpu.get_barrier_semaphore()
        for p in self.peers:
            pl.semaphore_signal(barrier, inc=1, device_id=peer(p), device_id_type=MESH)
        pl.semaphore_wait(barrier, len(self.peers))

    def start(self):
        for copy in self.copies():
            copy.start()

    def finish(self):
        for copy in self.copies():
            copy.wait()


def vmem(shape):
    return pl.BlockSpec(shape, lambda *_: (0,) * len(shape))


ANYWHERE = pl.BlockSpec(memory_space=pl.ANY)


def fused(
    plan, body, ins, outs, name, cid=None, peers=(), jobs=(), grid=None, in_specs=None, out_specs=None, scratch=(), us=10
):
    whole = (lambda shape: pl.BlockSpec(memory_space=pltpu.VMEM)) if grid is None else vmem
    in_specs = [None] * len(ins) if in_specs is None else in_specs
    out_specs = [None] * len(outs) if out_specs is None else out_specs
    in_specs = [whole(a.shape) if s is None else s for a, s in zip(ins, in_specs)]
    out_specs = [whole(o[0]) if s is None else s for o, s in zip(outs, out_specs)]
    ins, outs, scratch = list(ins), list(outs), list(scratch)
    n_in, n_out, n_scratch = len(ins), len(outs), len(scratch)
    aliases, places, count, peers = {}, [], 0, list(peers)
    across = [r for r in plan.ids if r % 2 == 0 and r > 0]
    for k, job in enumerate(jobs):
        place = None
        if job.z:
            place = len(ins)
            ins.append(job.own)
            in_specs.append(ANYWHERE)
        if job.far is not None:
            aliases[len(ins)] = n_out + k
            ins.append(job.far)
            in_specs.append(ANYWHERE)
            outs.append((job.far.shape, job.far.dtype))
        else:
            outs.append(((plan.nz - 1, plan.n_expert) + job.own.shape, job.own.dtype))
        out_specs.append(ANYWHERE)
        places.append(place)
        count += len(job.z) + len(job.x) * len(across) + len(job.c) * (1 + len(across))
        wanted = [(zr * plan.ny, 0) for zr in job.z]
        wanted += [(0, r) for r in across] if job.x else []
        wanted += [(0, 1)] if job.c else []
        peers += [p for p in wanted if p not in peers]
    if jobs:
        scratch += [DMA((count,)), DMA((count,))]

    def run(*refs):
        i, o, s = refs[: len(ins)], refs[len(ins) : len(ins) + len(outs)], refs[len(ins) + len(outs) :]
        if cid is None:
            return body(*i, *o, *s)
        sems = s[n_scratch:] if jobs else (None, None)
        bg = Background(plan, jobs, [None if p is None else i[p] for p in places], o[n_out:], *sems, peers)
        body(bg, *i[:n_in], *o[:n_out], *s[:n_scratch])

    moved = sum(a.size * a.dtype.itemsize for a in ins[:n_in])
    extra = {} if grid is None else {"grid": grid}
    got = pl.pallas_call(
        run,
        out_shape=[jax.ShapeDtypeStruct(s, d) for s, d in outs],
        in_specs=in_specs,
        out_specs=out_specs,
        scratch_shapes=scratch,
        input_output_aliases=aliases,
        name=name,
        compiler_params=pltpu.CompilerParams(
            vmem_limit_bytes=VMEM_LIMIT, collective_id=cid, has_side_effects=cid is not None
        ),
        cost_estimate=pl.CostEstimate(flops=int(us * 1.15e9), bytes_accessed=moved, transcendentals=0),
        **extra,
    )(*ins)
    return got[:n_out], got[n_out:]


def head_rows(values, h):
    rows = values[h * HEAD_DIM : (h + 1) * HEAD_DIM]
    zero = jnp.zeros_like(rows)
    return jnp.concatenate([rows, zero] if h % 2 == 0 else [zero, rows], axis=0)


def head_lanes(values, h):
    pair = values[:, (h // 2) * 128 : (h // 2 + 1) * 128]
    lane = lax.broadcasted_iota(jnp.int32, pair.shape, 1)
    keep = lane < HEAD_DIM if h % 2 == 0 else lane >= HEAD_DIM
    return jnp.where(keep, pair, jnp.zeros_like(pair))


def causal_allow(ids, rows):
    me = lax.axis_index("expert")
    parts = []
    for r in ids:
        key = xor(me, r) * rows + lax.broadcasted_iota(jnp.int32, (rows, rows), 0)
        query = me * rows + lax.broadcasted_iota(jnp.int32, (rows, rows), 1)
        parts.append((key <= query).astype(F32))
    return jnp.concatenate(parts, axis=0) > 0.5


def attend_forward(q_t, k, v_t, allow, o_t, lse, between=None):
    heads = q_t.shape[0] // HEAD_DIM
    for h in range(heads):
        if between is not None and h == heads // 2:
            between()
        pair = slice((h // 2) * 128, (h // 2 + 1) * 128)
        scores = nn(k[:, pair], head_rows(q_t, h))
        if allow is not None:
            scores = jnp.where(allow, scores, MASKED)
        top = jnp.max(scores, axis=0, keepdims=True)
        lifted = jnp.exp(scores - top)
        total = jnp.sum(lifted, axis=0, keepdims=True)
        rows = slice(h * HEAD_DIM, (h + 1) * HEAD_DIM)
        blended = nn(v_t[rows, :], lifted.astype(BF16)) * (1.0 / total)
        o_t[rows, :] = blended.astype(BF16)
        lse[h : h + 1, :] = top + jnp.log(total)


def attend_backward(q, k, v, k_t, do, lse, allow, dk, dv, dq_t, between=()):
    heads = q.shape[1] // HEAD_DIM
    q_t = q.astype(F32).T.astype(BF16)
    do_t = do.astype(F32).T.astype(BF16)
    for h2 in range(heads // 2):
        for at, act in between:
            if at == h2:
                act()
        pair = slice(h2 * 128, (h2 + 1) * 128)
        dk_pair = None
        for h in (2 * h2, 2 * h2 + 1):
            rows = slice(h * HEAD_DIM, (h + 1) * HEAD_DIM)
            scores = nn(k[:, pair], head_rows(q_t, h))
            weights = jnp.exp(scores - lse[h : h + 1, :])
            if allow is not None:
                weights = jnp.where(allow, weights, 0.0)
            weights_grad = nn(v[:, pair], head_rows(do_t, h))
            centre = jnp.sum(weights * weights_grad, axis=0, keepdims=True)
            scores_grad = (weights * (weights_grad - centre)).astype(BF16)
            dv_part = nn(weights.astype(BF16), head_lanes(do, h))
            dk_part = nn(scores_grad, head_lanes(q, h))
            dq_t[rows, :] = (nn(k_t[rows, :], scores_grad) * HEAD_DIM ** (-0.5)).astype(BF16)
            if dk_pair is None:
                dk_pair, dv_pair = dk_part, dv_part
            else:
                dk_pair, dv_pair = dk_pair + dk_part, dv_pair + dv_part
        dk[:, pair] = dk_pair.astype(BF16)
        dv[:, pair] = dv_pair.astype(BF16)


def project_rows(hm, win, k, k_t, v, v_t):
    feature = hm.shape[1]
    w_k, w_v = win[:, feature : 2 * feature], win[:, 2 * feature :]
    k[...] = nn(hm, w_k).astype(BF16)
    v[...] = nn(hm, w_v).astype(BF16)
    k_t[...] = tt(w_k, hm).astype(BF16)
    v_t[...] = tt(w_v, hm).astype(BF16)


def project_query(rows, win):
    return nn(rows, win[:, : rows.shape[1]]).astype(BF16).astype(F32) * HEAD_DIM ** (-0.5)


def attention_shapes(plan, rows, feature):
    length = plan.n_expert * rows
    return [
        ((length, feature), BF16),
        ((feature, length), BF16),
        ((length, feature), BF16),
        ((rows, feature), BF16),
        ((feature, rows), BF16),
        ((feature // HEAD_DIM, rows), F32),
    ]


def gather_rows(ids, col, returned):
    me = lax.axis_index("expert")
    total = None
    for r, rows in zip(ids, returned):
        slots = rows.shape[0] * rows.shape[1]
        local = col - xor(me, r) * slots
        hot = (local == lax.broadcasted_iota(jnp.int32, (col.shape[0], slots), 1)).astype(BF16)
        part = nn(hot, rows.reshape(slots, rows.shape[-1]))
        total = part if total is None else total + part
    return total


def fill_buffers(cap, col_of, token_of, sources, dest):
    experts = dest.shape[0]
    slots = experts * cap
    me = lax.axis_index("expert")
    for s in range(sources):
        for p in range(2):
            local = col_of(s, p) - me * slots
            hot = (local == lax.broadcasted_iota(jnp.int32, (slots, local.shape[1]), 0)).astype(BF16)
            rows = nn(hot, token_of(s, p)).astype(BF16)
            at = (2 * s + p) * cap
            for j in range(experts):
                dest[j, at : at + cap, :] = rows[j * cap : (j + 1) * cap]


def column(ref, s, layer, p):
    return ref[s, pl.ds(2 * layer + p, 1), :]


class Return:
    def __init__(self, ids, stage, ret, send_sems, recv_sems):
        self.ids, self.stage, self.ret, self.sems = ids, stage, ret, (send_sems, recv_sems)

    def copy(self, s, n):
        return send(
            self.stage.at[s, n], self.ret.at[s, n], self.sems[0].at[s, n], self.sems[1].at[s, n], (0, self.ids[s])
        )

    def put(self, j, rows, cap):
        for s in range(len(self.ids)):
            for p in range(2):
                at = (2 * s + p) * cap
                (self.ret if s == 0 else self.stage)[s, j, p] = rows[at : at + cap]

    def start(self, j):
        for s in range(1, len(self.ids)):
            self.copy(s, j).start()

    def finish(self, experts):
        for n in range(experts):
            for s in range(1, len(self.ids)):
                self.copy(s, n).wait()

    def rows(self, p):
        return [self.ret[s, :, p] for s in range(len(self.ids))]


def load(src, dst, sem):
    return pltpu.make_async_copy(src, dst, sem)


def self_forward(plan, source, target, cols, out_grad, gains, inward, outward, jobs):
    ids, count = plan.ids, plan.n_expert
    _, rows, feature = source.shape
    length = count * rows

    def body(bg, *refs):
        src, tgt, col, og, g, win_any, wout_any = refs[:7]
        enc, dec = refs[7:16], refs[16:25]
        u_near, og_near, col_near = refs[25:28]
        near_s, near_t, v_t, win, wout, lsem, *sems = refs[28:]
        weights = [load(win_any.at[n], win.at[n], lsem.at[n]) for n in range(2)]
        weights += [load(wout_any.at[n], wout.at[n], lsem.at[2 + n]) for n in range(2)]
        for w in weights:
            w.start()
        g_s, g_t, g_u, g_og, g_col = [
            Gather(ids, ref, sems[2 * n], sems[2 * n + 1])
            for n, ref in enumerate((near_s, near_t, u_near, og_near, col_near))
        ]
        near_s[0] = src[0]
        near_t[0] = tgt[0]
        col_near[0] = col[...]
        og_near[0] = og[...]
        bg.greet()
        g_s.start()
        g_t.start()
        g_col.start()
        bg.start()

        def attend(near, outs, n, gain, gain_next, allow, first, between):
            after, nxt, hm, k, k_t, v, q, o_t, lse = outs
            hm[0:rows, :] = norm(near[0].astype(F32), g[gain : gain + 1]).astype(BF16)
            if n == 0:
                for w in weights:
                    w.wait()
            q_scaled = project_query(hm[0:rows, :], win[n])
            q[...] = q_scaled.astype(BF16)
            first()
            for b in range(1, count):
                hm[b * rows : (b + 1) * rows, :] = norm(near[b].astype(F32), g[gain : gain + 1]).astype(BF16)
            project_rows(hm[...], win[n], k, k_t, v, v_t)
            attend_forward(q_scaled.T.astype(BF16), k, v_t, allow, o_t, lse, between)
            merged = o_t[...].astype(F32).T.astype(BF16)
            after[...] = near[0].astype(F32) + nn(merged, wout[n])
            nxt[...] = norm(after[...], g[gain_next : gain_next + 1]).astype(BF16)

        def first_enc():
            g_s.forward()
            g_s.finish()
            g_og.start()

        def mid_enc():
            g_t.forward()
            g_col.forward()

        attend(near_s, enc, 0, 0, 1, None, first_enc, mid_enc)
        u_near[0] = enc[1][...]
        g_u.start()

        def mid_dec():
            g_u.forward()
            g_og.forward()

        attend(near_t, dec, 1, 3, 4, causal_allow(ids, rows), g_t.finish, mid_dec)
        g_u.finish()
        g_og.finish()
        g_col.finish()
        bg.finish()

    shapes = [((rows, feature), F32), ((rows, feature), BF16), ((length, feature), BF16)]
    shapes += attention_shapes(plan, rows, feature)
    outs, fars = fused(
        plan,
        body,
        [source, target, cols, out_grad, gains, inward, outward],
        shapes
        + shapes
        + [
            ((count, rows, feature), BF16),
            ((count, 2, rows, feature), BF16),
            ((count,) + cols.shape, jnp.int32),
        ],
        "self_forward",
        cid=1,
        peers=expert_peers(ids),
        jobs=jobs,
        in_specs=[None] * 5 + [ANYWHERE] * 2,
        scratch=[
            pltpu.VMEM((count, rows, feature), BF16),
            pltpu.VMEM((count, rows, feature), BF16),
            pltpu.VMEM((feature, length), BF16),
            pltpu.VMEM((2, feature, 3 * feature), BF16),
            pltpu.VMEM((2, feature, feature), BF16),
            DMA((4,)),
        ]
        + [DMA((count,))] * 10,
        us=35,
    )
    return outs[:9], outs[9:18], outs[18:], fars


def return_scratch(plan, experts, cap, feature):
    shape = (plan.n_expert, experts, 2, cap, feature)
    return [pltpu.VMEM(shape, BF16), pltpu.VMEM(shape, BF16), DMA(shape[:2]), DMA(shape[:2])]


def expert_forward(plan, near, col_near, own_col, residual, gains, weight_up, weight_down, jobs):
    ids, count = plan.ids, plan.n_expert
    experts, hidden, feature = weight_up.shape
    rows = near.shape[1]
    cap = 2 * rows // EXPERTS
    length = count * 2 * cap

    def body(bg, u, col, mine, res, g, up, down, out, nxt, buf, *scratch):
        j = pl.program_id(0)
        back = Return(ids, *scratch)

        @pl.when(j == 0)
        def _():
            bg.greet()
            bg.start()
            fill_buffers(cap, lambda s, p: col[s, p : p + 1, :], lambda s, p: u[s], count, buf)

        act = gelu(nt(buf[j], up[0])).astype(BF16)
        back.put(j, nn(act, down[0]).astype(BF16), cap)
        back.start(j)

        @pl.when(j == experts - 1)
        def _():
            back.finish(experts)
            for p in range(2):
                after = res[...] + gather_rows(ids, mine[p], back.rows(p))
                out[p] = after
                nxt[p] = norm(after, g[2:3]).astype(BF16)
            bg.finish()

    weight = pl.BlockSpec((1, hidden, feature), lambda j: (j, 0, 0))
    return fused(
        plan,
        body,
        [near, col_near, own_col, residual, gains, weight_up, weight_down],
        [((2, rows, feature), F32), ((2, rows, feature), BF16)],
        "expert_forward",
        cid=2,
        peers=expert_peers(ids),
        jobs=jobs,
        grid=(experts,),
        in_specs=[None] * 5 + [weight, weight],
        scratch=[pltpu.VMEM((experts, length, feature), BF16)] + return_scratch(plan, experts, cap, feature),
        us=22,
    )


def cross_forward(plan, hc, mid, memory, gains, inward, outward, jobs):
    ids, count = plan.ids, plan.n_expert
    rows, feature = hc.shape
    length = count * rows

    def body(bg, h, res, mem, g, win_any, wout_any, t2, w, w_near, hm, k, k_t, v, q, o_t, lse, v_t, win, wout, lsem, *sems):
        weights = [load(win_any.at[2], win, lsem.at[0]), load(wout_any.at[2], wout, lsem.at[1])]
        for x in weights:
            x.start()
        gather_m = [Gather(ids, hm.at[p], sems[p].at[0], sems[p].at[1]) for p in range(2)]
        gather_w = [Gather(ids, w_near.at[p], sems[2 + p].at[0], sems[2 + p].at[1]) for p in range(2)]
        for p in range(2):
            hm[p, 0] = mem[p]
        bg.greet()
        gather_m[0].start()
        gather_m[1].start()
        for x in weights:
            x.wait()
        q_scaled = project_query(h[...], win[...])
        q[...] = q_scaled.astype(BF16)
        q_t = q_scaled.T.astype(BF16)
        gather_m[0].forward()
        gather_m[0].finish()
        bg.start()
        for p in range(2):
            project_rows(hm[p].reshape(length, feature), win[...], k.at[p], k_t.at[p], v.at[p], v_t)
            between = gather_m[1].forward if p == 0 else gather_w[0].forward
            attend_forward(q_t, k.at[p], v_t, None, o_t.at[p], lse.at[p], between)
            after = res[...] + nn(o_t[p].astype(F32).T.astype(BF16), wout[...])
            t2[p] = after
            nxt = norm(after, g[5:6]).astype(BF16)
            w[p] = nxt
            w_near[p, 0] = nxt
            gather_w[p].start()
            if p == 0:
                gather_m[1].finish()
        gather_w[1].forward()
        gather_w[0].finish()
        gather_w[1].finish()
        bg.finish()

    saved = attention_shapes(plan, rows, feature)
    saved = [((2,) + s, d) if n != 3 else (s, d) for n, (s, d) in enumerate(saved)]
    return fused(
        plan,
        body,
        [hc, mid, memory, gains, inward, outward],
        [
            ((2, rows, feature), F32),
            ((2, rows, feature), BF16),
            ((2, count, rows, feature), BF16),
            ((2, count, rows, feature), BF16),
        ]
        + saved,
        "cross_forward",
        cid=3,
        peers=expert_peers(ids),
        jobs=jobs,
        in_specs=[None] * 4 + [ANYWHERE] * 2,
        scratch=[
            pltpu.VMEM((feature, length), BF16),
            pltpu.VMEM((feature, 3 * feature), BF16),
            pltpu.VMEM((feature, feature), BF16),
            DMA((2,)),
        ]
        + [DMA((2, count))] * 4,
        us=35,
    )


def decoder_experts(plan, w_near, og_near, col_near, own_col, crossed, out_grad, gains, weight_up, weight_down, jobs):
    ids, count = plan.ids, plan.n_expert
    experts, hidden, feature = weight_up.shape
    rows = crossed.shape[1]
    cap = 2 * rows // EXPERTS
    length = count * 2 * cap

    def body(bg, w, og, col, mine, t2, og_own, g, up, down, upstream, dg, result, buf, gbuf, *scratch):
        j = pl.program_id(0)
        back = Return(ids, *scratch)

        @pl.when(j == 0)
        def _():
            bg.greet()
            bg.start()
            fill_buffers(cap, lambda s, p: col[s, 2 + p : 3 + p, :], lambda s, p: w[p, s], count, buf)
            fill_buffers(cap, lambda s, p: col[s, 2 + p : 3 + p, :], lambda s, p: og[s, p], count, gbuf)

        value, slope = gelu_both(nt(buf[j], up[0]))
        hidden_grad = (slope * nt(gbuf[j], down[0])).astype(BF16)
        back.put(j, nn(hidden_grad, up[0]).astype(BF16), cap)
        back.start(j)
        res = nn(value.astype(BF16), down[0]).astype(BF16)
        for s in range(count):
            for p in range(2):
                at = (2 * s + p) * cap
                result[s, 0, p] = res[at : at + cap]

        @pl.when(j == experts - 1)
        def _():
            back.finish(experts)
            total = None
            for p in range(2):
                dw = gather_rows(ids, mine[p], back.rows(p))
                dx, gain = norm_back(t2[p], g[5:6], dw)
                upstream[p] = og_own[p] + dx
                total = gain if total is None else total + gain
            dg[...] = total
            bg.finish()

    weight = pl.BlockSpec((1, hidden, feature), lambda j: (j, 0, 0))
    return fused(
        plan,
        body,
        [w_near, og_near, col_near, own_col, crossed, out_grad, gains, weight_up, weight_down],
        [((2, rows, feature), F32), ((1, feature), F32), ((count, experts, 2, cap, feature), BF16)],
        "decoder_experts",
        cid=4,
        peers=expert_peers(ids),
        jobs=jobs,
        grid=(experts,),
        in_specs=[None] * 7 + [weight, weight],
        out_specs=[None, None, pl.BlockSpec((count, 1, 2, cap, feature), lambda j: (0, j, 0, 0, 0))],
        scratch=[pltpu.VMEM((experts, length, feature), BF16)] * 2 + return_scratch(plan, experts, cap, feature),
        us=30,
    )


def weight_grads(hq, hm, dq, dk, dv, o_t, d_branch):
    return [tn(hq, dq), tn(hm, dk), tn(hm, dv), nn(o_t, d_branch)]


def cross_backward(
    plan, upstream, result, own_col, crossed, final, hc, mid, gains, saved, inward, outward, jobs
):
    ids, count = plan.ids, plan.n_expert
    rows, feature = mid.shape
    length = count * rows
    experts, _, cap = result.shape[1:4]

    def body(bg, *refs):
        up, res_any, mine, t2, e2, h, t1, g = refs[:8]
        hm, k, k_t, v, q, o_t, lse, win_any, wout_any = refs[8:17]
        y, fg, fg_low, fg_near, dt1, dw, dg2, dg4 = refs[17:25]
        ret, dk, dv, dq_t, dw_acc, parts, got, win, wout, lsem, rs, rr, *sems = refs[25:]
        weights = [load(win_any.at[2], win, lsem.at[0]), load(wout_any.at[2], wout, lsem.at[1])]
        own = load(res_any.at[0], ret.at[0], lsem.at[2])
        for x in weights + [own]:
            x.start()
        scatter = [Scatter(ids, parts.at[p], got.at[p], sems[p].at[0], sems[p].at[1]) for p in range(2)]
        gather = [Gather(ids, fg_near.at[p], sems[2 + p].at[0], sems[2 + p].at[1]) for p in range(2)]

        def bring(s):
            return send(res_any.at[s], ret.at[s], rs.at[s], rr.at[s], (0, ids[s]))

        def memory_back(p):
            dx, gain = norm_back(e2[p], g[2:3], scatter[p].finish())
            fg[p] = dx
            fg_low[p] = dx.astype(BF16)
            fg_near[p, 0] = dx.astype(BF16)
            gather[p].start()
            if p == 0:
                dg2[...] = gain
            else:
                dg2[...] = dg2[...] + gain

        bg.greet()
        bg.start()
        for s in range(1, count):
            bring(s).start()
        for x in weights:
            x.wait()
        dh = None
        for p in range(2):
            d_branch = up[p].astype(BF16)
            do = nt(d_branch, wout[...]).astype(BF16)
            between = () if p == 0 else ((1, scatter[0].middle), (3, lambda: memory_back(0)))
            attend_backward(
                q[...], k.at[p], v.at[p], k_t.at[p], do, lse.at[p], None, dk, dv, dq_t, between
            )
            for b in range(count):
                span = slice(b * rows, (b + 1) * rows)
                part = nt(dk[span, :], win[:, feature : 2 * feature]) + nt(dv[span, :], win[:, 2 * feature :])
                parts[p, b] = part.astype(BF16)
            scatter[p].start()
            dq = dq_t[...].astype(F32).T.astype(BF16)
            back = nt(dq, win[:, :feature])
            dh = back if dh is None else dh + back
            if p == 1:
                scatter[1].middle()
                gather[0].forward()
            grads = weight_grads(
                h[...], hm[p].reshape(length, feature), dq, dk[...], dv[...], o_t[p], d_branch
            )
            for n, value in enumerate(grads):
                at = slice(n * feature, (n + 1) * feature)
                if p == 0:
                    dw_acc[:, at] = value
                else:
                    dw[:, at] = (dw_acc[:, at] + value).astype(BF16)
        memory_back(1)
        dx, gain = norm_back(t1[...], g[4:5], dh)
        dt1[...] = up[0] + up[1] + dx
        dg4[...] = gain
        own.wait()
        for s in range(1, count):
            bring(s).wait()
        gather[1].forward()
        for p in range(2):
            mixed = gather_rows(ids, mine[p], [ret[s, :, p] for s in range(count)])
            y[p] = (t2[p] + mixed).astype(BF16)
        gather[0].finish()
        gather[1].finish()
        bg.finish()

    block = (rows, feature)
    return fused(
        plan,
        body,
        [upstream, result, own_col, crossed, final, hc, mid, gains, *saved, inward, outward],
        [
            ((2,) + block, BF16),
            ((2,) + block, F32),
            ((2,) + block, BF16),
            ((2, count) + block, BF16),
            (block, F32),
            ((feature, 4 * feature), BF16),
            ((1, feature), F32),
            ((1, feature), F32),
        ],
        "cross_backward",
        cid=5,
        peers=expert_peers(ids),
        jobs=jobs,
        in_specs=[None, ANYWHERE] + [None] * 13 + [ANYWHERE] * 2,
        scratch=[
            pltpu.VMEM((count, experts, 2, cap, feature), BF16),
            pltpu.VMEM((length, feature), BF16),
            pltpu.VMEM((length, feature), BF16),
            pltpu.VMEM((feature, rows), BF16),
            pltpu.VMEM((feature, 4 * feature), F32),
            pltpu.VMEM((2, count) + block, BF16),
            pltpu.VMEM((2, count) + block, BF16),
            pltpu.VMEM((feature, 3 * feature), BF16),
            pltpu.VMEM((feature, feature), BF16),
            DMA((3,)),
            DMA((count,)),
            DMA((count,)),
        ]
        + [DMA((2, count))] * 4,
        us=45,
    )


def encoder_experts(plan, u_near, fg_near, col_near, own_col, attended, final_grad, gains, weight_up, weight_down, jobs):
    ids, count = plan.ids, plan.n_expert
    experts, hidden, feature = weight_up.shape
    rows = attended.shape[0]
    cap = 2 * rows // EXPERTS
    length = count * 2 * cap

    def body(bg, u, fgn, col, mine, e1, fg, g, up, down, de1, dg, buf, gbuf, *scratch):
        j = pl.program_id(0)
        back = Return(ids, *scratch)

        @pl.when(j == 0)
        def _():
            bg.greet()
            bg.start()
            fill_buffers(cap, lambda s, p: col[s, p : p + 1, :], lambda s, p: u[s], count, buf)
            fill_buffers(cap, lambda s, p: col[s, p : p + 1, :], lambda s, p: fgn[p, s], count, gbuf)

        _, slope = gelu_both(nt(buf[j], up[0]))
        hidden_grad = (slope * nt(gbuf[j], down[0])).astype(BF16)
        back.put(j, nn(hidden_grad, up[0]).astype(BF16), cap)
        back.start(j)

        @pl.when(j == experts - 1)
        def _():
            back.finish(experts)
            du = gather_rows(ids, mine[0], back.rows(0)) + gather_rows(ids, mine[1], back.rows(1))
            dx, gain = norm_back(e1[...], g[1:2], du)
            de1[...] = fg[0] + fg[1] + dx
            dg[...] = gain
            bg.finish()

    weight = pl.BlockSpec((1, hidden, feature), lambda j: (j, 0, 0))
    return fused(
        plan,
        body,
        [u_near, fg_near, col_near, own_col, attended, final_grad, gains, weight_up, weight_down],
        [((rows, feature), F32), ((1, feature), F32)],
        "encoder_experts",
        cid=6,
        peers=expert_peers(ids),
        jobs=jobs,
        grid=(experts,),
        in_specs=[None] * 7 + [weight, weight],
        scratch=[pltpu.VMEM((experts, length, feature), BF16)] * 2 + return_scratch(plan, experts, cap, feature),
        us=30,
    )


def self_backward(plan, enc_up, dec_up, source, target, gains, enc_saved, dec_saved, inward, outward, jobs):
    ids, count = plan.ids, plan.n_expert
    _, rows, feature = source.shape
    length = count * rows

    def body(bg, *refs):
        ups, srcs, g = refs[:2], refs[2:4], refs[4]
        saved = (refs[5:12], refs[12:19])
        win_any, wout_any = refs[19:21]
        grads, dws, dgs = refs[21:23], refs[23:25], refs[25:27]
        dk, dv, dq_t, parts, got, win, wout, lsem, *sems = refs[27:]
        weights = [load(win_any.at[n], win.at[n], lsem.at[n]) for n in range(2)]
        weights += [load(wout_any.at[n], wout.at[n], lsem.at[2 + n]) for n in range(2)]
        for x in weights:
            x.start()
        scatter = [Scatter(ids, parts.at[n], got.at[n], sems[n].at[0], sems[n].at[1]) for n in range(2)]

        def finish(n):
            gain = 3 * n
            dx, dgain = norm_back(srcs[n][0].astype(F32), g[gain : gain + 1], scatter[n].finish())
            grads[n][...] = ups[n][...] + dx
            dgs[n][...] = dgain

        bg.greet()
        bg.start()
        for x in weights:
            x.wait()
        for n in range(2):
            hm, k, k_t, v, q, o_t, lse = saved[n]
            d_branch = ups[n][...].astype(BF16)
            do = nt(d_branch, wout[n]).astype(BF16)
            allow = causal_allow(ids, rows) if n == 1 else None
            between = () if n == 0 else ((1, scatter[0].middle), (3, lambda: finish(0)))
            attend_backward(q[...], k, v, k_t, do, lse, allow, dk, dv, dq_t, between)
            dq = dq_t[...].astype(F32).T.astype(BF16)
            for b in range(count):
                span = slice(b * rows, (b + 1) * rows)
                part = nt(dk[span, :], win[n, :, feature : 2 * feature])
                part = part + nt(dv[span, :], win[n, :, 2 * feature :])
                if b == 0:
                    part = part + nt(dq, win[n, :, :feature])
                parts[n, b] = part.astype(BF16)
            scatter[n].start()
            if n == 1:
                scatter[1].middle()
            for i, value in enumerate(
                weight_grads(hm[0:rows, :], hm[...], dq, dk[...], dv[...], o_t[...], d_branch)
            ):
                dws[n][:, i * feature : (i + 1) * feature] = value.astype(BF16)
        finish(1)
        bg.finish()

    block = (rows, feature)
    return fused(
        plan,
        body,
        [enc_up, dec_up, source, target, gains, *enc_saved, *dec_saved, inward, outward],
        [(block, F32)] * 2 + [((feature, 4 * feature), BF16)] * 2 + [((1, feature), F32)] * 2,
        "self_backward",
        cid=7,
        peers=expert_peers(ids),
        jobs=jobs,
        in_specs=[None] * 19 + [ANYWHERE] * 2,
        scratch=[
            pltpu.VMEM((length, feature), BF16),
            pltpu.VMEM((length, feature), BF16),
            pltpu.VMEM((feature, rows), BF16),
            pltpu.VMEM((2, count) + block, BF16),
            pltpu.VMEM((2, count) + block, BF16),
            pltpu.VMEM((2, feature, 3 * feature), BF16),
            pltpu.VMEM((2, feature, feature), BF16),
            DMA((4,)),
        ]
        + [DMA((2, count))] * 2,
        us=40,
    )


def transfers(plan, name, cid, jobs):
    def body(bg):
        bg.greet()
        bg.start()
        bg.finish()

    return fused(plan, body, [], [], name, cid=cid, jobs=jobs, us=30)[1]


def expert_weights(plan, place, layer, tokens, grads, cols, weight_up, weight_down):
    count, ny, nz = plan.n_expert, plan.ny, plan.nz
    experts, hidden, feature = weight_up.shape
    rows = tokens[0].shape[-2]
    cap = 2 * rows // EXPERTS
    sources = count * nz
    length = sources * 2 * cap
    span = hidden // (ny * nz)
    at = [(None, s) if s < count else (s // count - 1, s % count) for s in range(sources)]

    def body(place_ref, tn_, tf, gn, gf, cn, cf, up, down, up_out, down_out, buf, gbuf):
        @pl.when((pl.program_id(0) == 0) & (pl.program_id(1) == 0))
        def _():
            def col_of(s, p):
                z, i = at[s]
                row = slice(2 * layer + p, 2 * layer + p + 1)
                return cn[i, row, :] if z is None else cf[z, i, row, :]

            def token_of(s, p):
                z, i = at[s]
                if layer == 0:
                    return tn_[i] if z is None else tf[z, i]
                return tn_[p, i] if z is None else tf[z, i, p]

            def grad_of(s, p):
                z, i = at[s]
                if z is None:
                    return gn[p, i] if layer == 0 else gn[i, p]
                return gf[z, i, p]

            fill_buffers(cap, col_of, token_of, sources, buf)
            fill_buffers(cap, col_of, grad_of, sources, gbuf)

        j = pl.program_id(0)
        x, g = buf[j], gbuf[j]
        value, slope = gelu_both(nt(up[0], x))
        hidden_grad = (slope * nt(down[0], g)).astype(BF16)
        up_out[0, 0] = nn(hidden_grad, x).astype(BF16)
        down_out[0, 0] = nn(value.astype(BF16), g).astype(BF16)

    ins = [*tokens, *grads, *cols, weight_up, weight_down]
    weight = pl.BlockSpec((1, span, feature), lambda j, r, place_ref: (j, place_ref[0] * ny + (place_ref[1] ^ r), 0))
    out = pl.BlockSpec((1, 1, span, feature), lambda j, r, *_: (r, j, 0, 0))
    return pl.pallas_call(
        body,
        out_shape=[jax.ShapeDtypeStruct((ny, experts, span, feature), BF16)] * 2,
        grid_spec=pltpu.PrefetchScalarGridSpec(
            num_scalar_prefetch=1,
            grid=(experts, ny),
            in_specs=[vmem(a.shape) for a in ins[:6]] + [weight, weight],
            out_specs=[out, out],
            scratch_shapes=[pltpu.VMEM((experts, length, feature), BF16)] * 2,
        ),
        name="expert_weights",
        compiler_params=pltpu.CompilerParams(vmem_limit_bytes=VMEM_LIMIT),
        cost_estimate=pl.CostEstimate(flops=int(21 * 1.15e9), bytes_accessed=0, transcendentals=0),
    )(place, *ins)


AXES = ("dp", "expert")


def local(
    plan,
    source,
    target,
    attention_in,
    attention_out,
    gains,
    encoder_up,
    encoder_down,
    decoder_up,
    decoder_down,
    encoder_route,
    encoder_slot,
    decoder_route,
    decoder_slot,
    output_grad,
):
    _, rows, feature = source.shape
    cap = 2 * rows // EXPERTS
    n_dp, n_expert, ny = plan.n_dp, plan.n_expert, plan.ny
    dp = lax.axis_index("dp").astype(jnp.int32)
    place = jnp.stack([dp // ny, dp % ny])
    zr = plan.zr
    za, zb, zc = zr[0::3], zr[1::3], zr[2::3]
    weights = (attention_in, attention_out)

    cols = jnp.stack([encoder_route * cap + encoder_slot, decoder_route * cap + decoder_slot]).reshape(4, rows)
    own_cols = cols.reshape(2, 2, rows, 1)
    out_grad = output_grad.reshape(2, rows, feature)
    og = out_grad.astype(BF16)

    enc, dec, (u_near, og_near, col_near), (col_far, og_far) = self_forward(
        plan, source, target, cols, og, gains, *weights, [Job(cols, None, z=zr), Job(og, None, z=za + zb)]
    )
    e1, u, *enc_saved = enc
    t1, hc, *dec_saved = dec
    (e2, memory), (col_far, og_far) = expert_forward(
        plan,
        u_near,
        col_near,
        own_cols[0],
        e1,
        gains,
        encoder_up,
        encoder_down,
        [Job(None, col_far, x=zr), Job(og, og_far, z=zc, x=za)],
    )
    (t2, w, w_near, *cross_saved), (col_far, og_far, u_far) = cross_forward(
        plan, hc, t1, memory, gains, *weights, [Job(None, col_far, c=zr), Job(None, og_far, x=zb, c=za), Job(u, None, z=zr)]
    )
    (upstream, dg5, result), (og_far, w_far) = decoder_experts(
        plan,
        w_near,
        og_near,
        col_near,
        own_cols[1],
        t2,
        out_grad,
        gains,
        decoder_up,
        decoder_down,
        [Job(None, og_far, x=zc, c=zb), Job(w, None, z=zb + za)],
    )
    (decoder_output, fg, fg_low, fg_near, dt1, cross_dw, dg2, dg4), (og_far, w_far, u_far) = cross_backward(
        plan,
        upstream,
        result,
        own_cols[1],
        t2,
        e2,
        hc,
        t1,
        gains,
        cross_saved,
        *weights,
        [Job(None, og_far, c=zc), Job(w, w_far, z=zc), Job(None, u_far, x=zr)],
    )
    (de1, dg1), (w_far, u_far, fg_far) = encoder_experts(
        plan,
        u_near,
        fg_near,
        col_near,
        own_cols[0],
        e1,
        fg,
        gains,
        encoder_up,
        encoder_down,
        [Job(None, w_far, x=za), Job(None, u_far, c=zr), Job(fg_low, None, z=zr)],
    )
    (source_grad, target_grad, enc_dw, dec_dw, dg0, dg3), (w_far,) = self_backward(
        plan,
        de1,
        dt1,
        source,
        target,
        gains,
        enc_saved,
        dec_saved,
        *weights,
        [Job(None, w_far, x=zb + zc, c=za)],
    )
    w_far, fg_far = transfers(plan, "far_a", 8, [Job(None, w_far, c=zb + zc), Job(None, fg_far, x=zr)])
    dec_g = expert_weights(
        plan, place, 1, (w_near, w_far), (og_near, og_far), (col_near, col_far), decoder_up, decoder_down
    )
    (fg_far,) = transfers(plan, "far_b", 9, [Job(None, fg_far, c=zr)])
    enc_g = expert_weights(
        plan, place, 0, (u_near, u_far), (fg_near, fg_far), (col_near, col_far), encoder_up, encoder_down
    )

    def swap(value, d, e):
        pairs = []
        for i in range(n_dp):
            for k in range(n_expert):
                pairs.append((i * n_expert + k, (i ^ d) * n_expert + (k ^ e)))
        return lax.ppermute(value, AXES, pairs)

    def finish_weights(grads):
        blocks = [grads[i] for i in range(ny)]
        half = ny // 2
        while half >= 1:
            got = swap(jnp.concatenate([b[None] for b in blocks[half:]], axis=0), half, 0)
            if half == 1:
                return blocks[0].astype(F32) + got[0].astype(F32)
            blocks = [(blocks[i].astype(F32) + got[i].astype(F32)).astype(BF16) for i in range(half)]
            half //= 2

    counts = jnp.sum(
        (
            jnp.stack([encoder_route, decoder_route]).reshape(2, 2, rows, 1)
            == jnp.arange(EXPERTS, dtype=jnp.int32)
        ).astype(F32),
        axis=2,
    )
    gain_grads = jnp.concatenate([dg0, dg1, dg2, dg3, dg4, dg5], axis=0)
    dw = lax.psum(jnp.stack([enc_dw, dec_dw, cross_dw]), AXES).astype(F32)
    gain_grads, counts = lax.psum((gain_grads, counts), AXES)
    return (
        decoder_output.reshape(2, 1, rows, feature),
        source_grad[None],
        target_grad[None],
        dw[..., : 3 * feature],
        dw[..., 3 * feature :],
        gain_grads,
        finish_weights(enc_g[0]),
        finish_weights(enc_g[1]),
        finish_weights(dec_g[0]),
        finish_weights(dec_g[1]),
        counts.astype(jnp.int32),
    )


def solution(mesh):
    plan = Plan(mesh.shape["dp"], mesh.shape["expert"])
    in_specs = (
        P("dp", "expert", None),
        P("dp", "expert", None),
        P(),
        P(),
        P(),
        P("expert", None, None),
        P("expert", None, None),
        P("expert", None, None),
        P("expert", None, None),
        P(None, "dp", "expert"),
        P(None, "dp", "expert"),
        P(None, "dp", "expert"),
        P(None, "dp", "expert"),
        P(None, "dp", "expert", None),
    )
    out_specs = (
        P(None, "dp", "expert", None),
        P("dp", "expert", None),
        P("dp", "expert", None),
        P(),
        P(),
        P(),
        P("expert", "dp", None),
        P("expert", "dp", None),
        P("expert", "dp", None),
        P("expert", "dp", None),
        P(),
    )
    return jax.shard_map(
        functools.partial(local, plan),
        mesh=mesh,
        in_specs=in_specs,
        out_specs=out_specs,
        check_vma=False,
    )
```

```python
import functools

import jax
import jax.numpy as jnp
from jax import lax
from jax.experimental import pallas as pl
from jax.experimental.pallas import tpu as pltpu
from jax.sharding import PartitionSpec as P

HEAD_DIM = 64
EXPERTS = 16
NORM_EPSILON = 1e-05
MASKED = -1e30
F32 = jnp.float32
BF16 = jnp.bfloat16
VMEM_LIMIT = 60 << 20
MESH = pl.DeviceIdType.MESH
DMA = pltpu.SemaphoreType.DMA


def nn(a, b):
    return jnp.dot(a, b, preferred_element_type=F32)


def nt(a, b):
    return lax.dot_general(a, b, (((1,), (1,)), ((), ())), preferred_element_type=F32)


def tn(a, b):
    return lax.dot_general(a, b, (((0,), (0,)), ((), ())), preferred_element_type=F32)


def tt(a, b):
    return lax.dot_general(a, b, (((0,), (1,)), ((), ())), preferred_element_type=F32)


def norm_parts(x):
    mean = jnp.mean(x, axis=-1, keepdims=True)
    centered = x - mean
    spread = jnp.mean(centered * centered, axis=-1, keepdims=True)
    scale = lax.rsqrt(spread + NORM_EPSILON)
    return centered * scale, scale


def norm(x, gain):
    return norm_parts(x)[0] * gain


def norm_back(x, gain, grad):
    hat, scale = norm_parts(x)
    inner = grad * gain
    dx = scale * (
        inner
        - jnp.mean(inner, axis=-1, keepdims=True)
        - hat * jnp.mean(inner * hat, axis=-1, keepdims=True)
    )
    return dx, jnp.sum(grad * hat, axis=0, keepdims=True)


NORM_ROWS = 64


def norm_rows(src, dst, gain):
    for at in range(0, src.shape[0], NORM_ROWS):
        span = slice(at, at + NORM_ROWS)
        dst[span, :] = norm(src[span, :].astype(F32), gain).astype(dst.dtype)


def norm_back_rows(x, gain, grad, store):
    total = None
    for at in range(0, x.shape[0], NORM_ROWS):
        span = slice(at, at + NORM_ROWS)
        dx, part = norm_back(x[span, :].astype(F32), gain, grad[span, :].astype(F32))
        store(span, dx)
        total = part if total is None else total + part
    return total


GELU_A = 0.7978845608028654
GELU_B = 0.044715


def gelu(x):
    return 0.5 * x * (1.0 + jnp.tanh(x * (GELU_A + (GELU_A * GELU_B) * (x * x))))


def gelu_both(x):
    sq = x * x
    th = jnp.tanh(x * (GELU_A + (GELU_A * GELU_B) * sq))
    half = 0.5 * (1.0 + th)
    slope = half + (0.5 * x) * (1.0 - th * th) * (GELU_A + (3.0 * GELU_A * GELU_B) * sq)
    return x * half, slope


WIDE = 256
TALL = 64


def gelu_pair(raw, grad, act, slopes):
    for at in range(0, raw.shape[0], TALL):
        span = slice(at, at + TALL)
        value, slope = gelu_both(raw[span])
        if act is not None:
            act[span, :] = value.astype(BF16)
        slopes[span, :] = (slope * grad[span]).astype(BF16)


def xor(value, bits):
    b = 1
    while b <= bits:
        if bits & b:
            value = value + b * (1 - 2 * lax.rem(lax.div(value, b), 2))
        b *= 2
    return value


def peer(to):
    return (xor(lax.axis_index("dp"), to[0]), xor(lax.axis_index("expert"), to[1]))


def send(src, dst, send_sem, recv_sem, to):
    return pltpu.make_async_remote_copy(
        src_ref=src, dst_ref=dst, send_sem=send_sem, recv_sem=recv_sem, device_id=peer(to), device_id_type=MESH
    )


def expert_peers(ids):
    return [(0, r) for r in ids[1:]]


class Gather:
    def __init__(self, ids, near, send_sems, recv_sems):
        self.pos = {r: i for i, r in enumerate(ids)}
        self.far = [r for r in ids if r % 2 == 0 and r > 0]
        self.near, self.sems = near, (send_sems, recv_sems)

    def copy(self, r, src, to):
        at = self.pos[r]
        return send(src, self.near.at[at], self.sems[0].at[at], self.sems[1].at[at], (0, to))

    def first(self, r):
        return self.copy(r, self.near.at[0], r)

    def second(self, r):
        return self.copy(r ^ 1, self.near.at[self.pos[r]], 1)

    def start(self):
        for r in self.far:
            self.first(r).start()
        self.first(1).start()

    def forward(self):
        for r in self.far:
            self.first(r).wait_recv()
            self.second(r).start()

    def finish(self):
        for r in self.far:
            self.second(r).wait_recv()
        self.first(1).wait_recv()
        for r in self.far:
            self.first(r).wait_send()
            self.second(r).wait_send()
        self.first(1).wait_send()


class Scatter:
    def __init__(self, ids, parts, got, send_sems, recv_sems):
        self.pos = {r: i for i, r in enumerate(ids)}
        self.odd = [r for r in ids if r % 2]
        self.even = [r for r in ids if r % 2 == 0]
        self.parts, self.got, self.sems = parts, got, (send_sems, recv_sems)

    def copy(self, r, to):
        at = self.pos[r]
        return send(
            self.parts.at[at], self.got.at[self.pos[r ^ 1]], self.sems[0].at[at], self.sems[1].at[at], (0, to)
        )

    def start(self):
        for r in self.odd:
            self.copy(r, 1).start()

    def middle(self):
        for r in self.odd:
            self.copy(r, 1).wait_recv()
        for r in self.even[1:]:
            at = self.pos[r]
            self.parts[at] = (self.parts[at].astype(F32) + self.got[at].astype(F32)).astype(BF16)
            self.copy(r, r).start()

    def finish(self):
        total = self.parts[0].astype(F32) + self.got[0].astype(F32)
        for r in self.even[1:]:
            self.copy(r, r).wait_recv()
            total = total + self.got[self.pos[r ^ 1]].astype(F32)
        for r in self.odd:
            self.copy(r, 1).wait_send()
        for r in self.even[1:]:
            self.copy(r, r).wait_send()
        return total


class Job:
    def __init__(self, own, far, z=(), x=(), c=(), s=(), then_x=(), then_c=(), near=None, by_pass=False):
        self.own, self.far, self.z, self.x, self.c, self.s = own, far, list(z), list(x), list(c), list(s)
        self.then_x, self.then_c, self.near, self.by_pass = list(then_x), list(then_c), near, by_pass

    def inputs(self):
        return ([self.own] if self.z else []) + ([self.near] if self.s else [])

    def shape(self, plan):
        return (plan.nz - 1, plan.n_expert) + self.own.shape

    def moves(self, plan, refs, far):
        for zr in self.z:
            yield "z", zr, refs[0], far.at[zr - 1, 0], (zr * plan.ny, 0)
        for zr in self.s:
            for r in plan.across:
                at = plan.pos[r]
                if self.by_pass:
                    for p in range(2):
                        yield "s", zr, refs[-1].at[p, at], far.at[zr - 1, at, p], (zr * plan.ny, 0)
                else:
                    yield "s", zr, refs[-1].at[at], far.at[zr - 1, at], (zr * plan.ny, 0)
        yield from self.steps("x", plan, far, self.x)
        yield from self.steps("c", plan, far, self.c)

    def steps(self, kind, plan, far, zrs):
        for zr in zrs:
            if kind == "x":
                for r in plan.across:
                    yield "x", zr, far.at[zr - 1, 0], far.at[zr - 1, plan.pos[r]], (0, r)
            else:
                for r in [0] + plan.across:
                    yield "c", zr, far.at[zr - 1, plan.pos[r]], far.at[zr - 1, plan.pos[r ^ 1]], (0, 1)

    def second(self, plan, refs, far):
        yield from self.steps("x", plan, far, self.then_x)
        yield from self.steps("c", plan, far, self.then_c)

    def targets(self, plan):
        return (
            [(zr * plan.ny, 0) for zr in self.z + self.s]
            + ([(0, r) for r in plan.across] if self.x or self.then_x else [])
            + ([(0, 1)] if self.c or self.then_c else [])
        )


class Swap:
    def __init__(self, own, paced=False):
        self.own, self.far, self.paced = own, None, paced

    def inputs(self):
        return [self.own]

    def shape(self, plan):
        return (plan.ny - 1,) + self.own.shape[1:]

    def moves(self, plan, refs, far):
        for r in range(1, plan.ny):
            for j in range(self.own.shape[1]):
                yield "p" if self.paced else "y", r, refs[0].at[r, j], far.at[r - 1, j], (r, 0)

    def second(self, plan, refs, far):
        return ()

    def targets(self, plan):
        return [(r, 0) for r in range(1, plan.ny)]


class Plan:
    def __init__(self, n_dp, n_expert):
        self.n_dp, self.n_expert = n_dp, n_expert
        self.ny = 2 if n_dp <= 8 else 4
        self.nz = n_dp // self.ny
        ids, bit = [0], n_expert // 2
        while bit >= 1:
            ids = ids + [i ^ bit for i in ids]
            bit //= 2
        self.ids = ids
        self.pos = {r: i for i, r in enumerate(ids)}
        self.across = [r for r in ids if r % 2 == 0 and r > 0]
        self.zr = list(range(1, self.nz))


class Background:
    def __init__(self, plan, jobs, owns, fars, send_sems, recv_sems, peers):
        self.plan, self.jobs, self.peers = plan, jobs, peers
        self.owns, self.fars, self.sems, self.began = owns, fars, (send_sems, recv_sems), False
        self.released = 0

    def copies(self):
        n = 0
        for job, own, far in zip(self.jobs, self.owns, self.fars):
            moves = [(False, m) for m in job.moves(self.plan, own, far)]
            moves += [(True, m) for m in job.second(self.plan, own, far)]
            for late, (kind, zr, src, dst, to) in moves:
                yield job, late, kind, zr, send(src, dst, self.sems[0].at[n], self.sems[1].at[n], to)
                n += 1

    def greet(self):
        barrier = pltpu.get_barrier_semaphore()
        for p in self.peers:
            pl.semaphore_signal(barrier, inc=1, device_id=peer(p), device_id_type=MESH)
        pl.semaphore_wait(barrier, len(self.peers))

    def start(self):
        for _, late, kind, _, copy in self.copies():
            if not late and kind != "p":
                copy.start()

    def release(self, n):
        paced = [copy for _, _, kind, _, copy in self.copies() if kind == "p"]
        for copy in paced[self.released : self.released + n]:
            copy.start()
        self.released += n

    def second(self):
        needs = [(job, zr) for job, late, _, zr, _ in self.copies() if late]
        for job, late, kind, zr, copy in self.copies():
            if not late and kind in "zx" and (job, zr) in needs:
                copy.wait_recv()
        for _, late, _, _, copy in self.copies():
            if late:
                copy.start()
        self.began = True

    def finish(self):
        if not self.began:
            self.second()
        self.release(sum(kind == "p" for _, _, kind, _, _ in self.copies()) - self.released)
        needs = [(job, zr) for job, late, _, zr, _ in self.copies() if late]
        for job, late, kind, zr, copy in self.copies():
            if not late and kind in "zx" and (job, zr) in needs:
                copy.wait_send()
            else:
                copy.wait()


class Blank:
    def __init__(self):
        self.at = self

    def __getitem__(self, at):
        return self


class AllReduce:
    LEAST = 16

    def __init__(self, plan, acc, groups, tmp, small, small_tmp, sems, small_sems, credits=None):
        self.acc, self.groups, self.tmp, self.small, self.small_tmp = acc, groups, tmp, small, small_tmp
        self.sems, self.small_sems, self.credits = sems, small_sems, credits
        self.orders = [[(0, 1)] + o for o in self.rotations(plan)]
        self.steps = len(self.orders[0])
        self.spans = [[(0, acc.shape[1])] for _ in groups]

    @staticmethod
    def rotations(plan):
        def powers(n):
            return [1 << i for i in range(n.bit_length() - 1)]

        x = [(0, 2 * b) for b in powers(plan.n_expert // 2)]
        y = [(b, 0) for b in powers(plan.ny)]
        z = [(plan.ny * b, 0) for b in powers(plan.nz)]
        return [x + y + z, y + z + x, z + x + y]

    @classmethod
    def tmp_rows(cls, plan, rows):
        total = 0
        for _ in range(1 + len(cls.rotations(plan)[0])):
            rows = max(rows // 2, cls.LEAST)
            total += rows
        return total

    @classmethod
    def peers(cls, plan):
        return [(0, 1)] + cls.rotations(plan)[0]

    @staticmethod
    def side(to):
        axis, bits = ("dp", to[0]) if to[0] else ("expert", to[1])
        return lax.rem(lax.div(lax.axis_index(axis), bits), 2)

    def halves(self, g, step):
        return self.spans[g][step][1] > self.LEAST

    def place(self, g, step):
        to = self.orders[g % 3][step]
        low, length = self.spans[g][step]
        if length <= self.LEAST:
            return to, low, low, length
        half = length // 2
        side = self.side(to)
        return to, low + (1 - side) * half, low + side * half, half

    def view(self, ref, g, low, length):
        index, first, width = self.groups[g]
        if not isinstance(low, int):
            low = pl.multiple_of(low, self.LEAST)
        return ref.at[index, pl.ds(low, length), pl.ds(first, width)]

    def offset(self, g, step):
        return sum(self.place(g, n)[3] for n in range(step))

    def reduce_copy(self, g, step):
        to, sent, _, length = self.place(g, step)
        dst = self.view(self.tmp, g, self.offset(g, step), length)
        return send(self.view(self.acc, g, sent, length), dst, self.sems.at[0, g, step], self.sems.at[1, g, step], to)

    def small_copy(self, step):
        to = self.orders[0][step]
        return send(
            self.small, self.small_tmp.at[step], self.small_sems.at[0, step], self.small_sems.at[1, step], to
        )

    def reduce_start(self, step):
        for g in range(len(self.groups)):
            self.reduce_copy(g, step).start()
        if self.small is not None:
            self.small_copy(step).start()

    def reduce_finish(self, step):
        for g in range(len(self.groups)):
            self.reduce_copy(g, step).wait()
            _, _, kept, length = self.place(g, step)
            mine = self.view(self.acc, g, kept, length)
            got = self.view(self.tmp, g, self.offset(g, step), length)
            mine[...] = (mine[...].astype(F32) + got[...].astype(F32)).astype(BF16)
            if self.halves(g, step):
                pl.semaphore_signal(
                    self.credits.at[g, step],
                    inc=1,
                    device_id=peer(self.orders[g % 3][step]),
                    device_id_type=MESH,
                )
            self.spans[g].append((kept, length))
        if self.small is not None:
            self.small_copy(step).wait()
            self.small[...] = self.small[...] + self.small_tmp[step]

    def spread_copy(self, g, step):
        to = self.orders[g % 3][step]
        low, length = self.spans[g][step + 1]
        mine = self.view(self.acc, g, low, length)
        return send(mine, mine, self.sems.at[2, g, step], self.sems.at[3, g, step], to)

    def spread(self, step, action):
        for g in range(len(self.groups)):
            if self.halves(g, step):
                copy = self.spread_copy(g, step)
                if action == "start":
                    pl.semaphore_wait(self.credits.at[g, step], 1)
                    copy.start()
                else:
                    copy.wait()

    def run(self):
        for step in range(self.steps):
            self.reduce_start(step)
            yield
            self.reduce_finish(step)
        for step in reversed(range(self.steps)):
            self.spread(step, "start")
            yield
            self.spread(step, "wait")


def vmem(shape):
    return pl.BlockSpec(shape, lambda *_: (0,) * len(shape))


ANYWHERE = pl.BlockSpec(memory_space=pl.ANY)


def fused(
    plan, body, ins, outs, name, cid=None, peers=(), jobs=(), grid=None, in_specs=None, out_specs=None, scratch=(), us=10
):
    whole = (lambda shape: pl.BlockSpec(memory_space=pltpu.VMEM)) if grid is None else vmem
    in_specs = [None] * len(ins) if in_specs is None else in_specs
    out_specs = [None] * len(outs) if out_specs is None else out_specs
    in_specs = [whole(a.shape) if s is None else s for a, s in zip(ins, in_specs)]
    out_specs = [whole(o[0]) if s is None else s for o, s in zip(outs, out_specs)]
    ins, outs, scratch = list(ins), list(outs), list(scratch)
    n_in, n_out, n_scratch = len(ins), len(outs), len(scratch)
    aliases, places, count, peers = {}, [], 0, list(peers)
    for k, job in enumerate(jobs):
        place = range(len(ins), len(ins) + len(job.inputs()))
        ins += job.inputs()
        in_specs += [ANYWHERE] * len(job.inputs())
        if job.far is not None:
            aliases[len(ins)] = n_out + k
            ins.append(job.far)
            in_specs.append(ANYWHERE)
            outs.append((job.far.shape, job.far.dtype))
        else:
            outs.append((job.shape(plan), job.own.dtype))
        out_specs.append(ANYWHERE)
        places.append(place)
        blank = [Blank(), Blank()]
        count += len(list(job.moves(plan, blank, Blank()))) + len(list(job.second(plan, blank, Blank())))
        peers += [p for p in dict.fromkeys(job.targets(plan)) if p not in peers]
    if jobs:
        scratch += [DMA((count,)), DMA((count,))]

    def run(*refs):
        i, o, s = refs[: len(ins)], refs[len(ins) : len(ins) + len(outs)], refs[len(ins) + len(outs) :]
        if cid is None:
            return body(*i, *o, *s)
        sems = s[n_scratch:] if jobs else (None, None)
        bg = Background(plan, jobs, [[i[n] for n in p] for p in places], o[n_out:], *sems, peers)
        body(bg, *i[:n_in], *o[:n_out], *s[:n_scratch])

    moved = sum(a.size * a.dtype.itemsize for a in ins[:n_in])
    extra = {} if grid is None else {"grid": grid}
    got = pl.pallas_call(
        run,
        out_shape=[jax.ShapeDtypeStruct(s, d) for s, d in outs],
        in_specs=in_specs,
        out_specs=out_specs,
        scratch_shapes=scratch,
        input_output_aliases=aliases,
        name=name,
        compiler_params=pltpu.CompilerParams(
            vmem_limit_bytes=VMEM_LIMIT, collective_id=cid, has_side_effects=cid is not None
        ),
        cost_estimate=pl.CostEstimate(flops=int(us * 1.15e9), bytes_accessed=moved, transcendentals=0),
        **extra,
    )(*ins)
    return got[:n_out], got[n_out:]


CHUNK = 128


def zero_half(rows, half):
    zero = jnp.zeros_like(rows)
    return jnp.concatenate([rows, zero] if half == 0 else [zero, rows], axis=0)


def half_lanes(pair, half):
    lane = lax.broadcasted_iota(jnp.int32, pair.shape, 1)
    keep = lane < HEAD_DIM if half == 0 else lane >= HEAD_DIM
    return jnp.where(keep, pair, jnp.zeros_like(pair))


def fold(values, op):
    return op(values.reshape(values.shape[0] // 8, 8, values.shape[1]), axis=0)


def masked(scores, at, ids, rows):
    me = lax.axis_index("expert")
    first = xor(me, ids[at // rows]) * rows + at % rows
    key = first + lax.broadcasted_iota(jnp.int32, scores.shape, 0)
    query = me * rows + lax.broadcasted_iota(jnp.int32, scores.shape, 1)
    return jnp.where(key <= query, scores, MASKED)


def head_pairs(pairs, body, between):
    at = 0
    for stop, act in [*between, (pairs, None)]:
        if stop > at:
            lax.fori_loop(at, stop, lambda h2, _: (body(h2), 0)[1], 0)
            at = stop
        if act is not None:
            act()


def attend_forward(q_t, k, v_t, causal, o_t, lse, scratch, between=()):
    raw, low = scratch
    length = k.shape[0]

    def body(h2):
        first = pl.multiple_of(h2 * 128, 128)
        for half in range(2):
            rows = pl.ds(pl.multiple_of(h2 * 128 + half * HEAD_DIM, HEAD_DIM), HEAD_DIM)
            query = zero_half(q_t[rows, :], half)
            top = None
            for at in range(0, length, CHUNK):
                scores = nn(k[at : at + CHUNK, pl.ds(first, 128)], query)
                if causal is not None:
                    scores = masked(scores, at, *causal)
                raw[half, at : at + CHUNK, :] = scores
                part = fold(scores, jnp.max)
                top = part if top is None else jnp.maximum(top, part)
            top = jnp.max(top, axis=0, keepdims=True)
            total = None
            for at in range(0, length, CHUNK):
                lifted = jnp.exp(raw[half, at : at + CHUNK, :] - top)
                low[half, at : at + CHUNK, :] = lifted.astype(BF16)
                part = fold(lifted, jnp.sum)
                total = part if total is None else total + part
            total = jnp.sum(total, axis=0, keepdims=True)
            o_t[rows, :] = nn(v_t[rows, :], low[half]) * (1.0 / total)
            lse[pl.ds(2 * h2 + half, 1), :] = top + jnp.log(total)

    head_pairs(k.shape[1] // 128, body, between)


def attend_backward(q, k, v, k_t, do, o_t, lse, causal, dk, dv, dq_t, scratch, between=()):
    q_t, do_t, low = scratch
    length = k.shape[0]
    q_t[...] = q[...].astype(F32).T.astype(BF16)
    do_t[...] = do[...].astype(F32).T.astype(BF16)

    def body(h2):
        first = pl.multiple_of(h2 * 128, 128)
        pair = pl.ds(first, 128)
        q_pair, do_pair = q[:, pair], do[:, pair]
        parts = []
        for half in range(2):
            rows = pl.ds(pl.multiple_of(h2 * 128 + half * HEAD_DIM, HEAD_DIM), HEAD_DIM)
            do_rows = do_t[rows, :]
            centre = jnp.sum(do_rows.astype(F32) * o_t[rows, :], axis=0, keepdims=True)
            parts.append(
                (
                    rows,
                    zero_half(q_t[rows, :], half),
                    zero_half(do_rows, half),
                    half_lanes(q_pair, half),
                    half_lanes(do_pair, half),
                    lse[pl.ds(2 * h2 + half, 1), :],
                    centre,
                )
            )
        for at in range(0, length, CHUNK):
            span = slice(at, at + CHUNK)
            dk_pair = dv_pair = None
            for half, (_, q_row, do_row, q_lane, do_lane, total, centre) in enumerate(parts):
                scores = nn(k[span, pair], q_row)
                if causal is not None:
                    scores = masked(scores, at, *causal)
                weights = jnp.exp(scores - total)
                weights_grad = nn(v[span, pair], do_row)
                scores_grad = (weights * (weights_grad - centre)).astype(BF16)
                low[half, span, :] = scores_grad
                dv_part = nn(weights.astype(BF16), do_lane)
                dk_part = nn(scores_grad, q_lane)
                dv_pair = dv_part if dv_pair is None else dv_pair + dv_part
                dk_pair = dk_part if dk_pair is None else dk_pair + dk_part
            dk[span, pair] = dk_pair.astype(BF16)
            dv[span, pair] = dv_pair.astype(BF16)
        for half in range(2):
            rows = parts[half][0]
            dq_t[rows, :] = (nn(k_t[rows, :], low[half]) * HEAD_DIM ** (-0.5)).astype(BF16)

    head_pairs(k.shape[1] // 128, body, between)


def forward_scratch(plan, rows, feature):
    length = plan.n_expert * rows
    return [
        pltpu.VMEM((feature, rows), BF16),
        pltpu.VMEM((feature, length), BF16),
        pltpu.VMEM((2, length, rows), F32),
        pltpu.VMEM((2, length, rows), BF16),
    ]


def backward_scratch(plan, rows, feature):
    length = plan.n_expert * rows
    return [
        pltpu.VMEM((length, feature), BF16),
        pltpu.VMEM((length, feature), BF16),
        pltpu.VMEM((feature, rows), BF16),
        pltpu.VMEM((rows, feature), BF16),
        pltpu.VMEM((feature, rows), BF16),
        pltpu.VMEM((feature, rows), BF16),
        pltpu.VMEM((2, length, rows), BF16),
    ]


def project_rows(hm, win, k, k_t, v, v_t):
    feature = hm.shape[1]
    w_k, w_v = win[:, feature : 2 * feature], win[:, 2 * feature :]
    k[...] = nn(hm, w_k).astype(BF16)
    v[...] = nn(hm, w_v).astype(BF16)
    k_t[...] = tt(w_k, hm).astype(BF16)
    v_t[...] = tt(w_v, hm).astype(BF16)


def project_query(rows, win):
    return nn(rows, win[:, : rows.shape[1]]).astype(BF16).astype(F32) * HEAD_DIM ** (-0.5)


def attention_shapes(plan, rows, feature):
    length = plan.n_expert * rows
    return [
        ((length, feature), BF16),
        ((feature, length), BF16),
        ((length, feature), BF16),
        ((rows, feature), BF16),
        ((feature, rows), F32),
        ((feature // HEAD_DIM, rows), F32),
    ]


def gather_rows(ids, col, returned):
    me = lax.axis_index("expert")
    total = None
    for r, rows in zip(ids, returned):
        slots = rows.shape[0] * rows.shape[1]
        local = col - xor(me, r) * slots
        hot = (local == lax.broadcasted_iota(jnp.int32, (col.shape[0], slots), 1)).astype(BF16)
        part = nn(hot, rows.reshape(slots, rows.shape[-1]))
        total = part if total is None else total + part
    return total


def fill_buffers(cap, col_of, token_of, sources, dest):
    experts = dest.shape[0]
    slots = experts * cap
    me = lax.axis_index("expert")
    for s in sources:
        for p in range(2):
            local = col_of(s, p) - me * slots
            hot = (local == lax.broadcasted_iota(jnp.int32, (slots, local.shape[1]), 0)).astype(BF16)
            rows = nn(hot, token_of(s, p)).astype(BF16)
            at = (2 * s + p) * cap
            for j in range(experts):
                dest[j, at : at + cap, :] = rows[j * cap : (j + 1) * cap]


def column(ref, s, layer, p):
    return ref[s, pl.ds(2 * layer + p, 1), :]


class Return:
    def __init__(self, ids, stage, ret, send_sems, recv_sems):
        self.ids, self.stage, self.ret, self.sems = ids, stage, ret, (send_sems, recv_sems)

    def copy(self, s, n):
        return send(
            self.stage.at[s, n], self.ret.at[s, n], self.sems[0].at[s, n], self.sems[1].at[s, n], (0, self.ids[s])
        )

    def put(self, j, rows, cap):
        for s in range(len(self.ids)):
            for p in range(2):
                at = (2 * s + p) * cap
                (self.ret if s == 0 else self.stage)[s, j, p] = rows[at : at + cap]

    def start(self, j):
        for s in range(1, len(self.ids)):
            self.copy(s, j).start()

    def finish(self, experts):
        for n in range(experts):
            for s in range(1, len(self.ids)):
                self.copy(s, n).wait()

    def rows(self, p):
        return [self.ret[s, :, p] for s in range(len(self.ids))]


def load(src, dst, sem):
    return pltpu.make_async_copy(src, dst, sem)


def self_forward(plan, source, target, cols, out_grad, gains, inward, outward, jobs):
    ids, count = plan.ids, plan.n_expert
    _, rows, feature = source.shape
    length = count * rows

    def body(bg, *refs):
        src, tgt, col, og, g, win_any, wout_any = refs[:7]
        enc, dec = refs[7:16], refs[16:25]
        u_near, og_near, col_near = refs[25:28]
        near_s, near_t, win, wout, q_t, v_t, raw, low, lsem, *sems = refs[28:]
        weights = [load(win_any.at[n], win.at[n], lsem.at[n]) for n in range(2)]
        weights += [load(wout_any.at[n], wout.at[n], lsem.at[2 + n]) for n in range(2)]
        for w in weights:
            w.start()
        g_s, g_t, g_u, g_og, g_col = [
            Gather(ids, ref, sems[2 * n], sems[2 * n + 1])
            for n, ref in enumerate((near_s, near_t, u_near, og_near, col_near))
        ]
        near_s[0] = src[0]
        near_t[0] = tgt[0]
        col_near[0] = col[...]
        og_near[0] = og[...]
        bg.greet()
        g_s.start()
        g_t.start()
        g_col.start()
        bg.start()

        def attend(near, outs, n, gain, gain_next, causal, first, between):
            after, nxt, hm, k, k_t, v, q, o_t, lse = outs
            norm_rows(near.at[0], hm.at[0:rows], g[gain : gain + 1])
            if n == 0:
                for w in weights:
                    w.wait()
            q_scaled = project_query(hm[0:rows, :], win[n])
            q[...] = q_scaled.astype(BF16)
            first()
            for b in range(1, count):
                norm_rows(near.at[b], hm.at[b * rows : (b + 1) * rows], g[gain : gain + 1])
            project_rows(hm[...], win[n], k, k_t, v, v_t)
            q_t[...] = q_scaled.T.astype(BF16)
            attend_forward(q_t, k, v_t, causal, o_t, lse, (raw, low), [(2, between)])
            merged = o_t[...].T.astype(BF16)
            after[...] = near[0].astype(F32) + nn(merged, wout[n])
            norm_rows(after, nxt, g[gain_next : gain_next + 1])

        def first_enc():
            g_s.forward()
            g_s.finish()
            g_og.start()

        def mid_enc():
            g_t.forward()
            g_col.forward()

        attend(near_s, enc, 0, 0, 1, None, first_enc, mid_enc)
        u_near[0] = enc[1][...]
        g_u.start()

        def mid_dec():
            g_u.forward()
            g_og.forward()

        attend(near_t, dec, 1, 3, 4, (ids, rows), g_t.finish, mid_dec)
        g_u.finish()
        g_og.finish()
        g_col.finish()
        bg.finish()

    shapes = [((rows, feature), F32), ((rows, feature), BF16), ((length, feature), BF16)]
    shapes += attention_shapes(plan, rows, feature)
    outs, fars = fused(
        plan,
        body,
        [source, target, cols, out_grad, gains, inward, outward],
        shapes
        + shapes
        + [
            ((count, rows, feature), BF16),
            ((count, 2, rows, feature), BF16),
            ((count,) + cols.shape, jnp.int32),
        ],
        "self_forward",
        cid=1,
        peers=expert_peers(ids),
        jobs=jobs,
        in_specs=[None] * 5 + [ANYWHERE] * 2,
        scratch=[
            pltpu.VMEM((count, rows, feature), BF16),
            pltpu.VMEM((count, rows, feature), BF16),
            pltpu.VMEM((2, feature, 3 * feature), BF16),
            pltpu.VMEM((2, feature, feature), BF16),
            *forward_scratch(plan, rows, feature),
            DMA((4,)),
        ]
        + [DMA((count,))] * 10,
        us=35,
    )
    return outs[:9], outs[9:18], outs[18:], fars


def return_scratch(plan, experts, cap, feature):
    shape = (plan.n_expert, experts, 2, cap, feature)
    return [pltpu.VMEM(shape, BF16), pltpu.VMEM(shape, BF16), DMA(shape[:2]), DMA(shape[:2])]


def expert_forward(plan, near, col_near, own_col, residual, gains, weight_up, weight_down, jobs):
    ids, count = plan.ids, plan.n_expert
    experts, hidden, feature = weight_up.shape
    rows = near.shape[1]
    cap = 2 * rows // EXPERTS
    length = count * 2 * cap

    def body(bg, u, col, mine, res, g, up, down, out, nxt, buf, act, *scratch):
        j = pl.program_id(0)
        back = Return(ids, *scratch)

        @pl.when(j == 0)
        def _():
            bg.greet()
            bg.start()
            fill_buffers(cap, lambda s, p: col[s, p : p + 1, :], lambda s, p: u[s], range(count), buf)

        for at in range(0, hidden, WIDE):
            raw = nt(buf[j], up[0, at : at + WIDE])
            for n in range(0, length, TALL):
                act[n : n + TALL, at : at + WIDE] = gelu(raw[n : n + TALL]).astype(BF16)
        back.put(j, nn(act[...], down[0]).astype(BF16), cap)
        back.start(j)

        @pl.when(j == experts - 1)
        def _():
            back.finish(experts)
            for p in range(2):
                out[p] = res[...] + gather_rows(ids, mine[p], back.rows(p))
                norm_rows(out.at[p], nxt.at[p], g[2:3])
            bg.finish()

    weight = pl.BlockSpec((1, hidden, feature), lambda j: (j, 0, 0))
    return fused(
        plan,
        body,
        [near, col_near, own_col, residual, gains, weight_up, weight_down],
        [((2, rows, feature), F32), ((2, rows, feature), BF16)],
        "expert_forward",
        cid=2,
        peers=expert_peers(ids),
        jobs=jobs,
        grid=(experts,),
        in_specs=[None] * 5 + [weight, weight],
        scratch=[pltpu.VMEM((experts, length, feature), BF16), pltpu.VMEM((length, hidden), BF16)]
        + return_scratch(plan, experts, cap, feature),
        us=22,
    )


def cross_forward(plan, hc, mid, memory, gains, inward, outward, jobs):
    ids, count = plan.ids, plan.n_expert
    rows, feature = hc.shape
    length = count * rows

    def body(bg, h, res, mem, g, win_any, wout_any, t2, w, w_near, hm, k, k_t, v, q, o_t, lse, win, wout, q_t, v_t, raw, low, lsem, *sems):
        weights = [load(win_any.at[2], win, lsem.at[0]), load(wout_any.at[2], wout, lsem.at[1])]
        for x in weights:
            x.start()
        gather_m = [Gather(ids, hm.at[p], sems[p].at[0], sems[p].at[1]) for p in range(2)]
        gather_w = [Gather(ids, w_near.at[p], sems[2 + p].at[0], sems[2 + p].at[1]) for p in range(2)]
        for p in range(2):
            hm[p, 0] = mem[p]
        bg.greet()
        gather_m[0].start()
        gather_m[1].start()
        bg.start()
        for x in weights:
            x.wait()
        q_scaled = project_query(h[...], win[...])
        q[...] = q_scaled.astype(BF16)
        q_t[...] = q_scaled.T.astype(BF16)
        gather_m[0].forward()
        gather_m[0].finish()
        for p in range(2):
            project_rows(hm[p].reshape(length, feature), win[...], k.at[p], k_t.at[p], v.at[p], v_t)
            between = gather_m[1].forward if p == 0 else gather_w[0].forward
            attend_forward(q_t, k.at[p], v_t, None, o_t.at[p], lse.at[p], (raw, low), [(2, between)])
            t2[p] = res[...] + nn(o_t[p].T.astype(BF16), wout[...])
            norm_rows(t2.at[p], w_near.at[p, 0], g[5:6])
            w[p] = w_near[p, 0]
            gather_w[p].start()
            if p == 0:
                gather_m[1].finish()
        gather_w[1].forward()
        gather_w[0].finish()
        gather_w[1].finish()
        bg.finish()

    saved = attention_shapes(plan, rows, feature)
    saved = [((2,) + s, d) if n != 3 else (s, d) for n, (s, d) in enumerate(saved)]
    return fused(
        plan,
        body,
        [hc, mid, memory, gains, inward, outward],
        [
            ((2, rows, feature), F32),
            ((2, rows, feature), BF16),
            ((2, count, rows, feature), BF16),
            ((2, count, rows, feature), BF16),
        ]
        + saved,
        "cross_forward",
        cid=3,
        peers=expert_peers(ids),
        jobs=jobs,
        in_specs=[None] * 4 + [ANYWHERE] * 2,
        scratch=[
            pltpu.VMEM((feature, 3 * feature), BF16),
            pltpu.VMEM((feature, feature), BF16),
            *forward_scratch(plan, rows, feature),
            DMA((2,)),
        ]
        + [DMA((2, count))] * 4,
        us=35,
    )


def decoder_experts(plan, w_near, og_near, col_near, own_col, crossed, out_grad, gains, weight_up, weight_down, jobs):
    ids, count = plan.ids, plan.n_expert
    experts, hidden, feature = weight_up.shape
    rows = crossed.shape[1]
    cap = 2 * rows // EXPERTS
    length = count * 2 * cap

    def body(bg, w, og, col, mine, t2, og_own, g, up, down, upstream, dg, result, buf, gbuf, act, slopes, *scratch):
        j = pl.program_id(0)
        back = Return(ids, *scratch)

        @pl.when(j == 0)
        def _():
            bg.greet()
            bg.start()
            fill_buffers(cap, lambda s, p: col[s, 2 + p : 3 + p, :], lambda s, p: w[p, s], range(count), buf)
            fill_buffers(cap, lambda s, p: col[s, 2 + p : 3 + p, :], lambda s, p: og[s, p], range(count), gbuf)

        for at in range(0, hidden, WIDE):
            span = slice(at, at + WIDE)
            gelu_pair(nt(buf[j], up[0, span]), nt(gbuf[j], down[0, span]), act.at[:, span], slopes.at[:, span])
        back.put(j, nn(slopes[...], up[0]).astype(BF16), cap)
        back.start(j)
        res = nn(act[...], down[0]).astype(BF16)
        for s in range(count):
            for p in range(2):
                at = (2 * s + p) * cap
                result[s, 0, p] = res[at : at + cap]

        @pl.when(j == experts - 1)
        def _():
            bg.second()
            back.finish(experts)
            total = None
            for p in range(2):
                upstream[p] = gather_rows(ids, mine[p], back.rows(p))

                def store(span, dx):
                    upstream[p, span, :] = og_own[p, span, :] + dx

                gain = norm_back_rows(t2.at[p], g[5:6], upstream.at[p], store)
                total = gain if total is None else total + gain
            dg[...] = total
            bg.finish()

    weight = pl.BlockSpec((1, hidden, feature), lambda j: (j, 0, 0))
    return fused(
        plan,
        body,
        [w_near, og_near, col_near, own_col, crossed, out_grad, gains, weight_up, weight_down],
        [((2, rows, feature), F32), ((1, feature), F32), ((count, experts, 2, cap, feature), BF16)],
        "decoder_experts",
        cid=4,
        peers=expert_peers(ids),
        jobs=jobs,
        grid=(experts,),
        in_specs=[None] * 7 + [weight, weight],
        out_specs=[None, None, pl.BlockSpec((count, 1, 2, cap, feature), lambda j: (0, j, 0, 0, 0))],
        scratch=[pltpu.VMEM((experts, length, feature), BF16)] * 2
        + [pltpu.VMEM((length, hidden), BF16)] * 2
        + return_scratch(plan, experts, cap, feature),
        us=30,
    )


def weight_grads(hq, hm, dq, dk, dv, o_t, d_branch):
    return [tn(hq, dq), tn(hm, dk), tn(hm, dv), nn(o_t.astype(BF16), d_branch)]


def cross_backward(
    plan, upstream, final, hc, mid, gains, saved, inward, outward, jobs
):
    ids, count = plan.ids, plan.n_expert
    rows, feature = mid.shape
    length = count * rows

    def body(bg, *refs):
        up, e2, h, t1, g = refs[:5]
        hm, k, k_t, v, q, o_t, lse, win_any, wout_any = refs[5:14]
        fg, fg_low, fg_near, dt1, dw, dg2, dg4 = refs[14:21]
        dk, dv, dq_t, do, *work, dw_acc, parts, got, win, wout, lsem = refs[21:-4]
        sems = refs[-4:]
        weights = [load(win_any.at[2], win, lsem.at[0]), load(wout_any.at[2], wout, lsem.at[1])]
        for x in weights:
            x.start()
        scatter = [Scatter(ids, parts.at[p], got.at[p], sems[p].at[0], sems[p].at[1]) for p in range(2)]
        gather = [Gather(ids, fg_near.at[p], sems[2 + p].at[0], sems[2 + p].at[1]) for p in range(2)]

        def memory_back(p):
            fg[p] = scatter[p].finish()

            def store(span, dx):
                fg[p, span, :] = dx
                fg_low[p, span, :] = dx.astype(BF16)
                fg_near[p, 0, span, :] = dx.astype(BF16)

            gain = norm_back_rows(e2.at[p], g[2:3], fg.at[p], store)
            gather[p].start()
            if p == 0:
                dg2[...] = gain
            else:
                dg2[...] = dg2[...] + gain

        bg.greet()
        bg.start()
        for x in weights:
            x.wait()
        dh = None
        for p in range(2):
            d_branch = up[p].astype(BF16)
            do[...] = nt(d_branch, wout[...]).astype(BF16)
            between = () if p == 0 else ((1, scatter[0].middle), (2, lambda: memory_back(0)), (3, bg.second))
            attend_backward(
                q, k.at[p], v.at[p], k_t.at[p], do, o_t.at[p], lse.at[p], None, dk, dv, dq_t, work, between
            )
            for b in range(count):
                span = slice(b * rows, (b + 1) * rows)
                part = nt(dk[span, :], win[:, feature : 2 * feature]) + nt(dv[span, :], win[:, 2 * feature :])
                parts[p, b] = part.astype(BF16)
            scatter[p].start()
            dq = dq_t[...].astype(F32).T.astype(BF16)
            back = nt(dq, win[:, :feature])
            dh = back if dh is None else dh + back
            if p == 1:
                scatter[1].middle()
                gather[0].forward()
            grads = weight_grads(
                h[...], hm[p].reshape(length, feature), dq, dk[...], dv[...], o_t[p], d_branch
            )
            for n, value in enumerate(grads):
                at = slice(n * feature, (n + 1) * feature)
                if p == 0:
                    dw_acc[:, at] = value
                else:
                    dw[:, at] = (dw_acc[:, at] + value).astype(BF16)
        memory_back(1)
        dt1[...] = dh

        def store_mid(span, dx):
            dt1[span, :] = up[0, span, :] + up[1, span, :] + dx

        dg4[...] = norm_back_rows(t1, g[4:5], dt1, store_mid)
        gather[1].forward()
        gather[0].finish()
        gather[1].finish()
        bg.finish()

    block = (rows, feature)
    return fused(
        plan,
        body,
        [upstream, final, hc, mid, gains, *saved, inward, outward],
        [
            ((2,) + block, F32),
            ((2,) + block, BF16),
            ((2, count) + block, BF16),
            (block, F32),
            ((feature, 4 * feature), BF16),
            ((1, feature), F32),
            ((1, feature), F32),
        ],
        "cross_backward",
        cid=5,
        peers=expert_peers(ids),
        jobs=jobs,
        in_specs=[None] * 12 + [ANYWHERE] * 2,
        scratch=[
            *backward_scratch(plan, rows, feature),
            pltpu.VMEM((feature, 4 * feature), F32),
            pltpu.VMEM((2, count) + block, BF16),
            pltpu.VMEM((2, count) + block, BF16),
            pltpu.VMEM((feature, 3 * feature), BF16),
            pltpu.VMEM((feature, feature), BF16),
            DMA((2,)),
        ]
        + [DMA((2, count))] * 4,
        us=45,
    )


def encoder_experts(plan, u_near, fg_near, col_near, own_col, attended, final_grad, gains, weight_up, weight_down, jobs):
    ids, count = plan.ids, plan.n_expert
    experts, hidden, feature = weight_up.shape
    rows = attended.shape[0]
    cap = 2 * rows // EXPERTS
    length = count * 2 * cap

    def body(bg, u, fgn, col, mine, e1, fg, g, up, down, de1, dg, buf, gbuf, slopes, *scratch):
        j = pl.program_id(0)
        back = Return(ids, *scratch)

        @pl.when(j == 0)
        def _():
            bg.greet()
            bg.start()
            fill_buffers(cap, lambda s, p: col[s, p : p + 1, :], lambda s, p: u[s], range(count), buf)
            fill_buffers(cap, lambda s, p: col[s, p : p + 1, :], lambda s, p: fgn[p, s], range(count), gbuf)

        for at in range(0, hidden, WIDE):
            span = slice(at, at + WIDE)
            gelu_pair(nt(buf[j], up[0, span]), nt(gbuf[j], down[0, span]), None, slopes.at[:, span])
        back.put(j, nn(slopes[...], up[0]).astype(BF16), cap)
        back.start(j)

        @pl.when(j == experts - 1)
        def _():
            back.finish(experts)
            de1[...] = gather_rows(ids, mine[0], back.rows(0)) + gather_rows(ids, mine[1], back.rows(1))

            def store(span, dx):
                de1[span, :] = fg[0, span, :] + fg[1, span, :] + dx

            dg[...] = norm_back_rows(e1, g[1:2], de1, store)
            bg.finish()

    weight = pl.BlockSpec((1, hidden, feature), lambda j: (j, 0, 0))
    return fused(
        plan,
        body,
        [u_near, fg_near, col_near, own_col, attended, final_grad, gains, weight_up, weight_down],
        [((rows, feature), F32), ((1, feature), F32)],
        "encoder_experts",
        cid=6,
        peers=expert_peers(ids),
        jobs=jobs,
        grid=(experts,),
        in_specs=[None] * 7 + [weight, weight],
        scratch=[pltpu.VMEM((experts, length, feature), BF16)] * 2
        + [pltpu.VMEM((length, hidden), BF16)]
        + return_scratch(plan, experts, cap, feature),
        us=30,
    )


def column_groups(n_dw, width):
    if n_dw % 3 == 0:
        return [(n, 0, width) for n in range(n_dw)]
    cut = (width // 3) // 128 * 128
    groups = []
    for n in range(n_dw):
        groups += [(n, 0, cut), (n, cut, width - 2 * cut), (n, width - cut, cut)]
    return groups


def attention_back(plan, ids, n, up, saved, win, wout, work, parts, scatter, dw, causal, between, after):
    hm, k, k_t, v, q, o_t, lse = saved
    dk, dv, dq_t, do, *rest = work
    rows, feature = q.shape
    d_branch = up[...].astype(BF16)
    do[...] = nt(d_branch, wout[...]).astype(BF16)
    attend_backward(q, k, v, k_t, do, o_t, lse, causal, dk, dv, dq_t, rest, between)
    dq = dq_t[...].astype(F32).T.astype(BF16)
    for b in [i for i, r in enumerate(ids) if r % 2] + [i for i, r in enumerate(ids) if r % 2 == 0]:
        span = slice(b * rows, (b + 1) * rows)
        part = nt(dk[span, :], win[:, feature : 2 * feature]) + nt(dv[span, :], win[:, 2 * feature :])
        if b == 0:
            part = part + nt(dq, win[:, :feature])
        parts[b] = part.astype(BF16)
    scatter.start()
    after()
    for i, value in enumerate(
        weight_grads(hm[0:rows, :], hm[...], dq, dk[...], dv[...], o_t[...], d_branch)
    ):
        dw[:, i * feature : (i + 1) * feature] = value.astype(BF16)


def input_back(up, src, gain, scatter, grad):
    grad[...] = scatter.finish()

    def store(span, dx):
        grad[span, :] = up[span, :] + dx

    return norm_back_rows(src.at[0], gain, grad, store)


def attention_scratch(plan, rows, feature):
    count = plan.n_expert
    return [
        *backward_scratch(plan, rows, feature),
        pltpu.VMEM((count, rows, feature), BF16),
        pltpu.VMEM((count, rows, feature), BF16),
        pltpu.VMEM((feature, 3 * feature), BF16),
        pltpu.VMEM((feature, feature), BF16),
    ]


def decoder_backward(plan, dec_up, target, gains, saved, inward, outward, jobs):
    ids, count = plan.ids, plan.n_expert
    _, rows, feature = target.shape

    def body(bg, *refs):
        up, src, g = refs[:3]
        saved_refs, win_any, wout_any = refs[3:10], refs[10], refs[11]
        grad, dw, dg = refs[12:15]
        *work, parts, got, win, wout, lsem, sems = refs[15:]
        weights = [load(win_any.at[1], win, lsem.at[0]), load(wout_any.at[1], wout, lsem.at[1])]
        for x in weights:
            x.start()
        bg.greet()
        bg.start()
        for x in weights:
            x.wait()
        scatter = Scatter(ids, parts, got, sems.at[0], sems.at[1])
        attention_back(
            plan, ids, 1, up, saved_refs, win, wout, work, parts, scatter, dw, (ids, rows), (), lambda: None
        )
        scatter.middle()
        bg.second()
        dg[...] = input_back(up, src, g[3:4], scatter, grad)
        bg.finish()

    return fused(
        plan,
        body,
        [dec_up, target, gains, *saved, inward, outward],
        [((rows, feature), F32), ((feature, 4 * feature), BF16), ((1, feature), F32)],
        "decoder_backward",
        cid=7,
        peers=expert_peers(ids),
        jobs=jobs,
        in_specs=[None] * 10 + [ANYWHERE] * 2,
        scratch=attention_scratch(plan, rows, feature) + [DMA((2,)), DMA((2, count))],
        us=28,
    )


def encoder_backward(plan, enc_up, source, gains, saved, inward, outward, sums, small, jobs):
    ids, count = plan.ids, plan.n_expert
    _, rows, feature = source.shape
    width = 4 * feature
    groups = column_groups(1, width)
    steps = 1 + len(AllReduce.rotations(plan)[0])
    n_dw = len(sums) + 1

    def body(bg, *refs):
        up, src, g, sm = refs[:4]
        saved_refs, win_any, wout_any = refs[4:11], refs[11], refs[12]
        sums_any = refs[13 : 13 + n_dw - 1]
        grad, sum_out, small_out = refs[12 + n_dw : 15 + n_dw]
        *work, parts, got, win, wout, acc, tmp, small_tmp, lsem, asem, ssem, credits, sems = refs[15 + n_dw :]
        weights = [load(win_any.at[0], win, lsem.at[0]), load(wout_any.at[0], wout, lsem.at[1])]
        firsts = [load(ref, acc.at[n], lsem.at[2 + n]) for n, ref in enumerate(sums_any)]
        for x in weights + firsts:
            x.start()
        small_out[...] = sm[...]
        bg.greet()
        bg.start()

        def reduce(n):
            return AllReduce(
                plan, acc.at[n : n + 1], groups, tmp.at[n : n + 1], None, None, asem.at[n], None, credits.at[n]
            ).run()

        for x in firsts:
            x.wait()
        runs = [reduce(n) for n in range(n_dw - 1)]

        def step(release=1):
            for run in runs:
                next(run, None)
            bg.release(release)

        step(0)
        for x in weights:
            x.wait()
        scatter = Scatter(ids, parts, got, sems.at[0], sems.at[1])
        between = ((2, step),)
        attention_back(
            plan, ids, 0, up, saved_refs, win, wout, work, parts, scatter, acc.at[n_dw - 1], None, between, step
        )
        runs.append(reduce(n_dw - 1))
        step()
        scatter.middle()
        step(1)
        small_out[0:1, :] = input_back(up, src, g[0:1], scatter, grad)
        runs.append(AllReduce(plan, acc, [], None, small_out, small_tmp, None, ssem).run())
        for _ in range(2 * steps):
            step()
        last = load(acc, sum_out, lsem.at[0])
        last.start()
        last.wait()
        bg.finish()

    peers = expert_peers(ids)
    return fused(
        plan,
        body,
        [enc_up, source, gains, small, *saved, inward, outward, *sums],
        [((rows, feature), F32), ((n_dw, feature, width), BF16), (small.shape, F32)],
        "encoder_backward",
        cid=9,
        peers=peers + [p for p in AllReduce.peers(plan) if p not in peers],
        jobs=jobs,
        in_specs=[None] * 11 + [ANYWHERE] * (2 + len(sums)),
        out_specs=[None, ANYWHERE, None],
        scratch=attention_scratch(plan, rows, feature)
        + [
            pltpu.VMEM((n_dw, feature, width), BF16),
            pltpu.VMEM((n_dw, AllReduce.tmp_rows(plan, feature), width), BF16),
            pltpu.VMEM((steps,) + small.shape, F32),
            DMA((1 + n_dw,)),
            DMA((n_dw, 4, len(groups), steps)),
            DMA((2, steps)),
            pltpu.SemaphoreType.REGULAR((n_dw, len(groups), steps)),
            DMA((2, count)),
        ],
        us=90,
    )


def column_groups(n_dw, width):
    if n_dw % 3 == 0:
        return [(n, 0, width) for n in range(n_dw)]
    cut = (width // 3) // 128 * 128
    groups = []
    for n in range(n_dw):
        groups += [(n, 0, cut), (n, cut, width - 2 * cut), (n, width - cut, cut)]
    return groups


def self_backward(plan, enc_up, dec_up, source, target, gains, enc_saved, dec_saved, inward, outward, jobs):
    ids, count = plan.ids, plan.n_expert
    _, rows, feature = source.shape
    length = count * rows

    def body(bg, *refs):
        ups, srcs, g = refs[:2], refs[2:4], refs[4]
        saved = (refs[5:12], refs[12:19])
        win_any, wout_any = refs[19:21]
        grads, dws, dgs = refs[21:23], refs[23:25], refs[25:27]
        dk, dv, dq_t, do, *work, parts, got, win, wout, lsem = refs[27:-2]
        sems = refs[-2:]
        weights = [load(win_any.at[n], win.at[n], lsem.at[n]) for n in range(2)]
        weights += [load(wout_any.at[n], wout.at[n], lsem.at[2 + n]) for n in range(2)]
        for x in weights:
            x.start()
        scatter = [Scatter(ids, parts.at[n], got.at[n], sems[n].at[0], sems[n].at[1]) for n in range(2)]

        def finish(n):
            gain = 3 * n
            grads[n][...] = scatter[n].finish()

            def store(span, dx):
                grads[n][span, :] = ups[n][span, :] + dx

            dgs[n][...] = norm_back_rows(srcs[n].at[0], g[gain : gain + 1], grads[n], store)

        bg.greet()
        bg.start()
        for x in weights:
            x.wait()
        for n in range(2):
            hm, k, k_t, v, q, o_t, lse = saved[n]
            d_branch = ups[n][...].astype(BF16)
            do[...] = nt(d_branch, wout[n]).astype(BF16)
            causal = (ids, rows) if n == 1 else None
            between = () if n == 0 else ((0, bg.second), (1, scatter[0].middle), (3, lambda: finish(0)))
            attend_backward(q, k, v, k_t, do, o_t, lse, causal, dk, dv, dq_t, work, between)
            dq = dq_t[...].astype(F32).T.astype(BF16)
            for b in range(count):
                span = slice(b * rows, (b + 1) * rows)
                part = nt(dk[span, :], win[n, :, feature : 2 * feature])
                part = part + nt(dv[span, :], win[n, :, 2 * feature :])
                if b == 0:
                    part = part + nt(dq, win[n, :, :feature])
                parts[n, b] = part.astype(BF16)
            scatter[n].start()
            if n == 1:
                scatter[1].middle()
            for i, value in enumerate(
                weight_grads(hm[0:rows, :], hm[...], dq, dk[...], dv[...], o_t[...], d_branch)
            ):
                dws[n][:, i * feature : (i + 1) * feature] = value.astype(BF16)
        finish(1)
        bg.finish()

    block = (rows, feature)
    return fused(
        plan,
        body,
        [enc_up, dec_up, source, target, gains, *enc_saved, *dec_saved, inward, outward],
        [(block, F32)] * 2 + [((feature, 4 * feature), BF16)] * 2 + [((1, feature), F32)] * 2,
        "self_backward",
        cid=7,
        peers=expert_peers(ids),
        jobs=jobs,
        in_specs=[None] * 19 + [ANYWHERE] * 2,
        scratch=[
            *backward_scratch(plan, rows, feature),
            pltpu.VMEM((2, count) + block, BF16),
            pltpu.VMEM((2, count) + block, BF16),
            pltpu.VMEM((2, feature, 3 * feature), BF16),
            pltpu.VMEM((2, feature, feature), BF16),
            DMA((4,)),
        ]
        + [DMA((2, count))] * 2,
        us=40,
    )


def weight_sources(plan, layer, tokens, grads, cols):
    count = plan.n_expert

    def col_of(s, p):
        row = slice(2 * layer + p, 2 * layer + p + 1)
        return cols[0][s, row, :] if s < count else cols[1][s // count - 1, s % count, row, :]

    def token_of(s, p):
        if layer == 0:
            return tokens[0][s] if s < count else tokens[1][s // count - 1, s % count]
        return tokens[0][p, s] if s < count else tokens[1][s // count - 1, s % count, p]

    def grad_of(s, p):
        if s < count:
            return grads[0][p, s] if layer == 0 else grads[0][s, p]
        return grads[1][s // count - 1, s % count, p]

    return col_of, token_of, grad_of


def weight_products(up, down, buf, gbuf, act, slopes):
    for at in range(0, buf.shape[0], WIDE):
        span = slice(at, at + WIDE)
        gelu_pair(nt(up, buf[span, :]), nt(down, gbuf[span, :]), act.at[:, span], slopes.at[:, span])
    return nn(slopes[...], buf[...]).astype(BF16), nn(act[...], gbuf[...]).astype(BF16)


def expert_weights(plan, layer, cid, tokens, grads, cols, weight_up, weight_down, jobs, home=None):
    count, ny, nz, ids = plan.n_expert, plan.ny, plan.nz, plan.ids
    experts, hidden, feature = weight_up.shape
    rows = tokens[0].shape[-2]
    cap = 2 * rows // EXPERTS
    sources = count * nz
    length = sources * 2 * cap
    span = hidden // plan.n_dp
    block = ny * span

    def body(bg, *refs):
        cn, cf = refs[:2]
        if home is not None:
            mine, res = refs[2:4]
        big, up_any, down_any = refs[n_small : n_small + 4], refs[n_small + 4], refs[n_small + 5]
        outs = refs[n_in:]
        up_out, down_out = outs[:2]
        held, (up, down, buf, gbuf, act, slopes, lsem) = outs[n_out : n_out + 4], outs[n_out + 4 : n_out + 11]
        first = pl.multiple_of(lax.div(lax.axis_index("dp"), ny) * block, block)
        loads = [load(src, dst, lsem.at[n]) for n, (src, dst) in enumerate(zip(big, held))]
        loads.append(load(up_any.at[:, pl.ds(first, block)], up, lsem.at[4]))
        loads.append(load(down_any.at[:, pl.ds(first, block)], down, lsem.at[5]))
        for x in loads:
            x.start()
        bg.greet()
        if home is not None:
            ret, rs, rr = outs[n_out + 11 :]
            own = load(refs[n_in - 1].at[0], ret.at[0], lsem.at[6])
            own.start()
            bring = [
                send(refs[n_in - 1].at[s], ret.at[s], rs.at[s], rr.at[s], (0, ids[s])) for s in range(1, count)
            ]
            for x in bring:
                x.start()
        bg.start()
        col_of, token_of, grad_of = weight_sources(plan, layer, held[0:2], held[2:4], (cn, cf))
        for n, (reader, dest) in enumerate(((token_of, buf), (grad_of, gbuf))):
            loads[2 * n].wait()
            fill_buffers(cap, col_of, reader, range(count), dest)
            loads[2 * n + 1].wait()
            fill_buffers(cap, col_of, reader, range(count, sources), dest)
        loads[4].wait()
        loads[5].wait()
        y = lax.rem(lax.axis_index("dp"), ny)
        for r in reversed(range(ny)):
            at = pl.ds(pl.multiple_of(xor(y, r) * span, span), span)

            def product(j, _):
                up_out[r, j], down_out[r, j] = weight_products(
                    up[j, at, :], down[j, at, :], buf.at[j], gbuf.at[j], act, slopes
                )
                return 0

            lax.fori_loop(0, experts, product, 0)
        if home is not None:
            own.wait()
            for x in bring:
                x.wait()
            for p in range(2):
                mixed = gather_rows(ids, mine[p], [ret[s, :, p] for s in range(count)])
                outs[2][p] = (res[p] + mixed).astype(BF16)
        bg.finish()

    small = [*cols] + ([] if home is None else [home[1], home[2]])
    n_small = len(small)
    big = [tokens[0], tokens[1], grads[0], grads[1], weight_up, weight_down] + ([] if home is None else [home[0]])
    n_in = n_small + len(big)
    outs = [((ny, experts, span, feature), BF16)] * 2 + ([] if home is None else [((2, rows, feature), BF16)])
    n_out = len(outs)
    scratch = [pltpu.VMEM(a.shape, BF16) for a in big[:4]] + [
        pltpu.VMEM((experts, block, feature), BF16),
        pltpu.VMEM((experts, block, feature), BF16),
        pltpu.VMEM((experts, length, feature), BF16),
        pltpu.VMEM((experts, length, feature), BF16),
        pltpu.VMEM((span, length), BF16),
        pltpu.VMEM((span, length), BF16),
        DMA((7,)),
    ]
    if home is not None:
        scratch += [pltpu.VMEM(home[0].shape, BF16), DMA((count,)), DMA((count,))]
    return fused(
        plan,
        body,
        small + big,
        outs,
        ("encoder", "decoder")[layer] + "_weights",
        cid=cid,
        peers=[] if home is None else expert_peers(ids),
        jobs=jobs,
        in_specs=[None] * n_small + [ANYWHERE] * len(big),
        scratch=scratch,
        us=25,
    )


def finish(plan, sums, dec, dec_got, enc, enc_got):
    n_dw, feature, width = sums.shape
    _, experts, span, _ = enc[0].shape
    part = feature // experts
    ny = plan.ny

    def body(s, du, dd, dug, ddg, eu, ed, eug, edg, a_in, a_out, eu_out, ed_out, du_out, dd_out):
        for n in range(n_dw):
            a_in[n] = s[n_dw - 1 - n, :, : 3 * feature].astype(F32)
            a_out[n] = s[n_dw - 1 - n, :, 3 * feature :].astype(F32)
        for out, own, others in (
            (eu_out, eu[0, 0], [eug[r, 0] for r in range(ny - 1)]),
            (ed_out, ed[0, 0], [edg[r, 0] for r in range(ny - 1)]),
            (du_out, du[0, 0], [dug[r, 0] for r in range(ny - 1)]),
            (dd_out, dd[0, 0], [ddg[r, 0] for r in range(ny - 1)]),
        ):
            total = own.astype(F32)
            for other in others:
                total = total + other.astype(F32)
            out[0] = total

    block = (1, span, feature)
    first = pl.BlockSpec((1,) + block, lambda j: (0, j, 0, 0))
    others = pl.BlockSpec((ny - 1,) + block, lambda j: (0, j, 0, 0))
    own = pl.BlockSpec(block, lambda j: (j, 0, 0))
    return fused(
        plan,
        body,
        [sums, *dec, *dec_got, *enc, *enc_got],
        [((n_dw, feature, 3 * feature), F32), ((n_dw, feature, feature), F32)] + [((experts, span, feature), F32)] * 4,
        "finish",
        grid=(experts,),
        in_specs=[
            pl.BlockSpec((n_dw, part, width), lambda j: (0, j, 0)),
            first,
            first,
            others,
            others,
            first,
            first,
            others,
            others,
        ],
        out_specs=[
            pl.BlockSpec((n_dw, part, 3 * feature), lambda j: (0, j, 0)),
            pl.BlockSpec((n_dw, part, feature), lambda j: (0, j, 0)),
        ]
        + [own] * 4,
        us=10,
    )[0]


def local(
    plan,
    source,
    target,
    attention_in,
    attention_out,
    gains,
    encoder_up,
    encoder_down,
    decoder_up,
    decoder_down,
    encoder_route,
    encoder_slot,
    decoder_route,
    decoder_slot,
    output_grad,
):
    _, rows, feature = source.shape
    cap = 2 * rows // EXPERTS
    zr = plan.zr
    za, zb, zc = zr[0::3], zr[1::3], zr[2::3]
    weights = (attention_in, attention_out)

    cols = jnp.stack([encoder_route * cap + encoder_slot, decoder_route * cap + decoder_slot]).reshape(4, rows)
    own_cols = cols.reshape(2, 2, rows, 1)
    out_grad = output_grad.reshape(2, rows, feature)
    og = out_grad.astype(BF16)

    counts = jnp.sum(
        (
            jnp.stack([encoder_route, decoder_route]).reshape(4, rows, 1) == jnp.arange(EXPERTS, dtype=jnp.int32)
        ).astype(F32),
        axis=1,
    )

    enc, dec, (u_near, og_near, col_near), (col_far, og_far) = self_forward(
        plan, source, target, cols, og, gains, *weights, [Job(cols, None, z=zr), Job(og, None, z=za + zb)]
    )
    e1, u, *enc_saved = enc
    t1, hc, *dec_saved = dec
    (e2, memory), (col_far, og_far) = expert_forward(
        plan,
        u_near,
        col_near,
        own_cols[0],
        e1,
        gains,
        encoder_up,
        encoder_down,
        [Job(None, col_far, x=zr), Job(og, og_far, z=zc)],
    )
    (t2, w, w_near, *cross_saved), (col_far, og_far, u_far) = cross_forward(
        plan,
        hc,
        t1,
        memory,
        gains,
        *weights,
        [Job(None, col_far, c=zr), Job(None, og_far, s=za + zb, near=og_near), Job(u, None, z=zr)],
    )
    (upstream, dg5, result), (og_far, w_far) = decoder_experts(
        plan,
        w_near,
        og_near,
        col_near,
        own_cols[1],
        t2,
        out_grad,
        gains,
        decoder_up,
        decoder_down,
        [Job(None, og_far, c=za + zb, then_x=zc), Job(w, None, z=za + zb)],
    )
    (fg, fg_low, fg_near, dt1, cross_dw, dg2, dg4), (w_far, og_far, u_far) = cross_backward(
        plan,
        upstream,
        e2,
        hc,
        t1,
        gains,
        cross_saved,
        *weights,
        [
            Job(w, w_far, z=zc, s=za + zb, then_x=zc, near=w_near, by_pass=True),
            Job(None, og_far, c=zc),
            Job(None, u_far, x=zr),
        ],
    )
    (de1, dg1), (w_far, u_far, fg_far) = encoder_experts(
        plan,
        u_near,
        fg_near,
        col_near,
        own_cols[0],
        e1,
        fg,
        gains,
        encoder_up,
        encoder_down,
        [Job(None, w_far, c=zr), Job(None, u_far, c=zr), Job(fg_low, None, z=za + zb)],
    )
    dec_g, (fg_far,) = expert_weights(
        plan,
        1,
        8,
        (w_near, w_far),
        (og_near, og_far),
        (col_near, col_far),
        decoder_up,
        decoder_down,
        [Job(fg_low, fg_far, z=zc, x=za + zb)],
    )
    (target_grad, dec_dw, dg3), (fg_far, up_got) = decoder_backward(
        plan,
        dt1,
        target,
        gains,
        dec_saved,
        *weights,
        [Job(None, fg_far, x=zc, c=za + zb, then_c=zc), Swap(dec_g[0])],
    )
    (*enc_g, decoder_output), (down_got,) = expert_weights(
        plan,
        0,
        10,
        (u_near, u_far),
        (fg_near, fg_far),
        (col_near, col_far),
        encoder_up,
        encoder_down,
        [Swap(dec_g[1])],
        (result, own_cols[1], t2),
    )
    count_row = jnp.pad(counts.reshape(1, -1), ((0, 1), (0, feature - counts.size)))
    small = jnp.concatenate([jnp.zeros_like(dg1), dg1, dg2, dg3, dg4, dg5, count_row], axis=0)
    (source_grad, sums, small), enc_got = encoder_backward(
        plan,
        de1,
        source,
        gains,
        enc_saved,
        *weights,
        [cross_dw, dec_dw],
        small,
        [Swap(enc_g[0], paced=True), Swap(enc_g[1], paced=True)],
    )
    a_in, a_out, enc_up_g, enc_down_g, dec_up_g, dec_down_g = finish(
        plan, sums, dec_g, (up_got, down_got), enc_g, enc_got
    )
    return (
        decoder_output.reshape(2, 1, rows, feature),
        source_grad[None],
        target_grad[None],
        a_in,
        a_out,
        small[:6],
        enc_up_g,
        enc_down_g,
        dec_up_g,
        dec_down_g,
        small[6, : counts.size].reshape(2, 2, EXPERTS).astype(jnp.int32),
    )


def solution(mesh):
    plan = Plan(mesh.shape["dp"], mesh.shape["expert"])
    in_specs = (
        P("dp", "expert", None),
        P("dp", "expert", None),
        P(),
        P(),
        P(),
        P("expert", None, None),
        P("expert", None, None),
        P("expert", None, None),
        P("expert", None, None),
        P(None, "dp", "expert"),
        P(None, "dp", "expert"),
        P(None, "dp", "expert"),
        P(None, "dp", "expert"),
        P(None, "dp", "expert", None),
    )
    out_specs = (
        P(None, "dp", "expert", None),
        P("dp", "expert", None),
        P("dp", "expert", None),
        P(),
        P(),
        P(),
        P("expert", "dp", None),
        P("expert", "dp", None),
        P("expert", "dp", None),
        P("expert", "dp", None),
        P(),
    )
    return jax.shard_map(
        functools.partial(local, plan),
        mesh=mesh,
        in_specs=in_specs,
        out_specs=out_specs,
        check_vma=False,
    )
```

```python
import functools

import jax
import jax.numpy as jnp
from jax import lax
from jax.experimental import pallas as pl
from jax.experimental.pallas import tpu as pltpu
from jax.sharding import PartitionSpec as P

HEAD_DIM = 64
EXPERTS = 16
NORM_EPSILON = 1e-05
MASKED = -1e30
F32 = jnp.float32
BF16 = jnp.bfloat16
VMEM_LIMIT = 60 << 20
MESH = pl.DeviceIdType.MESH
DMA = pltpu.SemaphoreType.DMA


def nn(a, b):
    return jnp.dot(a, b, preferred_element_type=F32)


def nt(a, b):
    return lax.dot_general(a, b, (((1,), (1,)), ((), ())), preferred_element_type=F32)


def tn(a, b):
    return lax.dot_general(a, b, (((0,), (0,)), ((), ())), preferred_element_type=F32)


def tt(a, b):
    return lax.dot_general(a, b, (((0,), (1,)), ((), ())), preferred_element_type=F32)


def norm_parts(x):
    mean = jnp.mean(x, axis=-1, keepdims=True)
    centered = x - mean
    spread = jnp.mean(centered * centered, axis=-1, keepdims=True)
    scale = lax.rsqrt(spread + NORM_EPSILON)
    return centered * scale, scale


def norm(x, gain):
    return norm_parts(x)[0] * gain


def norm_back(x, gain, grad):
    hat, scale = norm_parts(x)
    inner = grad * gain
    dx = scale * (
        inner
        - jnp.mean(inner, axis=-1, keepdims=True)
        - hat * jnp.mean(inner * hat, axis=-1, keepdims=True)
    )
    return dx, jnp.sum(grad * hat, axis=0, keepdims=True)


NORM_ROWS = 64


def norm_rows(src, dst, gain):
    for at in range(0, src.shape[0], NORM_ROWS):
        span = slice(at, at + NORM_ROWS)
        dst[span, :] = norm(src[span, :].astype(F32), gain).astype(dst.dtype)


def norm_back_rows(x, gain, grad, store):
    total = None
    for at in range(0, x.shape[0], NORM_ROWS):
        span = slice(at, at + NORM_ROWS)
        dx, part = norm_back(x[span, :].astype(F32), gain, grad[span, :].astype(F32))
        store(span, dx)
        total = part if total is None else total + part
    return total


GELU_A = 0.7978845608028654
GELU_B = 0.044715


def gelu(x):
    return 0.5 * x * (1.0 + jnp.tanh(x * (GELU_A + (GELU_A * GELU_B) * (x * x))))


def gelu_both(x):
    sq = x * x
    th = jnp.tanh(x * (GELU_A + (GELU_A * GELU_B) * sq))
    half = 0.5 * (1.0 + th)
    slope = half + (0.5 * x) * (1.0 - th * th) * (GELU_A + (3.0 * GELU_A * GELU_B) * sq)
    return x * half, slope


WIDE = 256
TALL = 64


def gelu_pair(raw, grad, act, slopes):
    for at in range(0, raw.shape[0], TALL):
        span = slice(at, at + TALL)
        value, slope = gelu_both(raw[span])
        if act is not None:
            act[span, :] = value.astype(BF16)
        slopes[span, :] = (slope * grad[span]).astype(BF16)


def xor(value, bits):
    b = 1
    while b <= bits:
        if bits & b:
            value = value + b * (1 - 2 * lax.rem(lax.div(value, b), 2))
        b *= 2
    return value


def peer(to):
    return (xor(lax.axis_index("dp"), to[0]), xor(lax.axis_index("expert"), to[1]))


def send(src, dst, send_sem, recv_sem, to):
    return pltpu.make_async_remote_copy(
        src_ref=src, dst_ref=dst, send_sem=send_sem, recv_sem=recv_sem, device_id=peer(to), device_id_type=MESH
    )


def expert_peers(ids):
    return [(0, r) for r in ids[1:]]


class Gather:
    def __init__(self, ids, near, send_sems, recv_sems):
        self.pos = {r: i for i, r in enumerate(ids)}
        self.far = [r for r in ids if r % 2 == 0 and r > 0]
        self.near, self.sems = near, (send_sems, recv_sems)

    def copy(self, r, src, to):
        at = self.pos[r]
        return send(src, self.near.at[at], self.sems[0].at[at], self.sems[1].at[at], (0, to))

    def first(self, r):
        return self.copy(r, self.near.at[0], r)

    def second(self, r):
        return self.copy(r ^ 1, self.near.at[self.pos[r]], 1)

    def start(self):
        for r in self.far:
            self.first(r).start()
        self.first(1).start()

    def forward(self):
        for r in self.far:
            self.first(r).wait_recv()
            self.second(r).start()

    def finish(self):
        for r in self.far:
            self.second(r).wait_recv()
        self.first(1).wait_recv()
        for r in self.far:
            self.first(r).wait_send()
            self.second(r).wait_send()
        self.first(1).wait_send()


class Scatter:
    def __init__(self, ids, parts, got, send_sems, recv_sems):
        self.pos = {r: i for i, r in enumerate(ids)}
        self.odd = [r for r in ids if r % 2]
        self.even = [r for r in ids if r % 2 == 0]
        self.parts, self.got, self.sems = parts, got, (send_sems, recv_sems)

    def copy(self, r, to):
        at = self.pos[r]
        return send(
            self.parts.at[at], self.got.at[self.pos[r ^ 1]], self.sems[0].at[at], self.sems[1].at[at], (0, to)
        )

    def start(self):
        for r in self.odd:
            self.copy(r, 1).start()

    def middle(self):
        for r in self.odd:
            self.copy(r, 1).wait_recv()
        for r in self.even[1:]:
            at = self.pos[r]
            self.parts[at] = (self.parts[at].astype(F32) + self.got[at].astype(F32)).astype(BF16)
            self.copy(r, r).start()

    def finish(self):
        total = self.parts[0].astype(F32) + self.got[0].astype(F32)
        for r in self.even[1:]:
            self.copy(r, r).wait_recv()
            total = total + self.got[self.pos[r ^ 1]].astype(F32)
        for r in self.odd:
            self.copy(r, 1).wait_send()
        for r in self.even[1:]:
            self.copy(r, r).wait_send()
        return total


class Job:
    def __init__(self, own, far, z=(), x=(), c=(), s=(), later=(), near=None, by_pass=False, local=False):
        self.own, self.far, self.near, self.by_pass, self.local = own, far, near, by_pass, local
        self.todo = [(0, "z", z), (0, "s", s), (0, "x", x), (0, "c", c), *later]

    def has(self, kind):
        return any(k == kind and len(zrs) > 0 for _, k, zrs in self.todo)

    def inputs(self):
        if self.local:
            return []
        return ([self.own] if self.has("z") else []) + ([self.near] if self.has("s") else [])

    def shape(self, plan):
        return (plan.nz - 1, plan.n_expert) + self.own.shape

    def moves(self, plan, refs, far):
        for stage, kind, zrs in self.todo:
            for zr in zrs:
                z = (zr * plan.ny, 0)
                if kind == "z" and not self.local:
                    yield stage, kind, zr, refs[0], far.at[zr - 1, 0], z
                elif kind in "zs":
                    for r in [0] if kind == "z" else plan.across:
                        at = plan.pos[r]
                        if self.by_pass:
                            for p in range(2):
                                yield stage, kind, zr, refs[-1].at[p, at], far.at[zr - 1, at, p], z
                        else:
                            yield stage, kind, zr, refs[-1].at[at], far.at[zr - 1, at], z
                elif kind == "x":
                    for r in plan.across:
                        yield stage, kind, zr, far.at[zr - 1, 0], far.at[zr - 1, plan.pos[r]], (0, r)
                else:
                    for r in [0] + plan.across:
                        yield stage, kind, zr, far.at[zr - 1, plan.pos[r]], far.at[zr - 1, plan.pos[r ^ 1]], (0, 1)

    def before(self, kind):
        return {"x": "z", "c": "zsx"}.get(kind, "")

    def targets(self, plan):
        return (
            [(zr * plan.ny, 0) for _, kind, zrs in self.todo if kind in "zs" for zr in zrs]
            + ([(0, r) for r in plan.across] if self.has("x") else [])
            + ([(0, 1)] if self.has("c") else [])
        )


class Swap:
    def __init__(self, own, paced=False):
        self.own, self.far, self.paced = own, None, paced

    def inputs(self):
        return [self.own]

    def shape(self, plan):
        return (plan.ny - 1,) + self.own.shape[1:]

    def moves(self, plan, refs, far):
        for r in range(1, plan.ny):
            for j in range(self.own.shape[1]):
                yield 0, "p" if self.paced else "y", r, refs[0].at[r, j], far.at[r - 1, j], (r, 0)

    def before(self, kind):
        return ""

    def targets(self, plan):
        return [(r, 0) for r in range(1, plan.ny)]


class Plan:
    def __init__(self, n_dp, n_expert):
        self.n_dp, self.n_expert = n_dp, n_expert
        self.ny = 2 if n_dp <= 8 else 4
        self.nz = n_dp // self.ny
        ids, bit = [0], n_expert // 2
        while bit >= 1:
            ids = ids + [i ^ bit for i in ids]
            bit //= 2
        self.ids = ids
        self.pos = {r: i for i, r in enumerate(ids)}
        self.across = [r for r in ids if r % 2 == 0 and r > 0]
        self.zr = list(range(1, self.nz))


class Background:
    def __init__(self, plan, jobs, owns, fars, send_sems, recv_sems, peers):
        self.plan, self.jobs, self.peers = plan, jobs, peers
        self.owns, self.fars, self.sems = owns, fars, (send_sems, recv_sems)
        self.released, self.begun, self.arrived = 0, set(), set()

    def bind(self, n, ref):
        self.owns[n] = [ref]

    def copies(self):
        n = 0
        for job, own, far in zip(self.jobs, self.owns, self.fars):
            for stage, kind, zr, src, dst, to in job.moves(self.plan, own, far):
                yield n, job, stage, kind, zr, send(src, dst, self.sems[0].at[n], self.sems[1].at[n], to)
                n += 1

    def greet(self):
        barrier = pltpu.get_barrier_semaphore()
        for p in self.peers:
            pl.semaphore_signal(barrier, inc=1, device_id=peer(p), device_id_type=MESH)
        pl.semaphore_wait(barrier, len(self.peers))

    def start(self, stage=0):
        self.begun.add(stage)
        copies = list(self.copies())
        mine = [c for c in copies if c[2] == stage and c[3] != "p"]
        needs = [(job, k, zr) for _, job, _, kind, zr, _ in mine for k in job.before(kind)]
        for n, job, at, kind, zr, copy in copies:
            if (job, kind, zr) in needs and n not in self.arrived and at in self.begun:
                copy.wait_recv()
                self.arrived.add(n)
        for c in mine:
            c[-1].start()

    def release(self, n):
        paced = [c[-1] for c in self.copies() if c[3] == "p"]
        for copy in paced[self.released : self.released + n]:
            copy.start()
        self.released += n

    def finish(self):
        for stage in sorted({c[2] for c in self.copies()} - self.begun):
            self.start(stage)
        self.release(sum(c[3] == "p" for c in self.copies()) - self.released)
        for n, _, _, _, _, copy in self.copies():
            if n in self.arrived:
                copy.wait_send()
            else:
                copy.wait()


class Blank:
    def __init__(self):
        self.at = self

    def __getitem__(self, at):
        return self


class AllReduce:
    LEAST = 16

    def __init__(self, plan, acc, groups, tmp, small, small_tmp, sems, small_sems, credits=None):
        self.acc, self.groups, self.tmp, self.small, self.small_tmp = acc, groups, tmp, small, small_tmp
        self.sems, self.small_sems, self.credits = sems, small_sems, credits
        self.orders = [[(0, 1)] + o for o in self.rotations(plan)]
        self.steps = len(self.orders[0])
        self.spans = [[(0, acc.shape[1])] for _ in groups]

    @staticmethod
    def rotations(plan):
        def powers(n):
            return [1 << i for i in range(n.bit_length() - 1)]

        x = [(0, 2 * b) for b in powers(plan.n_expert // 2)]
        y = [(b, 0) for b in powers(plan.ny)]
        z = [(plan.ny * b, 0) for b in powers(plan.nz)]
        return [x + y + z, y + z + x, z + x + y]

    @classmethod
    def tmp_rows(cls, plan, rows):
        total = 0
        for _ in range(1 + len(cls.rotations(plan)[0])):
            rows = max(rows // 2, cls.LEAST)
            total += rows
        return total

    @classmethod
    def peers(cls, plan):
        return [(0, 1)] + cls.rotations(plan)[0]

    @staticmethod
    def side(to):
        axis, bits = ("dp", to[0]) if to[0] else ("expert", to[1])
        return lax.rem(lax.div(lax.axis_index(axis), bits), 2)

    def halves(self, g, step):
        return self.spans[g][step][1] > self.LEAST

    def place(self, g, step):
        to = self.orders[g % 3][step]
        low, length = self.spans[g][step]
        if length <= self.LEAST:
            return to, low, low, length
        half = length // 2
        side = self.side(to)
        return to, low + (1 - side) * half, low + side * half, half

    def view(self, ref, g, low, length):
        index, first, width = self.groups[g]
        if not isinstance(low, int):
            low = pl.multiple_of(low, self.LEAST)
        return ref.at[index, pl.ds(low, length), pl.ds(first, width)]

    def offset(self, g, step):
        return sum(self.place(g, n)[3] for n in range(step))

    def reduce_copy(self, g, step):
        to, sent, _, length = self.place(g, step)
        dst = self.view(self.tmp, g, self.offset(g, step), length)
        return send(self.view(self.acc, g, sent, length), dst, self.sems.at[0, g, step], self.sems.at[1, g, step], to)

    def small_copy(self, step):
        to = self.orders[0][step]
        return send(
            self.small, self.small_tmp.at[step], self.small_sems.at[0, step], self.small_sems.at[1, step], to
        )

    def reduce_start(self, step):
        for g in range(len(self.groups)):
            self.reduce_copy(g, step).start()
        if self.small is not None:
            self.small_copy(step).start()

    def reduce_finish(self, step):
        for g in range(len(self.groups)):
            self.reduce_copy(g, step).wait()
            _, _, kept, length = self.place(g, step)
            mine = self.view(self.acc, g, kept, length)
            got = self.view(self.tmp, g, self.offset(g, step), length)
            mine[...] = (mine[...].astype(F32) + got[...].astype(F32)).astype(BF16)
            if self.halves(g, step):
                pl.semaphore_signal(
                    self.credits.at[g, step],
                    inc=1,
                    device_id=peer(self.orders[g % 3][step]),
                    device_id_type=MESH,
                )
            self.spans[g].append((kept, length))
        if self.small is not None:
            self.small_copy(step).wait()
            self.small[...] = self.small[...] + self.small_tmp[step]

    def spread_copy(self, g, step):
        to = self.orders[g % 3][step]
        low, length = self.spans[g][step + 1]
        mine = self.view(self.acc, g, low, length)
        return send(mine, mine, self.sems.at[2, g, step], self.sems.at[3, g, step], to)

    def spread(self, step, action):
        for g in range(len(self.groups)):
            if self.halves(g, step):
                copy = self.spread_copy(g, step)
                if action == "start":
                    pl.semaphore_wait(self.credits.at[g, step], 1)
                    copy.start()
                else:
                    copy.wait()

    def run(self):
        for step in range(self.steps):
            self.reduce_start(step)
            yield
            self.reduce_finish(step)
        for step in reversed(range(self.steps)):
            self.spread(step, "start")
            yield
            self.spread(step, "wait")


def vmem(shape):
    return pl.BlockSpec(shape, lambda *_: (0,) * len(shape))


ANYWHERE = pl.BlockSpec(memory_space=pl.ANY)


def fused(
    plan, body, ins, outs, name, cid=None, peers=(), jobs=(), grid=None, in_specs=None, out_specs=None, scratch=(), us=10
):
    whole = (lambda shape: pl.BlockSpec(memory_space=pltpu.VMEM)) if grid is None else vmem
    in_specs = [None] * len(ins) if in_specs is None else in_specs
    out_specs = [None] * len(outs) if out_specs is None else out_specs
    in_specs = [whole(a.shape) if s is None else s for a, s in zip(ins, in_specs)]
    out_specs = [whole(o[0]) if s is None else s for o, s in zip(outs, out_specs)]
    ins, outs, scratch = list(ins), list(outs), list(scratch)
    n_in, n_out, n_scratch = len(ins), len(outs), len(scratch)
    aliases, places, count, peers = {}, [], 0, list(peers)
    for k, job in enumerate(jobs):
        place = range(len(ins), len(ins) + len(job.inputs()))
        ins += job.inputs()
        in_specs += [ANYWHERE] * len(job.inputs())
        if job.far is not None:
            aliases[len(ins)] = n_out + k
            ins.append(job.far)
            in_specs.append(ANYWHERE)
            outs.append((job.far.shape, job.far.dtype))
        else:
            outs.append((job.shape(plan), job.own.dtype))
        out_specs.append(ANYWHERE)
        places.append(place)
        blank = [Blank(), Blank()]
        count += len(list(job.moves(plan, blank, Blank())))
        peers += [p for p in dict.fromkeys(job.targets(plan)) if p not in peers]
    if jobs:
        scratch += [DMA((count,)), DMA((count,))]

    def run(*refs):
        i, o, s = refs[: len(ins)], refs[len(ins) : len(ins) + len(outs)], refs[len(ins) + len(outs) :]
        if cid is None:
            return body(*i, *o, *s)
        sems = s[n_scratch:] if jobs else (None, None)
        bg = Background(plan, jobs, [[i[n] for n in p] for p in places], o[n_out:], *sems, peers)
        body(bg, *i[:n_in], *o[:n_out], *s[:n_scratch])

    moved = sum(a.size * a.dtype.itemsize for a in ins[:n_in])
    extra = {} if grid is None else {"grid": grid}
    got = pl.pallas_call(
        run,
        out_shape=[jax.ShapeDtypeStruct(s, d) for s, d in outs],
        in_specs=in_specs,
        out_specs=out_specs,
        scratch_shapes=scratch,
        input_output_aliases=aliases,
        name=name,
        compiler_params=pltpu.CompilerParams(
            vmem_limit_bytes=VMEM_LIMIT, collective_id=cid, has_side_effects=cid is not None
        ),
        cost_estimate=pl.CostEstimate(flops=int(us * 1.15e9), bytes_accessed=moved, transcendentals=0),
        **extra,
    )(*ins)
    return got[:n_out], got[n_out:]


CHUNK = 128


def zero_half(rows, half):
    zero = jnp.zeros_like(rows)
    return jnp.concatenate([rows, zero] if half == 0 else [zero, rows], axis=0)


def half_lanes(pair, half):
    lane = lax.broadcasted_iota(jnp.int32, pair.shape, 1)
    keep = lane < HEAD_DIM if half == 0 else lane >= HEAD_DIM
    return jnp.where(keep, pair, jnp.zeros_like(pair))


def fold(values, op):
    return op(values.reshape(values.shape[0] // 8, 8, values.shape[1]), axis=0)


def masked(scores, at, ids, rows):
    me = lax.axis_index("expert")
    first = xor(me, ids[at // rows]) * rows + at % rows
    key = first + lax.broadcasted_iota(jnp.int32, scores.shape, 0)
    query = me * rows + lax.broadcasted_iota(jnp.int32, scores.shape, 1)
    return jnp.where(key <= query, scores, MASKED)


def head_pairs(pairs, body, between):
    at = 0
    for stop, act in [*between, (pairs, None)]:
        if stop > at:
            lax.fori_loop(at, stop, lambda h2, _: (body(h2), 0)[1], 0)
            at = stop
        if act is not None:
            act()


def attend_forward(q_t, k, v_t, causal, o_t, lse, scratch, between=()):
    raw, low = scratch
    length = k.shape[0]

    def body(h2):
        first = pl.multiple_of(h2 * 128, 128)
        for half in range(2):
            rows = pl.ds(pl.multiple_of(h2 * 128 + half * HEAD_DIM, HEAD_DIM), HEAD_DIM)
            query = zero_half(q_t[rows, :], half)
            top = None
            for at in range(0, length, CHUNK):
                scores = nn(k[at : at + CHUNK, pl.ds(first, 128)], query)
                if causal is not None:
                    scores = masked(scores, at, *causal)
                raw[half, at : at + CHUNK, :] = scores
                part = fold(scores, jnp.max)
                top = part if top is None else jnp.maximum(top, part)
            top = jnp.max(top, axis=0, keepdims=True)
            total = None
            for at in range(0, length, CHUNK):
                lifted = jnp.exp(raw[half, at : at + CHUNK, :] - top)
                low[half, at : at + CHUNK, :] = lifted.astype(BF16)
                part = fold(lifted, jnp.sum)
                total = part if total is None else total + part
            total = jnp.sum(total, axis=0, keepdims=True)
            o_t[rows, :] = nn(v_t[rows, :], low[half]) * (1.0 / total)
            lse[pl.ds(2 * h2 + half, 1), :] = top + jnp.log(total)

    head_pairs(k.shape[1] // 128, body, between)


def attend_backward(q, k, v, k_t, do, o_t, lse, causal, dk, dv, dq_t, scratch, between=()):
    q_t, do_t, low = scratch
    length = k.shape[0]
    q_t[...] = q[...].astype(F32).T.astype(BF16)
    do_t[...] = do[...].astype(F32).T.astype(BF16)

    def body(h2):
        first = pl.multiple_of(h2 * 128, 128)
        pair = pl.ds(first, 128)
        q_pair, do_pair = q[:, pair], do[:, pair]
        parts = []
        for half in range(2):
            rows = pl.ds(pl.multiple_of(h2 * 128 + half * HEAD_DIM, HEAD_DIM), HEAD_DIM)
            do_rows = do_t[rows, :]
            centre = jnp.sum(do_rows.astype(F32) * o_t[rows, :], axis=0, keepdims=True)
            parts.append(
                (
                    rows,
                    zero_half(q_t[rows, :], half),
                    zero_half(do_rows, half),
                    half_lanes(q_pair, half),
                    half_lanes(do_pair, half),
                    lse[pl.ds(2 * h2 + half, 1), :],
                    centre,
                )
            )
        for at in range(0, length, CHUNK):
            span = slice(at, at + CHUNK)
            dk_pair = dv_pair = None
            for half, (_, q_row, do_row, q_lane, do_lane, total, centre) in enumerate(parts):
                scores = nn(k[span, pair], q_row)
                if causal is not None:
                    scores = masked(scores, at, *causal)
                weights = jnp.exp(scores - total)
                weights_grad = nn(v[span, pair], do_row)
                scores_grad = (weights * (weights_grad - centre)).astype(BF16)
                low[half, span, :] = scores_grad
                dv_part = nn(weights.astype(BF16), do_lane)
                dk_part = nn(scores_grad, q_lane)
                dv_pair = dv_part if dv_pair is None else dv_pair + dv_part
                dk_pair = dk_part if dk_pair is None else dk_pair + dk_part
            dk[span, pair] = dk_pair.astype(BF16)
            dv[span, pair] = dv_pair.astype(BF16)
        for half in range(2):
            rows = parts[half][0]
            dq_t[rows, :] = (nn(k_t[rows, :], low[half]) * HEAD_DIM ** (-0.5)).astype(BF16)

    head_pairs(k.shape[1] // 128, body, between)


def forward_scratch(plan, rows, feature):
    length = plan.n_expert * rows
    return [
        pltpu.VMEM((feature, rows), BF16),
        pltpu.VMEM((feature, length), BF16),
        pltpu.VMEM((2, length, rows), F32),
        pltpu.VMEM((2, length, rows), BF16),
    ]


def backward_scratch(plan, rows, feature):
    length = plan.n_expert * rows
    return [
        pltpu.VMEM((length, feature), BF16),
        pltpu.VMEM((length, feature), BF16),
        pltpu.VMEM((feature, rows), BF16),
        pltpu.VMEM((rows, feature), BF16),
        pltpu.VMEM((feature, rows), BF16),
        pltpu.VMEM((feature, rows), BF16),
        pltpu.VMEM((2, length, rows), BF16),
    ]


def project_rows(hm, win, k, k_t, v, v_t):
    feature = hm.shape[1]
    w_k, w_v = win[:, feature : 2 * feature], win[:, 2 * feature :]
    k[...] = nn(hm, w_k).astype(BF16)
    v[...] = nn(hm, w_v).astype(BF16)
    k_t[...] = tt(w_k, hm).astype(BF16)
    v_t[...] = tt(w_v, hm).astype(BF16)


def project_query(rows, win):
    return nn(rows, win[:, : rows.shape[1]]).astype(BF16).astype(F32) * HEAD_DIM ** (-0.5)


def attention_shapes(plan, rows, feature):
    length = plan.n_expert * rows
    return [
        ((length, feature), BF16),
        ((feature, length), BF16),
        ((length, feature), BF16),
        ((rows, feature), BF16),
        ((feature, rows), F32),
        ((feature // HEAD_DIM, rows), F32),
    ]


def gather_rows(ids, col, returned):
    me = lax.axis_index("expert")
    total = None
    for r, rows in zip(ids, returned):
        slots = rows.shape[0] * rows.shape[1]
        local = col - xor(me, r) * slots
        hot = (local == lax.broadcasted_iota(jnp.int32, (col.shape[0], slots), 1)).astype(BF16)
        part = nn(hot, rows.reshape(slots, rows.shape[-1]))
        total = part if total is None else total + part
    return total


def fill_buffers(cap, col_of, token_of, sources, dest):
    experts = dest.shape[0]
    slots = experts * cap
    me = lax.axis_index("expert")
    for s in sources:
        for p in range(2):
            local = col_of(s, p) - me * slots
            hot = (local == lax.broadcasted_iota(jnp.int32, (slots, local.shape[1]), 0)).astype(BF16)
            rows = nn(hot, token_of(s, p)).astype(BF16)
            at = (2 * s + p) * cap
            for j in range(experts):
                dest[j, at : at + cap, :] = rows[j * cap : (j + 1) * cap]


def column(ref, s, layer, p):
    return ref[s, pl.ds(2 * layer + p, 1), :]


class Return:
    def __init__(self, ids, stage, ret, send_sems, recv_sems):
        self.ids, self.stage, self.ret, self.sems = ids, stage, ret, (send_sems, recv_sems)

    def copy(self, s, n):
        return send(
            self.stage.at[s, n], self.ret.at[s, n], self.sems[0].at[s, n], self.sems[1].at[s, n], (0, self.ids[s])
        )

    def put(self, j, rows, cap):
        for s in range(len(self.ids)):
            for p in range(2):
                at = (2 * s + p) * cap
                (self.ret if s == 0 else self.stage)[s, j, p] = rows[at : at + cap]

    def start(self, j):
        for s in range(1, len(self.ids)):
            self.copy(s, j).start()

    def finish(self, experts):
        for n in range(experts):
            for s in range(1, len(self.ids)):
                self.copy(s, n).wait()

    def rows(self, p):
        return [self.ret[s, :, p] for s in range(len(self.ids))]


def load(src, dst, sem):
    return pltpu.make_async_copy(src, dst, sem)


def self_forward(plan, source, target, cols, out_grad, gains, inward, outward, jobs):
    ids, count = plan.ids, plan.n_expert
    _, rows, feature = source.shape
    length = count * rows

    def body(bg, *refs):
        src, tgt, col, og, g, win_any, wout_any = refs[:7]
        enc, dec = refs[7:16], refs[16:25]
        u_near, og_near, col_near = refs[25:28]
        near_s, near_t, win, wout, q_t, v_t, raw, low, lsem, *sems = refs[28:]
        weights = [load(win_any.at[n], win.at[n], lsem.at[n]) for n in range(2)]
        weights += [load(wout_any.at[n], wout.at[n], lsem.at[2 + n]) for n in range(2)]
        for w in weights:
            w.start()
        g_s, g_t, g_u, g_og, g_col = [
            Gather(ids, ref, sems[2 * n], sems[2 * n + 1])
            for n, ref in enumerate((near_s, near_t, u_near, og_near, col_near))
        ]
        near_s[0] = src[0]
        near_t[0] = tgt[0]
        col_near[0] = col[...]
        og_near[0] = og[...]
        bg.greet()
        g_s.start()
        g_t.start()
        g_col.start()
        bg.start()

        def attend(near, outs, n, gain, gain_next, causal, first, between):
            after, nxt, hm, k, k_t, v, q, o_t, lse = outs
            norm_rows(near.at[0], hm.at[0:rows], g[gain : gain + 1])
            if n == 0:
                for w in weights:
                    w.wait()
            q_scaled = project_query(hm[0:rows, :], win[n])
            q[...] = q_scaled.astype(BF16)
            first()
            for b in range(1, count):
                norm_rows(near.at[b], hm.at[b * rows : (b + 1) * rows], g[gain : gain + 1])
            project_rows(hm[...], win[n], k, k_t, v, v_t)
            q_t[...] = q_scaled.T.astype(BF16)
            attend_forward(q_t, k, v_t, causal, o_t, lse, (raw, low), [(2, between)])
            merged = o_t[...].T.astype(BF16)
            after[...] = near[0].astype(F32) + nn(merged, wout[n])
            norm_rows(after, nxt, g[gain_next : gain_next + 1])

        def first_enc():
            g_s.forward()
            g_s.finish()
            g_og.start()

        def mid_enc():
            g_t.forward()
            g_col.forward()

        attend(near_s, enc, 0, 0, 1, None, first_enc, mid_enc)
        u_near[0] = enc[1][...]
        g_u.start()

        def mid_dec():
            g_u.forward()
            g_og.forward()

        attend(near_t, dec, 1, 3, 4, (ids, rows), g_t.finish, mid_dec)
        g_u.finish()
        g_og.finish()
        g_col.finish()
        bg.finish()

    shapes = [((rows, feature), F32), ((rows, feature), BF16), ((length, feature), BF16)]
    shapes += attention_shapes(plan, rows, feature)
    outs, fars = fused(
        plan,
        body,
        [source, target, cols, out_grad, gains, inward, outward],
        shapes
        + shapes
        + [
            ((count, rows, feature), BF16),
            ((count, 2, rows, feature), BF16),
            ((count,) + cols.shape, jnp.int32),
        ],
        "self_forward",
        cid=1,
        peers=expert_peers(ids),
        jobs=jobs,
        in_specs=[None] * 5 + [ANYWHERE] * 2,
        scratch=[
            pltpu.VMEM((count, rows, feature), BF16),
            pltpu.VMEM((count, rows, feature), BF16),
            pltpu.VMEM((2, feature, 3 * feature), BF16),
            pltpu.VMEM((2, feature, feature), BF16),
            *forward_scratch(plan, rows, feature),
            DMA((4,)),
        ]
        + [DMA((count,))] * 10,
        us=35,
    )
    return outs[:9], outs[9:18], outs[18:], fars


def return_scratch(plan, experts, cap, feature):
    shape = (plan.n_expert, experts, 2, cap, feature)
    return [pltpu.VMEM(shape, BF16), pltpu.VMEM(shape, BF16), DMA(shape[:2]), DMA(shape[:2])]


def expert_forward(plan, near, col_near, own_col, residual, gains, weight_up, weight_down, jobs):
    ids, count = plan.ids, plan.n_expert
    experts, hidden, feature = weight_up.shape
    rows = near.shape[1]
    cap = 2 * rows // EXPERTS
    length = count * 2 * cap

    def body(bg, u, col, mine, res, g, up, down, out, nxt, buf, act, *scratch):
        j = pl.program_id(0)
        back = Return(ids, *scratch)

        @pl.when(j == 0)
        def _():
            bg.greet()
            bg.start()
            fill_buffers(cap, lambda s, p: col[s, p : p + 1, :], lambda s, p: u[s], range(count), buf)

        for at in range(0, hidden, WIDE):
            raw = nt(buf[j], up[0, at : at + WIDE])
            for n in range(0, length, TALL):
                act[n : n + TALL, at : at + WIDE] = gelu(raw[n : n + TALL]).astype(BF16)
        back.put(j, nn(act[...], down[0]).astype(BF16), cap)
        back.start(j)

        @pl.when(j == experts - 1)
        def _():
            back.finish(experts)
            for p in range(2):
                out[p] = res[...] + gather_rows(ids, mine[p], back.rows(p))
                norm_rows(out.at[p], nxt.at[p], g[2:3])
            bg.finish()

    weight = pl.BlockSpec((1, hidden, feature), lambda j: (j, 0, 0))
    return fused(
        plan,
        body,
        [near, col_near, own_col, residual, gains, weight_up, weight_down],
        [((2, rows, feature), F32), ((2, rows, feature), BF16)],
        "expert_forward",
        cid=2,
        peers=expert_peers(ids),
        jobs=jobs,
        grid=(experts,),
        in_specs=[None] * 5 + [weight, weight],
        scratch=[pltpu.VMEM((experts, length, feature), BF16), pltpu.VMEM((length, hidden), BF16)]
        + return_scratch(plan, experts, cap, feature),
        us=22,
    )


def weight_grads(hq, hm, dq, dk, dv, o_t, d_branch):
    return [tn(hq, dq), tn(hm, dk), tn(hm, dv), nn(o_t.astype(BF16), d_branch)]


def middle(plan, hc, mid, memory, final, cols, own_col, out_grad, og_near, gains, inward, outward, up, down, jobs):
    ids, count = plan.ids, plan.n_expert
    rows, feature = hc.shape
    length = count * rows
    experts, hidden, _ = up.shape
    cap = 2 * rows // EXPERTS
    slots = count * 2 * cap
    heads = feature // HEAD_DIM

    def body(bg, *refs):
        h, t1, mem, e2, g, col, mine, og_own = refs[:8]
        og_any, win_any, wout_any, up_any, down_any = refs[8:13]
        t2_out, w_out, res_out, fg, fg_low, fg_near, dt1, dw, dg2, dg4, dg5 = refs[13:24]
        t2, w_near, result, og, hm, k, k_t, v, q, o_t, lse, q_t, v_t, raw, low, do_t = refs[24:40]
        buf, gbuf, act, slopes, wup, wdown, stage, ret, rs, rr = refs[40:50]
        dk, dv, dq, dq_t, do, parts, got, upstream, win, wout, lsem, wsem, osem = refs[50:63]
        sems = refs[63:]
        weights = [load(win_any.at[2], win, lsem.at[0]), load(wout_any.at[2], wout, lsem.at[1])]
        og_load = load(og_any, og, lsem.at[2])
        gather_m = [Gather(ids, hm.at[p], sems[p].at[0], sems[p].at[1]) for p in range(2)]
        gather_w = [Gather(ids, w_near.at[p], sems[2 + p].at[0], sems[2 + p].at[1]) for p in range(2)]
        gather_f = [Gather(ids, fg_near.at[p], sems[4 + p].at[0], sems[4 + p].at[1]) for p in range(2)]
        scatter = [Scatter(ids, parts.at[p], got.at[p], sems[6 + p].at[0], sems[6 + p].at[1]) for p in range(2)]
        back = Return(ids, stage, ret, rs, rr)
        flushes = [load(t2, t2_out, osem.at[0]), load(w_near, w_out, osem.at[1]), load(result, res_out, osem.at[2])]
        bg.bind(0, w_near)

        def fetch(j):
            return [
                load(up_any.at[j], wup.at[j % 2], wsem.at[0, j % 2]),
                load(down_any.at[j], wdown.at[j % 2], wsem.at[1, j % 2]),
            ]

        for x in weights:
            x.start()
        for p in range(2):
            hm[p, 0] = mem[p]
        bg.greet()
        gather_m[0].start()
        gather_m[1].start()
        bg.start()
        for x in weights:
            x.wait()
        for x in [og_load] + [x for j in range(min(2, experts)) for x in fetch(j)]:
            x.start()
        q_scaled = project_query(h[...], win[...])
        q[...] = q_scaled.astype(BF16)
        q_t[...] = q_scaled.T.astype(BF16)
        gather_m[0].forward()
        gather_m[0].finish()
        for p in range(2):
            project_rows(hm[p].reshape(length, feature), win[...], k.at[p], k_t.at[p], v.at[p], v_t)
            between = gather_m[1].forward if p == 0 else gather_w[0].forward
            attend_forward(q_t, k.at[p], v_t, None, o_t.at[p], lse.at[p], (raw, low), [(2, between)])
            t2[p] = t1[...] + nn(o_t[p].T.astype(BF16), wout[...])
            norm_rows(t2.at[p], w_near.at[p, 0], g[5:6])
            gather_w[p].start()
            if p == 0:
                gather_m[1].finish()
        flushes[0].start()
        og_load.wait()
        column_of = lambda s, p: col[s, 2 + p : 3 + p, :]
        fill_buffers(cap, column_of, lambda s, p: og[s, p], range(count), gbuf)
        gather_w[0].finish()
        gather_w[1].forward()
        gather_w[1].finish()
        bg.start(1)
        flushes[1].start()
        fill_buffers(cap, column_of, lambda s, p: w_near[p, s], range(count), buf)
        for j in range(experts):
            for x in fetch(j):
                x.wait()
            for at in range(0, hidden, WIDE):
                span = slice(at, at + WIDE)
                gelu_pair(
                    nt(buf[j], wup[j % 2, span]), nt(gbuf[j], wdown[j % 2, span]), act.at[:, span], slopes.at[:, span]
                )
            back.put(j, nn(slopes[...], wup[j % 2]).astype(BF16), cap)
            back.start(j)
            res = nn(act[...], wdown[j % 2]).astype(BF16)
            for s in range(count):
                for p in range(2):
                    at = (2 * s + p) * cap
                    result[s, j, p] = res[at : at + cap]
            if j + 2 < experts:
                for x in fetch(j + 2):
                    x.start()
        flushes[2].start()
        bg.start(2)
        back.finish(experts)
        total = None
        for p in range(2):
            upstream[p] = gather_rows(ids, mine[p], back.rows(p))

            def store_up(span, dx):
                upstream[p, span, :] = og_own[p, span, :] + dx

            gain = norm_back_rows(t2.at[p], g[5:6], upstream.at[p], store_up)
            total = gain if total is None else total + gain
        dg5[...] = total

        def memory_back(p):
            fg[p] = scatter[p].finish()

            def store(span, dx):
                fg[p, span, :] = dx
                fg_low[p, span, :] = dx.astype(BF16)
                fg_near[p, 0, span, :] = dx.astype(BF16)

            gain = norm_back_rows(e2.at[p], g[2:3], fg.at[p], store)
            gather_f[p].start()
            if p == 0:
                dg2[...] = gain
            else:
                dg2[...] = dg2[...] + gain

        for p in range(2):
            do[...] = nt(upstream[p].astype(BF16), wout[...]).astype(BF16)
            between = () if p == 0 else ((1, scatter[0].middle), (2, lambda: memory_back(0)), (3, lambda: bg.start(3)))
            attend_backward(
                q, k.at[p], v.at[p], k_t.at[p], do, o_t.at[p], lse.at[p], None, dk.at[p], dv.at[p], dq_t, (q_t, do_t, low), between
            )
            for b in [i for i, r in enumerate(ids) if r % 2] + [i for i, r in enumerate(ids) if r % 2 == 0]:
                span = slice(b * rows, (b + 1) * rows)
                part = nt(dk[p, span, :], win[:, feature : 2 * feature])
                part = part + nt(dv[p, span, :], win[:, 2 * feature :])
                parts[p, b] = part.astype(BF16)
            scatter[p].start()
            dq[p] = dq_t[...].astype(F32).T.astype(BF16)
        scatter[1].middle()
        gather_f[0].forward()
        grads = None
        for p in range(2):
            more = weight_grads(
                h[...], hm[p].reshape(length, feature), dq[p], dk[p], dv[p], o_t[p], upstream[p].astype(BF16)
            )
            grads = more if grads is None else [x + y for x, y in zip(grads, more)]
        for n, value in enumerate(grads):
            dw[:, n * feature : (n + 1) * feature] = value.astype(BF16)
        memory_back(1)
        dt1[...] = nt(dq[0], win[:, :feature]) + nt(dq[1], win[:, :feature])

        def store_mid(span, dx):
            dt1[span, :] = upstream[0, span, :] + upstream[1, span, :] + dx

        dg4[...] = norm_back_rows(t1, g[4:5], dt1, store_mid)
        gather_f[1].forward()
        gather_f[0].finish()
        gather_f[1].finish()
        for x in flushes:
            x.wait()
        bg.finish()

    block = (rows, feature)
    two = (2,) + block
    near = (2, count) + block
    home = (count, experts, 2, cap, feature)
    keys = (2, length, feature)
    low_vmem = lambda *shape: pltpu.VMEM(shape, BF16)
    return fused(
        plan,
        body,
        [hc, mid, memory, final, gains, cols, own_col, out_grad, og_near, inward, outward, up, down],
        [
            (two, F32),
            (near, BF16),
            (home, BF16),
            (two, F32),
            (two, BF16),
            (near, BF16),
            (block, F32),
            ((feature, 4 * feature), BF16),
            ((1, feature), F32),
            ((1, feature), F32),
            ((1, feature), F32),
        ],
        "middle",
        cid=3,
        peers=expert_peers(ids),
        jobs=jobs,
        in_specs=[None] * 8 + [ANYWHERE] * 5,
        out_specs=[ANYWHERE] * 3 + [None] * 8,
        scratch=[
            pltpu.VMEM(two, F32),
            low_vmem(*near),
            low_vmem(*home),
            low_vmem(*og_near.shape),
            low_vmem(*near),
            low_vmem(*keys),
            low_vmem(2, feature, length),
            low_vmem(*keys),
            low_vmem(*block),
            pltpu.VMEM((2, feature, rows), F32),
            pltpu.VMEM((2, heads, rows), F32),
            low_vmem(feature, rows),
            low_vmem(feature, length),
            pltpu.VMEM((2, length, rows), F32),
            low_vmem(2, length, rows),
            low_vmem(feature, rows),
            low_vmem(experts, slots, feature),
            low_vmem(experts, slots, feature),
            low_vmem(slots, hidden),
            low_vmem(slots, hidden),
            low_vmem(2, hidden, feature),
            low_vmem(2, hidden, feature),
            *return_scratch(plan, experts, cap, feature),
            low_vmem(*keys),
            low_vmem(*keys),
            low_vmem(*two),
            low_vmem(feature, rows),
            low_vmem(*block),
            low_vmem(*near),
            low_vmem(*near),
            pltpu.VMEM(two, F32),
            low_vmem(feature, 3 * feature),
            low_vmem(feature, feature),
            DMA((3,)),
            DMA((2, 2)),
            DMA((3,)),
        ]
        + [DMA((2, count))] * 8,
        us=130,
    )


def encoder_experts(plan, u_near, fg_near, col_near, own_col, attended, final_grad, gains, weight_up, weight_down, jobs):
    ids, count = plan.ids, plan.n_expert
    experts, hidden, feature = weight_up.shape
    rows = attended.shape[0]
    cap = 2 * rows // EXPERTS
    length = count * 2 * cap

    def body(bg, u, fgn, col, mine, e1, fg, g, up, down, de1, dg, buf, gbuf, slopes, *scratch):
        j = pl.program_id(0)
        back = Return(ids, *scratch)

        @pl.when(j == 0)
        def _():
            bg.greet()
            bg.start()
            fill_buffers(cap, lambda s, p: col[s, p : p + 1, :], lambda s, p: u[s], range(count), buf)
            fill_buffers(cap, lambda s, p: col[s, p : p + 1, :], lambda s, p: fgn[p, s], range(count), gbuf)

        for at in range(0, hidden, WIDE):
            span = slice(at, at + WIDE)
            gelu_pair(nt(buf[j], up[0, span]), nt(gbuf[j], down[0, span]), None, slopes.at[:, span])
        back.put(j, nn(slopes[...], up[0]).astype(BF16), cap)
        back.start(j)

        @pl.when(j == experts - 1)
        def _():
            back.finish(experts)
            de1[...] = gather_rows(ids, mine[0], back.rows(0)) + gather_rows(ids, mine[1], back.rows(1))

            def store(span, dx):
                de1[span, :] = fg[0, span, :] + fg[1, span, :] + dx

            dg[...] = norm_back_rows(e1, g[1:2], de1, store)
            bg.finish()

    weight = pl.BlockSpec((1, hidden, feature), lambda j: (j, 0, 0))
    return fused(
        plan,
        body,
        [u_near, fg_near, col_near, own_col, attended, final_grad, gains, weight_up, weight_down],
        [((rows, feature), F32), ((1, feature), F32)],
        "encoder_experts",
        cid=6,
        peers=expert_peers(ids),
        jobs=jobs,
        grid=(experts,),
        in_specs=[None] * 7 + [weight, weight],
        scratch=[pltpu.VMEM((experts, length, feature), BF16)] * 2
        + [pltpu.VMEM((length, hidden), BF16)]
        + return_scratch(plan, experts, cap, feature),
        us=30,
    )


def column_groups(n_dw, width):
    if n_dw % 3 == 0:
        return [(n, 0, width) for n in range(n_dw)]
    cut = (width // 3) // 128 * 128
    groups = []
    for n in range(n_dw):
        groups += [(n, 0, cut), (n, cut, width - 2 * cut), (n, width - cut, cut)]
    return groups


def attention_back(plan, ids, n, up, saved, win, wout, work, parts, scatter, dw, causal, between, after):
    hm, k, k_t, v, q, o_t, lse = saved
    dk, dv, dq_t, do, *rest = work
    rows, feature = q.shape
    d_branch = up[...].astype(BF16)
    do[...] = nt(d_branch, wout[...]).astype(BF16)
    attend_backward(q, k, v, k_t, do, o_t, lse, causal, dk, dv, dq_t, rest, between)
    dq = dq_t[...].astype(F32).T.astype(BF16)
    for b in [i for i, r in enumerate(ids) if r % 2] + [i for i, r in enumerate(ids) if r % 2 == 0]:
        span = slice(b * rows, (b + 1) * rows)
        part = nt(dk[span, :], win[:, feature : 2 * feature]) + nt(dv[span, :], win[:, 2 * feature :])
        if b == 0:
            part = part + nt(dq, win[:, :feature])
        parts[b] = part.astype(BF16)
    scatter.start()
    after()
    for i, value in enumerate(
        weight_grads(hm[0:rows, :], hm[...], dq, dk[...], dv[...], o_t[...], d_branch)
    ):
        dw[:, i * feature : (i + 1) * feature] = value.astype(BF16)


def input_back(up, src, gain, scatter, grad):
    grad[...] = scatter.finish()

    def store(span, dx):
        grad[span, :] = up[span, :] + dx

    return norm_back_rows(src.at[0], gain, grad, store)


def attention_scratch(plan, rows, feature):
    count = plan.n_expert
    return [
        *backward_scratch(plan, rows, feature),
        pltpu.VMEM((count, rows, feature), BF16),
        pltpu.VMEM((count, rows, feature), BF16),
        pltpu.VMEM((feature, 3 * feature), BF16),
        pltpu.VMEM((feature, feature), BF16),
    ]


def decoder_backward(plan, dec_up, target, gains, saved, inward, outward, jobs):
    ids, count = plan.ids, plan.n_expert
    _, rows, feature = target.shape

    def body(bg, *refs):
        up, src, g = refs[:3]
        saved_refs, win_any, wout_any = refs[3:10], refs[10], refs[11]
        grad, dw, dg = refs[12:15]
        *work, parts, got, win, wout, lsem, sems = refs[15:]
        weights = [load(win_any.at[1], win, lsem.at[0]), load(wout_any.at[1], wout, lsem.at[1])]
        for x in weights:
            x.start()
        bg.greet()
        bg.start()
        for x in weights:
            x.wait()
        scatter = Scatter(ids, parts, got, sems.at[0], sems.at[1])
        attention_back(
            plan, ids, 1, up, saved_refs, win, wout, work, parts, scatter, dw, (ids, rows), (), lambda: None
        )
        scatter.middle()
        bg.start(1)
        dg[...] = input_back(up, src, g[3:4], scatter, grad)
        bg.finish()

    return fused(
        plan,
        body,
        [dec_up, target, gains, *saved, inward, outward],
        [((rows, feature), F32), ((feature, 4 * feature), BF16), ((1, feature), F32)],
        "decoder_backward",
        cid=7,
        peers=expert_peers(ids),
        jobs=jobs,
        in_specs=[None] * 10 + [ANYWHERE] * 2,
        scratch=attention_scratch(plan, rows, feature) + [DMA((2,)), DMA((2, count))],
        us=28,
    )


def encoder_backward(plan, enc_up, source, gains, saved, inward, outward, sums, small, jobs):
    ids, count = plan.ids, plan.n_expert
    _, rows, feature = source.shape
    width = 4 * feature
    groups = column_groups(1, width)
    steps = 1 + len(AllReduce.rotations(plan)[0])
    n_dw = len(sums) + 1

    def body(bg, *refs):
        up, src, g, sm = refs[:4]
        saved_refs, win_any, wout_any = refs[4:11], refs[11], refs[12]
        sums_any = refs[13 : 13 + n_dw - 1]
        grad, sum_out, small_out = refs[12 + n_dw : 15 + n_dw]
        *work, parts, got, win, wout, acc, tmp, small_tmp, lsem, asem, ssem, credits, sems = refs[15 + n_dw :]
        weights = [load(win_any.at[0], win, lsem.at[0]), load(wout_any.at[0], wout, lsem.at[1])]
        firsts = [load(ref, acc.at[n], lsem.at[2 + n]) for n, ref in enumerate(sums_any)]
        for x in weights + firsts:
            x.start()
        small_out[...] = sm[...]
        bg.greet()
        bg.start()

        def reduce(n):
            return AllReduce(
                plan, acc.at[n : n + 1], groups, tmp.at[n : n + 1], None, None, asem.at[n], None, credits.at[n]
            ).run()

        for x in firsts:
            x.wait()
        runs = [reduce(n) for n in range(n_dw - 1)]

        def step(release=1):
            for run in runs:
                next(run, None)
            bg.release(release)

        step(0)
        for x in weights:
            x.wait()
        scatter = Scatter(ids, parts, got, sems.at[0], sems.at[1])
        between = ((2, step),)
        attention_back(
            plan, ids, 0, up, saved_refs, win, wout, work, parts, scatter, acc.at[n_dw - 1], None, between, step
        )
        runs.append(reduce(n_dw - 1))
        step()
        scatter.middle()
        step(1)
        small_out[0:1, :] = input_back(up, src, g[0:1], scatter, grad)
        runs.append(AllReduce(plan, acc, [], None, small_out, small_tmp, None, ssem).run())
        for _ in range(2 * steps):
            step()
        last = load(acc, sum_out, lsem.at[0])
        last.start()
        last.wait()
        bg.finish()

    peers = expert_peers(ids)
    return fused(
        plan,
        body,
        [enc_up, source, gains, small, *saved, inward, outward, *sums],
        [((rows, feature), F32), ((n_dw, feature, width), BF16), (small.shape, F32)],
        "encoder_backward",
        cid=9,
        peers=peers + [p for p in AllReduce.peers(plan) if p not in peers],
        jobs=jobs,
        in_specs=[None] * 11 + [ANYWHERE] * (2 + len(sums)),
        out_specs=[None, ANYWHERE, None],
        scratch=attention_scratch(plan, rows, feature)
        + [
            pltpu.VMEM((n_dw, feature, width), BF16),
            pltpu.VMEM((n_dw, AllReduce.tmp_rows(plan, feature), width), BF16),
            pltpu.VMEM((steps,) + small.shape, F32),
            DMA((1 + n_dw,)),
            DMA((n_dw, 4, len(groups), steps)),
            DMA((2, steps)),
            pltpu.SemaphoreType.REGULAR((n_dw, len(groups), steps)),
            DMA((2, count)),
        ],
        us=90,
    )


def column_groups(n_dw, width):
    if n_dw % 3 == 0:
        return [(n, 0, width) for n in range(n_dw)]
    cut = (width // 3) // 128 * 128
    groups = []
    for n in range(n_dw):
        groups += [(n, 0, cut), (n, cut, width - 2 * cut), (n, width - cut, cut)]
    return groups


def self_backward(plan, enc_up, dec_up, source, target, gains, enc_saved, dec_saved, inward, outward, jobs):
    ids, count = plan.ids, plan.n_expert
    _, rows, feature = source.shape
    length = count * rows

    def body(bg, *refs):
        ups, srcs, g = refs[:2], refs[2:4], refs[4]
        saved = (refs[5:12], refs[12:19])
        win_any, wout_any = refs[19:21]
        grads, dws, dgs = refs[21:23], refs[23:25], refs[25:27]
        dk, dv, dq_t, do, *work, parts, got, win, wout, lsem = refs[27:-2]
        sems = refs[-2:]
        weights = [load(win_any.at[n], win.at[n], lsem.at[n]) for n in range(2)]
        weights += [load(wout_any.at[n], wout.at[n], lsem.at[2 + n]) for n in range(2)]
        for x in weights:
            x.start()
        scatter = [Scatter(ids, parts.at[n], got.at[n], sems[n].at[0], sems[n].at[1]) for n in range(2)]

        def finish(n):
            gain = 3 * n
            grads[n][...] = scatter[n].finish()

            def store(span, dx):
                grads[n][span, :] = ups[n][span, :] + dx

            dgs[n][...] = norm_back_rows(srcs[n].at[0], g[gain : gain + 1], grads[n], store)

        bg.greet()
        bg.start()
        for x in weights:
            x.wait()
        for n in range(2):
            hm, k, k_t, v, q, o_t, lse = saved[n]
            d_branch = ups[n][...].astype(BF16)
            do[...] = nt(d_branch, wout[n]).astype(BF16)
            causal = (ids, rows) if n == 1 else None
            between = () if n == 0 else ((0, lambda: bg.start(1)), (1, scatter[0].middle), (3, lambda: finish(0)))
            attend_backward(q, k, v, k_t, do, o_t, lse, causal, dk, dv, dq_t, work, between)
            dq = dq_t[...].astype(F32).T.astype(BF16)
            for b in range(count):
                span = slice(b * rows, (b + 1) * rows)
                part = nt(dk[span, :], win[n, :, feature : 2 * feature])
                part = part + nt(dv[span, :], win[n, :, 2 * feature :])
                if b == 0:
                    part = part + nt(dq, win[n, :, :feature])
                parts[n, b] = part.astype(BF16)
            scatter[n].start()
            if n == 1:
                scatter[1].middle()
            for i, value in enumerate(
                weight_grads(hm[0:rows, :], hm[...], dq, dk[...], dv[...], o_t[...], d_branch)
            ):
                dws[n][:, i * feature : (i + 1) * feature] = value.astype(BF16)
        finish(1)
        bg.finish()

    block = (rows, feature)
    return fused(
        plan,
        body,
        [enc_up, dec_up, source, target, gains, *enc_saved, *dec_saved, inward, outward],
        [(block, F32)] * 2 + [((feature, 4 * feature), BF16)] * 2 + [((1, feature), F32)] * 2,
        "self_backward",
        cid=7,
        peers=expert_peers(ids),
        jobs=jobs,
        in_specs=[None] * 19 + [ANYWHERE] * 2,
        scratch=[
            *backward_scratch(plan, rows, feature),
            pltpu.VMEM((2, count) + block, BF16),
            pltpu.VMEM((2, count) + block, BF16),
            pltpu.VMEM((2, feature, 3 * feature), BF16),
            pltpu.VMEM((2, feature, feature), BF16),
            DMA((4,)),
        ]
        + [DMA((2, count))] * 2,
        us=40,
    )


def weight_sources(plan, layer, tokens, grads, cols):
    count = plan.n_expert

    def col_of(s, p):
        row = slice(2 * layer + p, 2 * layer + p + 1)
        return cols[0][s, row, :] if s < count else cols[1][s // count - 1, s % count, row, :]

    def token_of(s, p):
        if layer == 0:
            return tokens[0][s] if s < count else tokens[1][s // count - 1, s % count]
        return tokens[0][p, s] if s < count else tokens[1][s // count - 1, s % count, p]

    def grad_of(s, p):
        if s < count:
            return grads[0][p, s] if layer == 0 else grads[0][s, p]
        return grads[1][s // count - 1, s % count, p]

    return col_of, token_of, grad_of


def weight_products(up, down, buf, gbuf, act, slopes):
    for at in range(0, buf.shape[0], WIDE):
        span = slice(at, at + WIDE)
        gelu_pair(nt(up, buf[span, :]), nt(down, gbuf[span, :]), act.at[:, span], slopes.at[:, span])
    return nn(slopes[...], buf[...]).astype(BF16), nn(act[...], gbuf[...]).astype(BF16)


def expert_weights(plan, layer, cid, tokens, grads, cols, weight_up, weight_down, jobs, home=None):
    count, ny, nz, ids = plan.n_expert, plan.ny, plan.nz, plan.ids
    experts, hidden, feature = weight_up.shape
    rows = tokens[0].shape[-2]
    cap = 2 * rows // EXPERTS
    sources = count * nz
    length = sources * 2 * cap
    span = hidden // plan.n_dp
    block = ny * span

    def body(bg, *refs):
        cn, cf = refs[:2]
        if home is not None:
            mine, res = refs[2:4]
        big, up_any, down_any = refs[n_small : n_small + 4], refs[n_small + 4], refs[n_small + 5]
        outs = refs[n_in:]
        up_out, down_out = outs[:2]
        held, (up, down, buf, gbuf, act, slopes, lsem) = outs[n_out : n_out + 4], outs[n_out + 4 : n_out + 11]
        first = pl.multiple_of(lax.div(lax.axis_index("dp"), ny) * block, block)
        loads = [load(src, dst, lsem.at[n]) for n, (src, dst) in enumerate(zip(big, held))]
        loads.append(load(up_any.at[:, pl.ds(first, block)], up, lsem.at[4]))
        loads.append(load(down_any.at[:, pl.ds(first, block)], down, lsem.at[5]))
        for x in loads:
            x.start()
        bg.greet()
        if home is not None:
            ret, rs, rr = outs[n_out + 11 :]
            own = load(refs[n_in - 1].at[0], ret.at[0], lsem.at[6])
            own.start()
            bring = [
                send(refs[n_in - 1].at[s], ret.at[s], rs.at[s], rr.at[s], (0, ids[s])) for s in range(1, count)
            ]
            for x in bring:
                x.start()
        bg.start()
        col_of, token_of, grad_of = weight_sources(plan, layer, held[0:2], held[2:4], (cn, cf))
        for n, (reader, dest) in enumerate(((token_of, buf), (grad_of, gbuf))):
            loads[2 * n].wait()
            fill_buffers(cap, col_of, reader, range(count), dest)
            loads[2 * n + 1].wait()
            fill_buffers(cap, col_of, reader, range(count, sources), dest)
        loads[4].wait()
        loads[5].wait()
        y = lax.rem(lax.axis_index("dp"), ny)
        for r in reversed(range(ny)):
            at = pl.ds(pl.multiple_of(xor(y, r) * span, span), span)

            def product(j, _):
                up_out[r, j], down_out[r, j] = weight_products(
                    up[j, at, :], down[j, at, :], buf.at[j], gbuf.at[j], act, slopes
                )
                return 0

            lax.fori_loop(0, experts, product, 0)
        if home is not None:
            own.wait()
            for x in bring:
                x.wait()
            for p in range(2):
                mixed = gather_rows(ids, mine[p], [ret[s, :, p] for s in range(count)])
                outs[2][p] = (res[p] + mixed).astype(BF16)
        bg.finish()

    small = [*cols] + ([] if home is None else [home[1], home[2]])
    n_small = len(small)
    big = [tokens[0], tokens[1], grads[0], grads[1], weight_up, weight_down] + ([] if home is None else [home[0]])
    n_in = n_small + len(big)
    outs = [((ny, experts, span, feature), BF16)] * 2 + ([] if home is None else [((2, rows, feature), BF16)])
    n_out = len(outs)
    scratch = [pltpu.VMEM(a.shape, BF16) for a in big[:4]] + [
        pltpu.VMEM((experts, block, feature), BF16),
        pltpu.VMEM((experts, block, feature), BF16),
        pltpu.VMEM((experts, length, feature), BF16),
        pltpu.VMEM((experts, length, feature), BF16),
        pltpu.VMEM((span, length), BF16),
        pltpu.VMEM((span, length), BF16),
        DMA((7,)),
    ]
    if home is not None:
        scratch += [pltpu.VMEM(home[0].shape, BF16), DMA((count,)), DMA((count,))]
    return fused(
        plan,
        body,
        small + big,
        outs,
        ("encoder", "decoder")[layer] + "_weights",
        cid=cid,
        peers=[] if home is None else expert_peers(ids),
        jobs=jobs,
        in_specs=[None] * n_small + [ANYWHERE] * len(big),
        scratch=scratch,
        us=25,
    )


def finish(plan, sums, dec, dec_got, enc, enc_got):
    n_dw, feature, width = sums.shape
    _, experts, span, _ = enc[0].shape
    part = feature // experts
    ny = plan.ny

    def body(s, du, dd, dug, ddg, eu, ed, eug, edg, a_in, a_out, eu_out, ed_out, du_out, dd_out):
        for n in range(n_dw):
            a_in[n] = s[n_dw - 1 - n, :, : 3 * feature].astype(F32)
            a_out[n] = s[n_dw - 1 - n, :, 3 * feature :].astype(F32)
        for out, own, others in (
            (eu_out, eu[0, 0], [eug[r, 0] for r in range(ny - 1)]),
            (ed_out, ed[0, 0], [edg[r, 0] for r in range(ny - 1)]),
            (du_out, du[0, 0], [dug[r, 0] for r in range(ny - 1)]),
            (dd_out, dd[0, 0], [ddg[r, 0] for r in range(ny - 1)]),
        ):
            total = own.astype(F32)
            for other in others:
                total = total + other.astype(F32)
            out[0] = total

    block = (1, span, feature)
    first = pl.BlockSpec((1,) + block, lambda j: (0, j, 0, 0))
    others = pl.BlockSpec((ny - 1,) + block, lambda j: (0, j, 0, 0))
    own = pl.BlockSpec(block, lambda j: (j, 0, 0))
    return fused(
        plan,
        body,
        [sums, *dec, *dec_got, *enc, *enc_got],
        [((n_dw, feature, 3 * feature), F32), ((n_dw, feature, feature), F32)] + [((experts, span, feature), F32)] * 4,
        "finish",
        grid=(experts,),
        in_specs=[
            pl.BlockSpec((n_dw, part, width), lambda j: (0, j, 0)),
            first,
            first,
            others,
            others,
            first,
            first,
            others,
            others,
        ],
        out_specs=[
            pl.BlockSpec((n_dw, part, 3 * feature), lambda j: (0, j, 0)),
            pl.BlockSpec((n_dw, part, feature), lambda j: (0, j, 0)),
        ]
        + [own] * 4,
        us=10,
    )[0]


def local(
    plan,
    source,
    target,
    attention_in,
    attention_out,
    gains,
    encoder_up,
    encoder_down,
    decoder_up,
    decoder_down,
    encoder_route,
    encoder_slot,
    decoder_route,
    decoder_slot,
    output_grad,
):
    _, rows, feature = source.shape
    cap = 2 * rows // EXPERTS
    zr = plan.zr
    za, zb, zc = zr[0::3], zr[1::3], zr[2::3]
    weights = (attention_in, attention_out)

    cols = jnp.stack([encoder_route * cap + encoder_slot, decoder_route * cap + decoder_slot]).reshape(4, rows)
    own_cols = cols.reshape(2, 2, rows, 1)
    out_grad = output_grad.reshape(2, rows, feature)
    og = out_grad.astype(BF16)

    counts = jnp.sum(
        (
            jnp.stack([encoder_route, decoder_route]).reshape(4, rows, 1) == jnp.arange(EXPERTS, dtype=jnp.int32)
        ).astype(F32),
        axis=1,
    )

    enc, dec, (u_near, og_near, col_near), (col_far, og_far) = self_forward(
        plan, source, target, cols, og, gains, *weights, [Job(cols, None, z=zr), Job(og, None, z=za + zb)]
    )
    e1, u, *enc_saved = enc
    t1, hc, *dec_saved = dec
    (e2, memory), (col_far, og_far) = expert_forward(
        plan,
        u_near,
        col_near,
        own_cols[0],
        e1,
        gains,
        encoder_up,
        encoder_down,
        [Job(None, col_far, x=zr), Job(og, og_far, z=zc)],
    )
    (t2, w_near, result, fg, fg_low, fg_near, dt1, cross_dw, dg2, dg4, dg5), (w_far, col_far, og_far, u_far) = middle(
        plan,
        hc,
        t1,
        memory,
        e2,
        col_near,
        own_cols[1],
        out_grad,
        og_near,
        gains,
        *weights,
        decoder_up,
        decoder_down,
        [
            Job(og, None, later=[(1, "z", zc + za + zb), (1, "s", za + zb), (3, "x", zc)], by_pass=True, local=True),
            Job(None, col_far, c=zr),
            Job(None, og_far, s=za + zb, near=og_near, later=[(1, "c", za + zb), (2, "x", zc)]),
            Job(u, None, z=zr),
        ],
    )
    (de1, dg1), (w_far, og_far, fg_far) = encoder_experts(
        plan,
        u_near,
        fg_near,
        col_near,
        own_cols[0],
        e1,
        fg,
        gains,
        encoder_up,
        encoder_down,
        [Job(None, w_far, c=zr), Job(None, og_far, c=zc), Job(fg_low, None, z=za + zb)],
    )
    dec_g, (fg_far,) = expert_weights(
        plan,
        1,
        8,
        (w_near, w_far),
        (og_near, og_far),
        (col_near, col_far),
        decoder_up,
        decoder_down,
        [Job(fg_low, fg_far, z=zc, x=za + zb)],
    )
    (target_grad, dec_dw, dg3), (fg_far, u_far, up_got) = decoder_backward(
        plan,
        dt1,
        target,
        gains,
        dec_saved,
        *weights,
        [
            Job(None, fg_far, x=zc, c=za + zb, later=[(1, "c", zc)]),
            Job(None, u_far, s=zr, near=u_near, later=[(1, "c", zr)]),
            Swap(dec_g[0]),
        ],
    )
    (*enc_g, decoder_output), (down_got,) = expert_weights(
        plan,
        0,
        10,
        (u_near, u_far),
        (fg_near, fg_far),
        (col_near, col_far),
        encoder_up,
        encoder_down,
        [Swap(dec_g[1])],
        (result, own_cols[1], t2),
    )
    count_row = jnp.pad(counts.reshape(1, -1), ((0, 1), (0, feature - counts.size)))
    small = jnp.concatenate([jnp.zeros_like(dg1), dg1, dg2, dg3, dg4, dg5, count_row], axis=0)
    (source_grad, sums, small), enc_got = encoder_backward(
        plan,
        de1,
        source,
        gains,
        enc_saved,
        *weights,
        [cross_dw, dec_dw],
        small,
        [Swap(enc_g[0], paced=True), Swap(enc_g[1], paced=True)],
    )
    a_in, a_out, enc_up_g, enc_down_g, dec_up_g, dec_down_g = finish(
        plan, sums, dec_g, (up_got, down_got), enc_g, enc_got
    )
    return (
        decoder_output.reshape(2, 1, rows, feature),
        source_grad[None],
        target_grad[None],
        a_in,
        a_out,
        small[:6],
        enc_up_g,
        enc_down_g,
        dec_up_g,
        dec_down_g,
        small[6, : counts.size].reshape(2, 2, EXPERTS).astype(jnp.int32),
    )


def solution(mesh):
    plan = Plan(mesh.shape["dp"], mesh.shape["expert"])
    in_specs = (
        P("dp", "expert", None),
        P("dp", "expert", None),
        P(),
        P(),
        P(),
        P("expert", None, None),
        P("expert", None, None),
        P("expert", None, None),
        P("expert", None, None),
        P(None, "dp", "expert"),
        P(None, "dp", "expert"),
        P(None, "dp", "expert"),
        P(None, "dp", "expert"),
        P(None, "dp", "expert", None),
    )
    out_specs = (
        P(None, "dp", "expert", None),
        P("dp", "expert", None),
        P("dp", "expert", None),
        P(),
        P(),
        P(),
        P("expert", "dp", None),
        P("expert", "dp", None),
        P("expert", "dp", None),
        P("expert", "dp", None),
        P(),
    )
    return jax.shard_map(
        functools.partial(local, plan),
        mesh=mesh,
        in_specs=in_specs,
        out_specs=out_specs,
        check_vma=False,
    )
```

```python
import functools

import jax
import jax.numpy as jnp
from jax import lax
from jax.experimental import pallas as pl
from jax.experimental.pallas import tpu as pltpu
from jax.sharding import PartitionSpec as P

HEAD_DIM = 64
EXPERTS = 16
NORM_EPSILON = 1e-05
MASKED = -1e30
F32 = jnp.float32
BF16 = jnp.bfloat16
VMEM_LIMIT = 60 << 20
MESH = pl.DeviceIdType.MESH
DMA = pltpu.SemaphoreType.DMA


def nn(a, b):
    return jnp.dot(a, b, preferred_element_type=F32)


def nt(a, b):
    return lax.dot_general(a, b, (((1,), (1,)), ((), ())), preferred_element_type=F32)


def tn(a, b):
    return lax.dot_general(a, b, (((0,), (0,)), ((), ())), preferred_element_type=F32)


def tt(a, b):
    return lax.dot_general(a, b, (((0,), (1,)), ((), ())), preferred_element_type=F32)


def norm_parts(x):
    mean = jnp.mean(x, axis=-1, keepdims=True)
    centered = x - mean
    spread = jnp.mean(centered * centered, axis=-1, keepdims=True)
    scale = lax.rsqrt(spread + NORM_EPSILON)
    return centered * scale, scale


def norm(x, gain):
    return norm_parts(x)[0] * gain


def norm_back(x, gain, grad):
    hat, scale = norm_parts(x)
    inner = grad * gain
    dx = scale * (
        inner
        - jnp.mean(inner, axis=-1, keepdims=True)
        - hat * jnp.mean(inner * hat, axis=-1, keepdims=True)
    )
    return dx, jnp.sum(grad * hat, axis=0, keepdims=True)


NORM_ROWS = 64


def norm_rows(src, dst, gain):
    for at in range(0, src.shape[0], NORM_ROWS):
        span = slice(at, at + NORM_ROWS)
        dst[span, :] = norm(src[span, :].astype(F32), gain).astype(dst.dtype)


def norm_back_rows(x, gain, grad, store):
    total = None
    for at in range(0, x.shape[0], NORM_ROWS):
        span = slice(at, at + NORM_ROWS)
        dx, part = norm_back(x[span, :].astype(F32), gain, grad[span, :].astype(F32))
        store(span, dx)
        total = part if total is None else total + part
    return total


GELU_A = 0.7978845608028654
GELU_B = 0.044715


def gelu(x):
    return 0.5 * x * (1.0 + jnp.tanh(x * (GELU_A + (GELU_A * GELU_B) * (x * x))))


def gelu_both(x):
    sq = x * x
    th = jnp.tanh(x * (GELU_A + (GELU_A * GELU_B) * sq))
    half = 0.5 * (1.0 + th)
    slope = half + (0.5 * x) * (1.0 - th * th) * (GELU_A + (3.0 * GELU_A * GELU_B) * sq)
    return x * half, slope


WIDE = 256
TALL = 64


def gelu_pair(raw, grad, act, slopes):
    for at in range(0, raw.shape[0], TALL):
        span = slice(at, at + TALL)
        value, slope = gelu_both(raw[span])
        if act is not None:
            act[span, :] = value.astype(BF16)
        slopes[span, :] = (slope * grad[span]).astype(BF16)


def xor(value, bits):
    b = 1
    while b <= bits:
        if bits & b:
            value = value + b * (1 - 2 * lax.rem(lax.div(value, b), 2))
        b *= 2
    return value


def peer(to):
    return (xor(lax.axis_index("dp"), to[0]), xor(lax.axis_index("expert"), to[1]))


def send(src, dst, send_sem, recv_sem, to):
    return pltpu.make_async_remote_copy(
        src_ref=src, dst_ref=dst, send_sem=send_sem, recv_sem=recv_sem, device_id=peer(to), device_id_type=MESH
    )


def expert_peers(ids):
    return [(0, r) for r in ids[1:]]


class Gather:
    def __init__(self, ids, near, send_sems, recv_sems):
        self.pos = {r: i for i, r in enumerate(ids)}
        self.far = [r for r in ids if r % 2 == 0 and r > 0]
        self.near, self.sems = near, (send_sems, recv_sems)

    def copy(self, r, src, to):
        at = self.pos[r]
        return send(src, self.near.at[at], self.sems[0].at[at], self.sems[1].at[at], (0, to))

    def first(self, r):
        return self.copy(r, self.near.at[0], r)

    def second(self, r):
        return self.copy(r ^ 1, self.near.at[self.pos[r]], 1)

    def start(self):
        for r in self.far:
            self.first(r).start()
        self.first(1).start()

    def forward(self):
        for r in self.far:
            self.first(r).wait_recv()
            self.second(r).start()

    def finish(self):
        for r in self.far:
            self.second(r).wait_recv()
        self.first(1).wait_recv()
        for r in self.far:
            self.first(r).wait_send()
            self.second(r).wait_send()
        self.first(1).wait_send()


class Scatter:
    def __init__(self, ids, parts, got, send_sems, recv_sems):
        self.pos = {r: i for i, r in enumerate(ids)}
        self.odd = [r for r in ids if r % 2]
        self.even = [r for r in ids if r % 2 == 0]
        self.parts, self.got, self.sems = parts, got, (send_sems, recv_sems)

    def copy(self, r, to):
        at = self.pos[r]
        return send(
            self.parts.at[at], self.got.at[self.pos[r ^ 1]], self.sems[0].at[at], self.sems[1].at[at], (0, to)
        )

    def start(self):
        for r in self.odd:
            self.copy(r, 1).start()

    def middle(self):
        for r in self.odd:
            self.copy(r, 1).wait_recv()
        for r in self.even[1:]:
            at = self.pos[r]
            self.parts[at] = (self.parts[at].astype(F32) + self.got[at].astype(F32)).astype(BF16)
            self.copy(r, r).start()

    def finish(self):
        total = self.parts[0].astype(F32) + self.got[0].astype(F32)
        for r in self.even[1:]:
            self.copy(r, r).wait_recv()
            total = total + self.got[self.pos[r ^ 1]].astype(F32)
        for r in self.odd:
            self.copy(r, 1).wait_send()
        for r in self.even[1:]:
            self.copy(r, r).wait_send()
        return total


class Job:
    def __init__(self, own, far, z=(), x=(), c=(), s=(), later=(), near=None, by_pass=False, local=False):
        self.own, self.far, self.near, self.by_pass, self.local = own, far, near, by_pass, local
        self.todo = [(0, "z", z), (0, "s", s), (0, "x", x), (0, "c", c), *later]

    def has(self, kind):
        return any(k == kind and len(zrs) > 0 for _, k, zrs in self.todo)

    def inputs(self):
        if self.local:
            return []
        return ([self.own] if self.has("z") else []) + ([self.near] if self.has("s") else [])

    def shape(self, plan):
        return (plan.nz - 1, plan.n_expert) + self.own.shape

    def moves(self, plan, refs, far):
        for stage, kind, zrs in self.todo:
            for zr in zrs:
                z = (zr * plan.ny, 0)
                if kind == "z" and not self.local:
                    yield stage, kind, zr, refs[0], far.at[zr - 1, 0], z
                elif kind in "zs":
                    for r in [0] if kind == "z" else plan.across:
                        at = plan.pos[r]
                        if self.by_pass:
                            for p in range(2):
                                yield stage, kind, zr, refs[-1].at[p, at], far.at[zr - 1, at, p], z
                        else:
                            yield stage, kind, zr, refs[-1].at[at], far.at[zr - 1, at], z
                elif kind == "x":
                    for r in plan.across:
                        yield stage, kind, zr, far.at[zr - 1, 0], far.at[zr - 1, plan.pos[r]], (0, r)
                else:
                    for r in [0] + plan.across:
                        yield stage, kind, zr, far.at[zr - 1, plan.pos[r]], far.at[zr - 1, plan.pos[r ^ 1]], (0, 1)

    def before(self, kind):
        return {"x": "z", "c": "zsx"}.get(kind, "")

    def targets(self, plan):
        return (
            [(zr * plan.ny, 0) for _, kind, zrs in self.todo if kind in "zs" for zr in zrs]
            + ([(0, r) for r in plan.across] if self.has("x") else [])
            + ([(0, 1)] if self.has("c") else [])
        )


class Swap:
    def __init__(self, own, paced=False):
        self.own, self.far, self.paced = own, None, paced

    def inputs(self):
        return [self.own]

    def shape(self, plan):
        return (plan.ny - 1,) + self.own.shape[1:]

    def moves(self, plan, refs, far):
        for r in range(1, plan.ny):
            for j in range(self.own.shape[1]):
                yield 0, "p" if self.paced else "y", r, refs[0].at[r, j], far.at[r - 1, j], (r, 0)

    def before(self, kind):
        return ""

    def targets(self, plan):
        return [(r, 0) for r in range(1, plan.ny)]


class Plan:
    def __init__(self, n_dp, n_expert):
        self.n_dp, self.n_expert = n_dp, n_expert
        self.ny = 2 if n_dp <= 8 else 4
        self.nz = n_dp // self.ny
        ids, bit = [0], n_expert // 2
        while bit >= 1:
            ids = ids + [i ^ bit for i in ids]
            bit //= 2
        self.ids = ids
        self.pos = {r: i for i, r in enumerate(ids)}
        self.across = [r for r in ids if r % 2 == 0 and r > 0]
        self.zr = list(range(1, self.nz))


class Background:
    def __init__(self, plan, jobs, owns, fars, send_sems, recv_sems, peers):
        self.plan, self.jobs, self.peers = plan, jobs, peers
        self.owns, self.fars, self.sems = owns, fars, (send_sems, recv_sems)
        self.released, self.begun, self.arrived = 0, set(), set()

    def bind(self, n, ref):
        self.owns[n] = [ref]

    def copies(self):
        n = 0
        for job, own, far in zip(self.jobs, self.owns, self.fars):
            for stage, kind, zr, src, dst, to in job.moves(self.plan, own, far):
                yield n, job, stage, kind, zr, send(src, dst, self.sems[0].at[n], self.sems[1].at[n], to)
                n += 1

    def greet(self):
        barrier = pltpu.get_barrier_semaphore()
        for p in self.peers:
            pl.semaphore_signal(barrier, inc=1, device_id=peer(p), device_id_type=MESH)
        pl.semaphore_wait(barrier, len(self.peers))

    def start(self, stage=0):
        self.begun.add(stage)
        copies = list(self.copies())
        mine = [c for c in copies if c[2] == stage and c[3] != "p"]
        needs = [(job, k, zr) for _, job, _, kind, zr, _ in mine for k in job.before(kind)]
        for n, job, at, kind, zr, copy in copies:
            if (job, kind, zr) in needs and n not in self.arrived and at in self.begun:
                copy.wait_recv()
                self.arrived.add(n)
        for c in mine:
            c[-1].start()

    def paced(self):
        return sum(c[3] == "p" for c in self.copies())

    def release(self, n):
        paced = [c[-1] for c in self.copies() if c[3] == "p"]
        for copy in paced[self.released : self.released + n]:
            copy.start()
        self.released += n

    def finish(self):
        for stage in sorted({c[2] for c in self.copies()} - self.begun):
            self.start(stage)
        self.release(sum(c[3] == "p" for c in self.copies()) - self.released)
        for n, _, _, _, _, copy in self.copies():
            if n in self.arrived:
                copy.wait_send()
            else:
                copy.wait()


class Blank:
    def __init__(self):
        self.at = self

    def __getitem__(self, at):
        return self


class AllReduce:
    LEAST = 16

    def __init__(self, plan, acc, groups, tmp, small, small_tmp, sems, small_sems, credits=None):
        self.acc, self.groups, self.tmp, self.small, self.small_tmp = acc, groups, tmp, small, small_tmp
        self.sems, self.small_sems, self.credits = sems, small_sems, credits
        self.orders = [[(0, 1)] + o for o in self.rotations(plan)]
        self.steps = len(self.orders[0])
        self.spans = [[(0, acc.shape[1])] for _ in groups]

    @staticmethod
    def rotations(plan):
        def powers(n):
            return [1 << i for i in range(n.bit_length() - 1)]

        x = [(0, 2 * b) for b in powers(plan.n_expert // 2)]
        y = [(b, 0) for b in powers(plan.ny)]
        z = [(plan.ny * b, 0) for b in powers(plan.nz)]
        return [x + z + y, z + x + y, y + z + x]

    @classmethod
    def tmp_rows(cls, plan, rows):
        total = 0
        for _ in range(1 + len(cls.rotations(plan)[0])):
            rows = max(rows // 2, cls.LEAST)
            total += rows
        return total

    @classmethod
    def peers(cls, plan):
        return [(0, 1)] + cls.rotations(plan)[0]

    @staticmethod
    def side(to):
        axis, bits = ("dp", to[0]) if to[0] else ("expert", to[1])
        return lax.rem(lax.div(lax.axis_index(axis), bits), 2)

    def halves(self, g, step):
        return self.spans[g][step][1] > self.LEAST

    def place(self, g, step):
        to = self.orders[g % 3][step]
        low, length = self.spans[g][step]
        if length <= self.LEAST:
            return to, low, low, length
        half = length // 2
        side = self.side(to)
        return to, low + (1 - side) * half, low + side * half, half

    def view(self, ref, g, low, length):
        index, first, width = self.groups[g]
        if not isinstance(low, int):
            low = pl.multiple_of(low, self.LEAST)
        return ref.at[index, pl.ds(low, length), pl.ds(first, width)]

    def offset(self, g, step):
        return sum(self.place(g, n)[3] for n in range(step))

    def reduce_copy(self, g, step):
        to, sent, _, length = self.place(g, step)
        dst = self.view(self.tmp, g, self.offset(g, step), length)
        return send(self.view(self.acc, g, sent, length), dst, self.sems.at[0, g, step], self.sems.at[1, g, step], to)

    def small_copy(self, step):
        to = self.orders[0][step]
        return send(
            self.small, self.small_tmp.at[step], self.small_sems.at[0, step], self.small_sems.at[1, step], to
        )

    def reduce_start(self, step):
        for g in range(len(self.groups)):
            self.reduce_copy(g, step).start()
        if self.small is not None:
            self.small_copy(step).start()

    def reduce_finish(self, step):
        for g in range(len(self.groups)):
            self.reduce_copy(g, step).wait()
            _, _, kept, length = self.place(g, step)
            mine = self.view(self.acc, g, kept, length)
            got = self.view(self.tmp, g, self.offset(g, step), length)
            mine[...] = (mine[...].astype(F32) + got[...].astype(F32)).astype(BF16)
            if self.halves(g, step):
                pl.semaphore_signal(
                    self.credits.at[g, step],
                    inc=1,
                    device_id=peer(self.orders[g % 3][step]),
                    device_id_type=MESH,
                )
            self.spans[g].append((kept, length))
        if self.small is not None:
            self.small_copy(step).wait()
            self.small[...] = self.small[...] + self.small_tmp[step]

    def spread_copy(self, g, step):
        to = self.orders[g % 3][step]
        low, length = self.spans[g][step + 1]
        mine = self.view(self.acc, g, low, length)
        return send(mine, mine, self.sems.at[2, g, step], self.sems.at[3, g, step], to)

    def spread(self, step, action):
        for g in range(len(self.groups)):
            if self.halves(g, step):
                copy = self.spread_copy(g, step)
                if action == "start":
                    pl.semaphore_wait(self.credits.at[g, step], 1)
                    copy.start()
                else:
                    copy.wait()

    def run(self):
        for step in range(self.steps):
            self.reduce_start(step)
            yield
            self.reduce_finish(step)
        for step in reversed(range(self.steps)):
            self.spread(step, "start")
            yield
            self.spread(step, "wait")


def vmem(shape):
    return pl.BlockSpec(shape, lambda *_: (0,) * len(shape))


ANYWHERE = pl.BlockSpec(memory_space=pl.ANY)


def fused(
    plan, body, ins, outs, name, cid=None, peers=(), jobs=(), grid=None, in_specs=None, out_specs=None, scratch=(), us=10
):
    whole = (lambda shape: pl.BlockSpec(memory_space=pltpu.VMEM)) if grid is None else vmem
    in_specs = [None] * len(ins) if in_specs is None else in_specs
    out_specs = [None] * len(outs) if out_specs is None else out_specs
    in_specs = [whole(a.shape) if s is None else s for a, s in zip(ins, in_specs)]
    out_specs = [whole(o[0]) if s is None else s for o, s in zip(outs, out_specs)]
    ins, outs, scratch = list(ins), list(outs), list(scratch)
    n_in, n_out, n_scratch = len(ins), len(outs), len(scratch)
    aliases, places, count, peers = {}, [], 0, list(peers)
    for k, job in enumerate(jobs):
        place = range(len(ins), len(ins) + len(job.inputs()))
        ins += job.inputs()
        in_specs += [ANYWHERE] * len(job.inputs())
        if job.far is not None:
            aliases[len(ins)] = n_out + k
            ins.append(job.far)
            in_specs.append(ANYWHERE)
            outs.append((job.far.shape, job.far.dtype))
        else:
            outs.append((job.shape(plan), job.own.dtype))
        out_specs.append(ANYWHERE)
        places.append(place)
        blank = [Blank(), Blank()]
        count += len(list(job.moves(plan, blank, Blank())))
        peers += [p for p in dict.fromkeys(job.targets(plan)) if p not in peers]
    if jobs:
        scratch += [DMA((count,)), DMA((count,))]

    def run(*refs):
        i, o, s = refs[: len(ins)], refs[len(ins) : len(ins) + len(outs)], refs[len(ins) + len(outs) :]
        if cid is None:
            return body(*i, *o, *s)
        sems = s[n_scratch:] if jobs else (None, None)
        bg = Background(plan, jobs, [[i[n] for n in p] for p in places], o[n_out:], *sems, peers)
        body(bg, *i[:n_in], *o[:n_out], *s[:n_scratch])

    moved = sum(a.size * a.dtype.itemsize for a in ins[:n_in])
    extra = {} if grid is None else {"grid": grid}
    got = pl.pallas_call(
        run,
        out_shape=[jax.ShapeDtypeStruct(s, d) for s, d in outs],
        in_specs=in_specs,
        out_specs=out_specs,
        scratch_shapes=scratch,
        input_output_aliases=aliases,
        name=name,
        compiler_params=pltpu.CompilerParams(
            vmem_limit_bytes=VMEM_LIMIT, collective_id=cid, has_side_effects=cid is not None
        ),
        cost_estimate=pl.CostEstimate(flops=int(us * 1.15e9), bytes_accessed=moved, transcendentals=0),
        **extra,
    )(*ins)
    return got[:n_out], got[n_out:]


CHUNK = 128


def zero_half(rows, half):
    zero = jnp.zeros_like(rows)
    return jnp.concatenate([rows, zero] if half == 0 else [zero, rows], axis=0)


def half_lanes(pair, half):
    lane = lax.broadcasted_iota(jnp.int32, pair.shape, 1)
    keep = lane < HEAD_DIM if half == 0 else lane >= HEAD_DIM
    return jnp.where(keep, pair, jnp.zeros_like(pair))


def fold(values, op):
    return op(values.reshape(values.shape[0] // 8, 8, values.shape[1]), axis=0)


def masked(scores, at, ids, rows):
    me = lax.axis_index("expert")
    first = xor(me, ids[at // rows]) * rows + at % rows
    key = first + lax.broadcasted_iota(jnp.int32, scores.shape, 0)
    query = me * rows + lax.broadcasted_iota(jnp.int32, scores.shape, 1)
    return jnp.where(key <= query, scores, MASKED)


def head_pairs(pairs, body, between):
    at = 0
    for stop, act in [*between, (pairs, None)]:
        if stop > at:
            lax.fori_loop(at, stop, lambda h2, _: (body(h2), 0)[1], 0)
            at = stop
        if act is not None:
            act()


def attend_forward(q_t, k, v_t, causal, o_t, lse, scratch, between=()):
    raw, low = scratch
    length = k.shape[0]

    def body(h2):
        first = pl.multiple_of(h2 * 128, 128)
        for half in range(2):
            rows = pl.ds(pl.multiple_of(h2 * 128 + half * HEAD_DIM, HEAD_DIM), HEAD_DIM)
            query = zero_half(q_t[rows, :], half)
            top = None
            for at in range(0, length, CHUNK):
                scores = nn(k[at : at + CHUNK, pl.ds(first, 128)], query)
                if causal is not None:
                    scores = masked(scores, at, *causal)
                raw[half, at : at + CHUNK, :] = scores
                part = fold(scores, jnp.max)
                top = part if top is None else jnp.maximum(top, part)
            top = jnp.max(top, axis=0, keepdims=True)
            total = None
            for at in range(0, length, CHUNK):
                lifted = jnp.exp(raw[half, at : at + CHUNK, :] - top)
                low[half, at : at + CHUNK, :] = lifted.astype(BF16)
                part = fold(lifted, jnp.sum)
                total = part if total is None else total + part
            total = jnp.sum(total, axis=0, keepdims=True)
            o_t[rows, :] = nn(v_t[rows, :], low[half]) * (1.0 / total)
            lse[pl.ds(2 * h2 + half, 1), :] = top + jnp.log(total)

    head_pairs(k.shape[1] // 128, body, between)


def attend_backward(q, k, v, k_t, do, o_t, lse, causal, dk, dv, dq_t, scratch, between=()):
    q_t, do_t, low = scratch
    length = k.shape[0]
    q_t[...] = q[...].astype(F32).T.astype(BF16)
    do_t[...] = do[...].astype(F32).T.astype(BF16)

    def body(h2):
        first = pl.multiple_of(h2 * 128, 128)
        pair = pl.ds(first, 128)
        q_pair, do_pair = q[:, pair], do[:, pair]
        parts = []
        for half in range(2):
            rows = pl.ds(pl.multiple_of(h2 * 128 + half * HEAD_DIM, HEAD_DIM), HEAD_DIM)
            do_rows = do_t[rows, :]
            centre = jnp.sum(do_rows.astype(F32) * o_t[rows, :], axis=0, keepdims=True)
            parts.append(
                (
                    rows,
                    zero_half(q_t[rows, :], half),
                    zero_half(do_rows, half),
                    half_lanes(q_pair, half),
                    half_lanes(do_pair, half),
                    lse[pl.ds(2 * h2 + half, 1), :],
                    centre,
                )
            )
        for at in range(0, length, CHUNK):
            span = slice(at, at + CHUNK)
            dk_pair = dv_pair = None
            for half, (_, q_row, do_row, q_lane, do_lane, total, centre) in enumerate(parts):
                scores = nn(k[span, pair], q_row)
                if causal is not None:
                    scores = masked(scores, at, *causal)
                weights = jnp.exp(scores - total)
                weights_grad = nn(v[span, pair], do_row)
                scores_grad = (weights * (weights_grad - centre)).astype(BF16)
                low[half, span, :] = scores_grad
                dv_part = nn(weights.astype(BF16), do_lane)
                dk_part = nn(scores_grad, q_lane)
                dv_pair = dv_part if dv_pair is None else dv_pair + dv_part
                dk_pair = dk_part if dk_pair is None else dk_pair + dk_part
            dk[span, pair] = dk_pair.astype(BF16)
            dv[span, pair] = dv_pair.astype(BF16)
        for half in range(2):
            rows = parts[half][0]
            dq_t[rows, :] = (nn(k_t[rows, :], low[half]) * HEAD_DIM ** (-0.5)).astype(BF16)

    head_pairs(k.shape[1] // 128, body, between)


def forward_scratch(plan, rows, feature):
    length = plan.n_expert * rows
    return [
        pltpu.VMEM((feature, rows), BF16),
        pltpu.VMEM((feature, length), BF16),
        pltpu.VMEM((2, length, rows), F32),
        pltpu.VMEM((2, length, rows), BF16),
    ]


def backward_scratch(plan, rows, feature):
    length = plan.n_expert * rows
    return [
        pltpu.VMEM((length, feature), BF16),
        pltpu.VMEM((length, feature), BF16),
        pltpu.VMEM((feature, rows), BF16),
        pltpu.VMEM((rows, feature), BF16),
        pltpu.VMEM((feature, rows), BF16),
        pltpu.VMEM((feature, rows), BF16),
        pltpu.VMEM((2, length, rows), BF16),
    ]


def project_rows(hm, win, k, k_t, v, v_t):
    feature = hm.shape[1]
    w_k, w_v = win[:, feature : 2 * feature], win[:, 2 * feature :]
    k[...] = nn(hm, w_k).astype(BF16)
    v[...] = nn(hm, w_v).astype(BF16)
    k_t[...] = tt(w_k, hm).astype(BF16)
    v_t[...] = tt(w_v, hm).astype(BF16)


def project_query(rows, win):
    return nn(rows, win[:, : rows.shape[1]]).astype(BF16).astype(F32) * HEAD_DIM ** (-0.5)


def attention_shapes(plan, rows, feature):
    length = plan.n_expert * rows
    return [
        ((length, feature), BF16),
        ((feature, length), BF16),
        ((length, feature), BF16),
        ((rows, feature), BF16),
        ((feature, rows), F32),
        ((feature // HEAD_DIM, rows), F32),
    ]


def gather_rows(ids, col, returned):
    me = lax.axis_index("expert")
    total = None
    for r, rows in zip(ids, returned):
        slots = rows.shape[0] * rows.shape[1]
        local = col - xor(me, r) * slots
        hot = (local == lax.broadcasted_iota(jnp.int32, (col.shape[0], slots), 1)).astype(BF16)
        part = nn(hot, rows.reshape(slots, rows.shape[-1]))
        total = part if total is None else total + part
    return total


def fill_buffers(cap, col_of, token_of, sources, dest):
    experts = dest.shape[0]
    slots = experts * cap
    me = lax.axis_index("expert")
    for s in sources:
        for p in range(2):
            local = col_of(s, p) - me * slots
            hot = (local == lax.broadcasted_iota(jnp.int32, (slots, local.shape[1]), 0)).astype(BF16)
            rows = nn(hot, token_of(s, p)).astype(BF16)
            at = (2 * s + p) * cap
            for j in range(experts):
                dest[j, at : at + cap, :] = rows[j * cap : (j + 1) * cap]


def column(ref, s, layer, p):
    return ref[s, pl.ds(2 * layer + p, 1), :]


class Return:
    def __init__(self, ids, stage, ret, send_sems, recv_sems):
        self.ids, self.stage, self.ret, self.sems = ids, stage, ret, (send_sems, recv_sems)

    def copy(self, s, n):
        return send(
            self.stage.at[s, n], self.ret.at[s, n], self.sems[0].at[s, n], self.sems[1].at[s, n], (0, self.ids[s])
        )

    def put(self, j, rows, cap):
        for s in range(len(self.ids)):
            for p in range(2):
                at = (2 * s + p) * cap
                (self.ret if s == 0 else self.stage)[s, j, p] = rows[at : at + cap]

    def start(self, j):
        for s in range(1, len(self.ids)):
            self.copy(s, j).start()

    def finish(self, experts):
        for n in range(experts):
            for s in range(1, len(self.ids)):
                self.copy(s, n).wait()

    def rows(self, p):
        return [self.ret[s, :, p] for s in range(len(self.ids))]


def load(src, dst, sem):
    return pltpu.make_async_copy(src, dst, sem)


def self_forward(plan, source, target, cols, out_grad, gains, inward, outward, jobs):
    ids, count = plan.ids, plan.n_expert
    _, rows, feature = source.shape
    length = count * rows

    def body(bg, *refs):
        src, tgt, col, og, g, win_any, wout_any = refs[:7]
        enc, dec = refs[7:16], refs[16:25]
        u_near, og_near, col_near = refs[25:28]
        near_s, near_t, win, wout, q_t, v_t, raw, low, lsem, *sems = refs[28:]
        weights = [load(win_any.at[n], win.at[n], lsem.at[n]) for n in range(2)]
        weights += [load(wout_any.at[n], wout.at[n], lsem.at[2 + n]) for n in range(2)]
        for w in weights:
            w.start()
        g_s, g_t, g_u, g_og, g_col = [
            Gather(ids, ref, sems[2 * n], sems[2 * n + 1])
            for n, ref in enumerate((near_s, near_t, u_near, og_near, col_near))
        ]
        near_s[0] = src[0]
        near_t[0] = tgt[0]
        col_near[0] = col[...]
        og_near[0] = og[...]
        bg.greet()
        g_s.start()
        g_t.start()
        g_col.start()
        bg.start()

        def attend(near, outs, n, gain, gain_next, causal, first, between):
            after, nxt, hm, k, k_t, v, q, o_t, lse = outs
            norm_rows(near.at[0], hm.at[0:rows], g[gain : gain + 1])
            if n == 0:
                for w in weights:
                    w.wait()
            q_scaled = project_query(hm[0:rows, :], win[n])
            q[...] = q_scaled.astype(BF16)
            first()
            for b in range(1, count):
                norm_rows(near.at[b], hm.at[b * rows : (b + 1) * rows], g[gain : gain + 1])
            project_rows(hm[...], win[n], k, k_t, v, v_t)
            q_t[...] = q_scaled.T.astype(BF16)
            attend_forward(q_t, k, v_t, causal, o_t, lse, (raw, low), [(2, between)])
            merged = o_t[...].T.astype(BF16)
            after[...] = near[0].astype(F32) + nn(merged, wout[n])
            norm_rows(after, nxt, g[gain_next : gain_next + 1])

        def first_enc():
            g_s.forward()
            g_s.finish()
            g_og.start()

        def mid_enc():
            g_t.forward()
            g_col.forward()

        attend(near_s, enc, 0, 0, 1, None, first_enc, mid_enc)
        u_near[0] = enc[1][...]
        g_u.start()

        def mid_dec():
            g_u.forward()
            g_og.forward()

        attend(near_t, dec, 1, 3, 4, (ids, rows), g_t.finish, mid_dec)
        g_u.finish()
        g_og.finish()
        g_col.finish()
        bg.finish()

    shapes = [((rows, feature), F32), ((rows, feature), BF16), ((length, feature), BF16)]
    shapes += attention_shapes(plan, rows, feature)
    outs, fars = fused(
        plan,
        body,
        [source, target, cols, out_grad, gains, inward, outward],
        shapes
        + shapes
        + [
            ((count, rows, feature), BF16),
            ((count, 2, rows, feature), BF16),
            ((count,) + cols.shape, jnp.int32),
        ],
        "self_forward",
        cid=1,
        peers=expert_peers(ids),
        jobs=jobs,
        in_specs=[None] * 5 + [ANYWHERE] * 2,
        scratch=[
            pltpu.VMEM((count, rows, feature), BF16),
            pltpu.VMEM((count, rows, feature), BF16),
            pltpu.VMEM((2, feature, 3 * feature), BF16),
            pltpu.VMEM((2, feature, feature), BF16),
            *forward_scratch(plan, rows, feature),
            DMA((4,)),
        ]
        + [DMA((count,))] * 10,
        us=35,
    )
    return outs[:9], outs[9:18], outs[18:], fars


def return_scratch(plan, experts, cap, feature):
    shape = (plan.n_expert, experts, 2, cap, feature)
    return [pltpu.VMEM(shape, BF16), pltpu.VMEM(shape, BF16), DMA(shape[:2]), DMA(shape[:2])]


def expert_forward(plan, near, col_near, own_col, residual, gains, weight_up, weight_down, jobs):
    ids, count = plan.ids, plan.n_expert
    experts, hidden, feature = weight_up.shape
    rows = near.shape[1]
    cap = 2 * rows // EXPERTS
    length = count * 2 * cap

    def body(bg, u, col, mine, res, g, up, down, out, nxt, buf, act, *scratch):
        j = pl.program_id(0)
        back = Return(ids, *scratch)

        @pl.when(j == 0)
        def _():
            bg.greet()
            bg.start()
            fill_buffers(cap, lambda s, p: col[s, p : p + 1, :], lambda s, p: u[s], range(count), buf)

        for at in range(0, hidden, WIDE):
            raw = nt(buf[j], up[0, at : at + WIDE])
            for n in range(0, length, TALL):
                act[n : n + TALL, at : at + WIDE] = gelu(raw[n : n + TALL]).astype(BF16)
        back.put(j, nn(act[...], down[0]).astype(BF16), cap)
        back.start(j)

        @pl.when(j == experts - 1)
        def _():
            back.finish(experts)
            for p in range(2):
                out[p] = res[...] + gather_rows(ids, mine[p], back.rows(p))
                norm_rows(out.at[p], nxt.at[p], g[2:3])
            bg.finish()

    weight = pl.BlockSpec((1, hidden, feature), lambda j: (j, 0, 0))
    return fused(
        plan,
        body,
        [near, col_near, own_col, residual, gains, weight_up, weight_down],
        [((2, rows, feature), F32), ((2, rows, feature), BF16)],
        "expert_forward",
        cid=2,
        peers=expert_peers(ids),
        jobs=jobs,
        grid=(experts,),
        in_specs=[None] * 5 + [weight, weight],
        scratch=[pltpu.VMEM((experts, length, feature), BF16), pltpu.VMEM((length, hidden), BF16)]
        + return_scratch(plan, experts, cap, feature),
        us=22,
    )


def weight_grads(hq, hm, dq, dk, dv, o_t, d_branch):
    return [tn(hq, dq), tn(hm, dk), tn(hm, dv), nn(o_t.astype(BF16), d_branch)]


def middle(plan, hc, mid, memory, final, cols, own_col, out_grad, og_near, gains, inward, outward, up, down, jobs):
    ids, count = plan.ids, plan.n_expert
    rows, feature = hc.shape
    length = count * rows
    experts, hidden, _ = up.shape
    cap = 2 * rows // EXPERTS
    slots = count * 2 * cap
    heads = feature // HEAD_DIM

    def body(bg, *refs):
        h, t1, mem, e2, g, col, mine, og_own = refs[:8]
        og_any, win_any, wout_any, up_any, down_any = refs[8:13]
        t2_out, w_out, res_out, fg, fg_low, fg_near, dt1, dw, dg2, dg4, dg5 = refs[13:24]
        t2, w_near, result, og, hm, k, k_t, v, q, o_t, lse, q_t, v_t, raw, low, do_t = refs[24:40]
        buf, gbuf, act, slopes, wup, wdown, stage, ret, rs, rr = refs[40:50]
        dk, dv, dq, dq_t, do, parts, got, upstream, win, wout, lsem, wsem, osem = refs[50:63]
        sems = refs[63:]
        weights = [load(win_any.at[2], win, lsem.at[0]), load(wout_any.at[2], wout, lsem.at[1])]
        og_load = load(og_any, og, lsem.at[2])
        gather_m = [Gather(ids, hm.at[p], sems[p].at[0], sems[p].at[1]) for p in range(2)]
        gather_w = [Gather(ids, w_near.at[p], sems[2 + p].at[0], sems[2 + p].at[1]) for p in range(2)]
        gather_f = [Gather(ids, fg_near.at[p], sems[4 + p].at[0], sems[4 + p].at[1]) for p in range(2)]
        scatter = [Scatter(ids, parts.at[p], got.at[p], sems[6 + p].at[0], sems[6 + p].at[1]) for p in range(2)]
        back = Return(ids, stage, ret, rs, rr)
        flushes = [load(t2, t2_out, osem.at[0]), load(w_near, w_out, osem.at[1]), load(result, res_out, osem.at[2])]
        bg.bind(0, w_near)

        def fetch(j):
            return [
                load(up_any.at[j], wup.at[j % 2], wsem.at[0, j % 2]),
                load(down_any.at[j], wdown.at[j % 2], wsem.at[1, j % 2]),
            ]

        for x in weights:
            x.start()
        for p in range(2):
            hm[p, 0] = mem[p]
        bg.greet()
        gather_m[0].start()
        gather_m[1].start()
        bg.start()
        for x in weights:
            x.wait()
        for x in [og_load] + [x for j in range(min(2, experts)) for x in fetch(j)]:
            x.start()
        q_scaled = project_query(h[...], win[...])
        q[...] = q_scaled.astype(BF16)
        q_t[...] = q_scaled.T.astype(BF16)
        gather_m[0].forward()
        gather_m[0].finish()
        for p in range(2):
            project_rows(hm[p].reshape(length, feature), win[...], k.at[p], k_t.at[p], v.at[p], v_t)
            between = gather_m[1].forward if p == 0 else gather_w[0].forward
            attend_forward(q_t, k.at[p], v_t, None, o_t.at[p], lse.at[p], (raw, low), [(2, between)])
            t2[p] = t1[...] + nn(o_t[p].T.astype(BF16), wout[...])
            norm_rows(t2.at[p], w_near.at[p, 0], g[5:6])
            gather_w[p].start()
            if p == 0:
                gather_m[1].finish()
        flushes[0].start()
        og_load.wait()
        column_of = lambda s, p: col[s, 2 + p : 3 + p, :]
        fill_buffers(cap, column_of, lambda s, p: og[s, p], range(count), gbuf)
        bg.start(1)
        gather_w[0].finish()
        gather_w[1].forward()
        gather_w[1].finish()
        bg.start(2)
        flushes[1].start()
        fill_buffers(cap, column_of, lambda s, p: w_near[p, s], range(count), buf)
        for j in range(experts):
            for x in fetch(j):
                x.wait()
            for at in range(0, hidden, WIDE):
                span = slice(at, at + WIDE)
                gelu_pair(
                    nt(buf[j], wup[j % 2, span]), nt(gbuf[j], wdown[j % 2, span]), act.at[:, span], slopes.at[:, span]
                )
            back.put(j, nn(slopes[...], wup[j % 2]).astype(BF16), cap)
            back.start(j)
            res = nn(act[...], wdown[j % 2]).astype(BF16)
            for s in range(count):
                for p in range(2):
                    at = (2 * s + p) * cap
                    result[s, j, p] = res[at : at + cap]
            if j + 2 < experts:
                for x in fetch(j + 2):
                    x.start()
        flushes[2].start()
        bg.start(3)
        back.finish(experts)
        total = None
        for p in range(2):
            upstream[p] = gather_rows(ids, mine[p], back.rows(p))

            def store_up(span, dx):
                upstream[p, span, :] = og_own[p, span, :] + dx

            gain = norm_back_rows(t2.at[p], g[5:6], upstream.at[p], store_up)
            total = gain if total is None else total + gain
        dg5[...] = total
        bg.start(4)

        def memory_back(p):
            fg[p] = scatter[p].finish()

            def store(span, dx):
                fg[p, span, :] = dx
                fg_low[p, span, :] = dx.astype(BF16)
                fg_near[p, 0, span, :] = dx.astype(BF16)

            gain = norm_back_rows(e2.at[p], g[2:3], fg.at[p], store)
            gather_f[p].start()
            if p == 0:
                dg2[...] = gain
            else:
                dg2[...] = dg2[...] + gain

        for p in range(2):
            do[...] = nt(upstream[p].astype(BF16), wout[...]).astype(BF16)
            between = () if p == 0 else ((1, scatter[0].middle), (2, lambda: memory_back(0)), (3, lambda: bg.start(5)))
            attend_backward(
                q, k.at[p], v.at[p], k_t.at[p], do, o_t.at[p], lse.at[p], None, dk.at[p], dv.at[p], dq_t, (q_t, do_t, low), between
            )
            for b in [i for i, r in enumerate(ids) if r % 2] + [i for i, r in enumerate(ids) if r % 2 == 0]:
                span = slice(b * rows, (b + 1) * rows)
                part = nt(dk[p, span, :], win[:, feature : 2 * feature])
                part = part + nt(dv[p, span, :], win[:, 2 * feature :])
                parts[p, b] = part.astype(BF16)
            scatter[p].start()
            dq[p] = dq_t[...].astype(F32).T.astype(BF16)
        scatter[1].middle()
        gather_f[0].forward()
        grads = None
        for p in range(2):
            more = weight_grads(
                h[...], hm[p].reshape(length, feature), dq[p], dk[p], dv[p], o_t[p], upstream[p].astype(BF16)
            )
            grads = more if grads is None else [x + y for x, y in zip(grads, more)]
        for n, value in enumerate(grads):
            dw[:, n * feature : (n + 1) * feature] = value.astype(BF16)
        memory_back(1)
        dt1[...] = nt(dq[0], win[:, :feature]) + nt(dq[1], win[:, :feature])

        def store_mid(span, dx):
            dt1[span, :] = upstream[0, span, :] + upstream[1, span, :] + dx

        dg4[...] = norm_back_rows(t1, g[4:5], dt1, store_mid)
        gather_f[1].forward()
        gather_f[0].finish()
        gather_f[1].finish()
        for x in flushes:
            x.wait()
        bg.finish()

    block = (rows, feature)
    two = (2,) + block
    near = (2, count) + block
    home = (count, experts, 2, cap, feature)
    keys = (2, length, feature)
    low_vmem = lambda *shape: pltpu.VMEM(shape, BF16)
    return fused(
        plan,
        body,
        [hc, mid, memory, final, gains, cols, own_col, out_grad, og_near, inward, outward, up, down],
        [
            (two, F32),
            (near, BF16),
            (home, BF16),
            (two, F32),
            (two, BF16),
            (near, BF16),
            (block, F32),
            ((feature, 4 * feature), BF16),
            ((1, feature), F32),
            ((1, feature), F32),
            ((1, feature), F32),
        ],
        "middle",
        cid=3,
        peers=expert_peers(ids),
        jobs=jobs,
        in_specs=[None] * 8 + [ANYWHERE] * 5,
        out_specs=[ANYWHERE] * 3 + [None] * 8,
        scratch=[
            pltpu.VMEM(two, F32),
            low_vmem(*near),
            low_vmem(*home),
            low_vmem(*og_near.shape),
            low_vmem(*near),
            low_vmem(*keys),
            low_vmem(2, feature, length),
            low_vmem(*keys),
            low_vmem(*block),
            pltpu.VMEM((2, feature, rows), F32),
            pltpu.VMEM((2, heads, rows), F32),
            low_vmem(feature, rows),
            low_vmem(feature, length),
            pltpu.VMEM((2, length, rows), F32),
            low_vmem(2, length, rows),
            low_vmem(feature, rows),
            low_vmem(experts, slots, feature),
            low_vmem(experts, slots, feature),
            low_vmem(slots, hidden),
            low_vmem(slots, hidden),
            low_vmem(2, hidden, feature),
            low_vmem(2, hidden, feature),
            *return_scratch(plan, experts, cap, feature),
            low_vmem(*keys),
            low_vmem(*keys),
            low_vmem(*two),
            low_vmem(feature, rows),
            low_vmem(*block),
            low_vmem(*near),
            low_vmem(*near),
            pltpu.VMEM(two, F32),
            low_vmem(feature, 3 * feature),
            low_vmem(feature, feature),
            DMA((3,)),
            DMA((2, 2)),
            DMA((3,)),
        ]
        + [DMA((2, count))] * 8,
        us=130,
    )


def encoder_experts(plan, u_near, fg_near, col_near, own_col, attended, final_grad, gains, weight_up, weight_down, jobs):
    ids, count = plan.ids, plan.n_expert
    experts, hidden, feature = weight_up.shape
    rows = attended.shape[0]
    cap = 2 * rows // EXPERTS
    length = count * 2 * cap

    def body(bg, u, fgn, col, mine, e1, fg, g, up, down, de1, dg, buf, gbuf, slopes, *scratch):
        j = pl.program_id(0)
        back = Return(ids, *scratch)

        @pl.when(j == 0)
        def _():
            bg.greet()
            bg.start()
            fill_buffers(cap, lambda s, p: col[s, p : p + 1, :], lambda s, p: u[s], range(count), buf)
            fill_buffers(cap, lambda s, p: col[s, p : p + 1, :], lambda s, p: fgn[p, s], range(count), gbuf)

        for at in range(0, hidden, WIDE):
            span = slice(at, at + WIDE)
            gelu_pair(nt(buf[j], up[0, span]), nt(gbuf[j], down[0, span]), None, slopes.at[:, span])
        back.put(j, nn(slopes[...], up[0]).astype(BF16), cap)
        back.start(j)

        @pl.when(j == experts - 1)
        def _():
            back.finish(experts)
            de1[...] = gather_rows(ids, mine[0], back.rows(0)) + gather_rows(ids, mine[1], back.rows(1))

            def store(span, dx):
                de1[span, :] = fg[0, span, :] + fg[1, span, :] + dx

            dg[...] = norm_back_rows(e1, g[1:2], de1, store)
            bg.finish()

    weight = pl.BlockSpec((1, hidden, feature), lambda j: (j, 0, 0))
    return fused(
        plan,
        body,
        [u_near, fg_near, col_near, own_col, attended, final_grad, gains, weight_up, weight_down],
        [((rows, feature), F32), ((1, feature), F32)],
        "encoder_experts",
        cid=6,
        peers=expert_peers(ids),
        jobs=jobs,
        grid=(experts,),
        in_specs=[None] * 7 + [weight, weight],
        scratch=[pltpu.VMEM((experts, length, feature), BF16)] * 2
        + [pltpu.VMEM((length, hidden), BF16)]
        + return_scratch(plan, experts, cap, feature),
        us=30,
    )


def attention_back(plan, ids, n, up, saved, win, wout, work, parts, scatter, dw, causal, between, after):
    hm, k, k_t, v, q, o_t, lse = saved
    dk, dv, dq_t, do, *rest = work
    rows, feature = q.shape
    d_branch = up[...].astype(BF16)
    do[...] = nt(d_branch, wout[...]).astype(BF16)
    attend_backward(q, k, v, k_t, do, o_t, lse, causal, dk, dv, dq_t, rest, between)
    dq = dq_t[...].astype(F32).T.astype(BF16)
    for b in [i for i, r in enumerate(ids) if r % 2] + [i for i, r in enumerate(ids) if r % 2 == 0]:
        span = slice(b * rows, (b + 1) * rows)
        part = nt(dk[span, :], win[:, feature : 2 * feature]) + nt(dv[span, :], win[:, 2 * feature :])
        if b == 0:
            part = part + nt(dq, win[:, :feature])
        parts[b] = part.astype(BF16)
    scatter.start()
    after()
    for i, value in enumerate(
        weight_grads(hm[0:rows, :], hm[...], dq, dk[...], dv[...], o_t[...], d_branch)
    ):
        dw[:, i * feature : (i + 1) * feature] = value.astype(BF16)


def input_back(up, src, gain, scatter, grad):
    grad[...] = scatter.finish()

    def store(span, dx):
        grad[span, :] = up[span, :] + dx

    return norm_back_rows(src.at[0], gain, grad, store)


def attention_scratch(plan, rows, feature):
    count = plan.n_expert
    return [
        *backward_scratch(plan, rows, feature),
        pltpu.VMEM((count, rows, feature), BF16),
        pltpu.VMEM((count, rows, feature), BF16),
        pltpu.VMEM((feature, 3 * feature), BF16),
        pltpu.VMEM((feature, feature), BF16),
    ]


def decoder_backward(plan, dec_up, target, gains, saved, inward, outward, jobs):
    ids, count = plan.ids, plan.n_expert
    _, rows, feature = target.shape

    def body(bg, *refs):
        up, src, g = refs[:3]
        saved_refs, win_any, wout_any = refs[3:10], refs[10], refs[11]
        grad, dw, dg = refs[12:15]
        *work, parts, got, win, wout, lsem, sems = refs[15:]
        weights = [load(win_any.at[1], win, lsem.at[0]), load(wout_any.at[1], wout, lsem.at[1])]
        for x in weights:
            x.start()
        bg.greet()
        bg.start()
        for x in weights:
            x.wait()
        scatter = Scatter(ids, parts, got, sems.at[0], sems.at[1])
        attention_back(
            plan, ids, 1, up, saved_refs, win, wout, work, parts, scatter, dw, (ids, rows), (), lambda: None
        )
        scatter.middle()
        bg.start(1)
        dg[...] = input_back(up, src, g[3:4], scatter, grad)
        bg.finish()

    return fused(
        plan,
        body,
        [dec_up, target, gains, *saved, inward, outward],
        [((rows, feature), F32), ((feature, 4 * feature), BF16), ((1, feature), F32)],
        "decoder_backward",
        cid=7,
        peers=expert_peers(ids),
        jobs=jobs,
        in_specs=[None] * 10 + [ANYWHERE] * 2,
        scratch=attention_scratch(plan, rows, feature) + [DMA((2,)), DMA((2, count))],
        us=28,
    )


def last(plan, enc_up, source, gains, saved, inward, outward, sums, small, tokens, grads, cols, up, down, home, jobs):
    ids, count, ny, nz = plan.ids, plan.n_expert, plan.ny, plan.nz
    _, rows, feature = source.shape
    width = 4 * feature
    groups = column_groups(width)
    steps = 1 + len(AllReduce.rotations(plan)[0])
    n_dw = len(sums) + 1
    result, own_col, crossed = home
    experts, hidden, _ = up.shape
    cap = 2 * rows // EXPERTS
    sources = count * nz
    length = sources * 2 * cap
    span = hidden // plan.n_dp
    block = ny * span

    def body(bg, *refs):
        ups, src, g, sm = refs[:4]
        saved_refs, cn, cf, mine, t2 = refs[4:11], refs[11], refs[12], refs[13], refs[14]
        win_any, wout_any, up_any, down_any, res_any = refs[15:20]
        big, sums_any = refs[20:24], refs[24 : 23 + n_dw]
        grad, sum_out, small_out, up_own, down_own, got_out, y_out = refs[23 + n_dw : 30 + n_dw]
        rest = refs[30 + n_dw :]
        *work, parts, got, win, wout = rest[:11]
        near, far = rest[11:13]
        wup, wdown, buf, gbuf, act, slopes, ret, acc, tmp, small_tmp = rest[13:23]
        lsem, asem, ssem, credits, ysem, rs, rr, sems, osem = rest[23:]
        weights = [load(win_any.at[0], win, lsem.at[0]), load(wout_any.at[0], wout, lsem.at[1])]
        first = pl.multiple_of(lax.div(lax.axis_index("dp"), ny) * block, block)
        firsts = [load(ref, acc.at[n], lsem.at[2 + n]) for n, ref in enumerate(sums_any)]
        at = 1 + n_dw
        held = (near.at[0], far.at[:, :, 0], near, far)
        bigs = [load(a, b, lsem.at[at + n]) for n, (a, b) in enumerate(zip(big, held))]
        bigs.append(load(up_any.at[:, pl.ds(first, block)], wup, lsem.at[at + 4]))
        bigs.append(load(down_any.at[:, pl.ds(first, block)], wdown, lsem.at[at + 5]))
        own = load(res_any.at[0], ret.at[0], lsem.at[at + 6])
        bring = [send(res_any.at[s], ret.at[s], rs.at[s], rr.at[s], (0, ids[s])) for s in range(1, count)]
        for x in weights + firsts + bigs[:2] + bigs[4:] + [own]:
            x.start()
        small_out[...] = sm[...]
        bg.greet()

        def reduce(n):
            return AllReduce(
                plan, acc.at[n : n + 1], groups, tmp.at[n : n + 1], None, None, asem.at[n], None, credits.at[n]
            ).run()

        for x in firsts:
            x.wait()
        others = [reduce(n) for n in range(n_dw - 1)]
        mine_run, waiting = [], []

        def step(n=1):
            for run in mine_run + others:
                next(run, None)
            for _ in range(n):
                if bg.released < bg.paced():
                    bg.release(1)
                elif waiting:
                    waiting.pop(0).start()

        step(2)
        bg.start()

        def after():
            step()
            for x in bring:
                x.start()

        for x in weights:
            x.wait()
        scatter = Scatter(ids, parts, got, sems.at[0], sems.at[1])
        attention_back(
            plan, ids, 0, ups, saved_refs, win, wout, work, parts, scatter, acc.at[n_dw - 1], None, ((2, lambda: step(0)),), after
        )
        mine_run.append(reduce(n_dw - 1))
        step()
        scatter.middle()
        col_of, token_of, grad_of = weight_sources(plan, 0, held[0:2], held[2:4], (cn, cf))
        bigs[0].wait()
        bigs[1].wait()
        fill_buffers(cap, col_of, token_of, range(sources), buf)
        for x in bigs[2:4]:
            x.start()
        small_out[0:1, :] = input_back(ups, src, g[0:1], scatter, grad)
        mine_run.append(AllReduce(plan, acc, [], None, small_out, small_tmp, None, ssem).run())
        step()
        for x in bigs[2:]:
            x.wait()
        fill_buffers(cap, col_of, grad_of, range(sources), gbuf)
        step()
        y = lax.rem(lax.axis_index("dp"), ny)

        def stage(r, j, n):
            at = ((r - 1) * experts + j) * 2 + n
            return (parts if at < count else got).at[at % count, pl.ds(0, span)]

        def to_y(r, j, n):
            return send(
                stage(r, j, n), got_out.at[r - 1, j, n], ysem.at[0, r - 1, j, n], ysem.at[1, r - 1, j, n], (r, 0)
            )

        flushes = []
        for r in reversed(range(ny)):
            place = pl.ds(pl.multiple_of(xor(y, r) * span, span), span)
            for j in range(experts):
                products = weight_products(
                    wup[j, place, :], wdown[j, place, :], buf.at[j], gbuf.at[j], act, slopes
                )
                for n, value in enumerate(products):
                    if r == 0:
                        here = far.at[0, j, n, pl.ds(0, span)]
                        here[...] = value
                        flush = load(here, (up_own, down_own)[n].at[j], osem.at[j, n])
                        flush.start()
                        flushes.append(flush)
                    else:
                        stage(r, j, n)[...] = value
                        waiting.append(to_y(r, j, n))
                if j % 2:
                    step()
        own.wait()
        for x in bring:
            x.wait()
        for p in range(2):
            mixed = gather_rows(ids, mine[p], [ret[s, :, p] for s in range(count)])
            y_out[p] = (t2[p] + mixed).astype(BF16)
        for _ in range(2 * steps):
            step()
        for run in others:
            for _ in run:
                pass
        while waiting:
            waiting.pop(0).start()
        final = load(acc, sum_out, lsem.at[0])
        final.start()
        for r in range(1, ny):
            for j in range(experts):
                for n in range(2):
                    to_y(r, j, n).wait()
        for x in flushes + [final]:
            x.wait()
        bg.finish()

    peers = expert_peers(ids)
    peers = peers + [p for p in AllReduce.peers(plan) + [(r, 0) for r in range(1, ny)] if p not in peers]
    big = [*tokens, *grads]
    own_block = (experts, span, feature)
    pair = (ny - 1, experts, 2, span, feature)
    return fused(
        plan,
        body,
        [enc_up, source, gains, small, *saved, *cols, own_col, crossed, inward, outward, up, down, result, *big, *sums],
        [
            ((rows, feature), F32),
            ((n_dw, feature, width), BF16),
            (small.shape, F32),
            (own_block, BF16),
            (own_block, BF16),
            (pair, BF16),
            ((2, rows, feature), BF16),
        ],
        "last",
        cid=9,
        peers=list(dict.fromkeys(peers)),
        jobs=jobs,
        in_specs=[None] * 15 + [ANYWHERE] * (9 + len(sums)),
        out_specs=[None, ANYWHERE, None, ANYWHERE, ANYWHERE, ANYWHERE, None],
        scratch=attention_scratch(plan, rows, feature)
        + [pltpu.VMEM(a.shape, BF16) for a in grads]
        + [
            pltpu.VMEM((experts, block, feature), BF16),
            pltpu.VMEM((experts, block, feature), BF16),
            pltpu.VMEM((experts, length, feature), BF16),
            pltpu.VMEM((experts, length, feature), BF16),
            pltpu.VMEM((span, length), BF16),
            pltpu.VMEM((span, length), BF16),
            pltpu.VMEM(result.shape, BF16),
            pltpu.VMEM((n_dw, feature, width), BF16),
            pltpu.VMEM((n_dw, AllReduce.tmp_rows(plan, feature), width), BF16),
            pltpu.VMEM((steps,) + small.shape, F32),
            DMA((8 + n_dw,)),
            DMA((n_dw, 4, len(groups), steps)),
            DMA((2, steps)),
            pltpu.SemaphoreType.REGULAR((n_dw, len(groups), steps)),
            DMA((2, ny - 1, experts, 2)),
            DMA((count,)),
            DMA((count,)),
            DMA((2, count)),
            DMA((experts, 2)),
        ],
        us=110,
    )


def column_groups(width):
    small, large = width * 3 // 16 // 128 * 128, width // 2 // 128 * 128
    return [(0, 0, large), (0, large, width - large - small), (0, width - small, small)]


def weight_sources(plan, layer, tokens, grads, cols):
    count = plan.n_expert

    def col_of(s, p):
        row = slice(2 * layer + p, 2 * layer + p + 1)
        return cols[0][s, row, :] if s < count else cols[1][s // count - 1, s % count, row, :]

    def token_of(s, p):
        if layer == 0:
            return tokens[0][s] if s < count else tokens[1][s // count - 1, s % count]
        return tokens[0][p, s] if s < count else tokens[1][s // count - 1, s % count, p]

    def grad_of(s, p):
        if s < count:
            return grads[0][p, s] if layer == 0 else grads[0][s, p]
        return grads[1][s // count - 1, s % count, p]

    return col_of, token_of, grad_of


def weight_products(up, down, buf, gbuf, act, slopes):
    for at in range(0, buf.shape[0], WIDE):
        span = slice(at, at + WIDE)
        gelu_pair(nt(up, buf[span, :]), nt(down, gbuf[span, :]), act.at[:, span], slopes.at[:, span])
    return nn(slopes[...], buf[...]).astype(BF16), nn(act[...], gbuf[...]).astype(BF16)


def expert_weights(plan, layer, cid, tokens, grads, cols, weight_up, weight_down, jobs):
    count, ny, nz, ids = plan.n_expert, plan.ny, plan.nz, plan.ids
    experts, hidden, feature = weight_up.shape
    rows = tokens[0].shape[-2]
    cap = 2 * rows // EXPERTS
    sources = count * nz
    length = sources * 2 * cap
    span = hidden // plan.n_dp
    block = ny * span

    def body(bg, *refs):
        cn, cf = refs[:2]
        big, up_any, down_any = refs[n_small : n_small + 4], refs[n_small + 4], refs[n_small + 5]
        outs = refs[n_in:]
        up_out, down_out = outs[:2]
        held, (up, down, buf, gbuf, act, slopes, lsem) = outs[n_out : n_out + 4], outs[n_out + 4 : n_out + 11]
        first = pl.multiple_of(lax.div(lax.axis_index("dp"), ny) * block, block)
        loads = [load(src, dst, lsem.at[n]) for n, (src, dst) in enumerate(zip(big, held))]
        loads.append(load(up_any.at[:, pl.ds(first, block)], up, lsem.at[4]))
        loads.append(load(down_any.at[:, pl.ds(first, block)], down, lsem.at[5]))
        for x in loads:
            x.start()
        bg.greet()
        bg.start()
        col_of, token_of, grad_of = weight_sources(plan, layer, held[0:2], held[2:4], (cn, cf))
        for n, (reader, dest) in enumerate(((token_of, buf), (grad_of, gbuf))):
            loads[2 * n].wait()
            fill_buffers(cap, col_of, reader, range(count), dest)
            loads[2 * n + 1].wait()
            fill_buffers(cap, col_of, reader, range(count, sources), dest)
        loads[4].wait()
        loads[5].wait()
        y = lax.rem(lax.axis_index("dp"), ny)
        for r in reversed(range(ny)):
            at = pl.ds(pl.multiple_of(xor(y, r) * span, span), span)

            def product(j, _):
                up_out[r, j], down_out[r, j] = weight_products(
                    up[j, at, :], down[j, at, :], buf.at[j], gbuf.at[j], act, slopes
                )
                return 0

            lax.fori_loop(0, experts, product, 0)
        bg.finish()

    small = [*cols]
    n_small = len(small)
    big = [tokens[0], tokens[1], grads[0], grads[1], weight_up, weight_down]
    n_in = n_small + len(big)
    outs = [((ny, experts, span, feature), BF16)] * 2
    n_out = len(outs)
    scratch = [pltpu.VMEM(a.shape, BF16) for a in big[:4]] + [
        pltpu.VMEM((experts, block, feature), BF16),
        pltpu.VMEM((experts, block, feature), BF16),
        pltpu.VMEM((experts, length, feature), BF16),
        pltpu.VMEM((experts, length, feature), BF16),
        pltpu.VMEM((span, length), BF16),
        pltpu.VMEM((span, length), BF16),
        DMA((6,)),
    ]
    return fused(
        plan,
        body,
        small + big,
        outs,
        ("encoder", "decoder")[layer] + "_weights",
        cid=cid,
        peers=[],
        jobs=jobs,
        in_specs=[None] * n_small + [ANYWHERE] * len(big),
        scratch=scratch,
        us=25,
    )


def finish(plan, sums, dec, dec_got, enc, enc_got, others_out):
    n_dw, feature, width = sums.shape
    experts, span, _ = enc[0].shape
    parts = 2
    part, some = feature // (experts * parts), span // parts
    ny = plan.ny

    def body(s, du, dd, dug, ddg, eu, ed, eg, p0, p1, p2, a_in, a_out, eu_out, ed_out, du_out, dd_out, q0, q1, q2):
        q0[...], q1[...], q2[...] = p0[...], p1[...], p2[...]
        for n in range(n_dw):
            a_in[n] = s[n_dw - 1 - n, :, : 3 * feature].astype(F32)
            a_out[n] = s[n_dw - 1 - n, :, 3 * feature :].astype(F32)
        for out, own, others in (
            (eu_out, eu[0], [eg[r, 0, 0] for r in range(ny - 1)]),
            (ed_out, ed[0], [eg[r, 0, 1] for r in range(ny - 1)]),
            (du_out, du[0, 0], [dug[r, 0] for r in range(ny - 1)]),
            (dd_out, dd[0, 0], [ddg[r, 0] for r in range(ny - 1)]),
        ):
            total = own.astype(F32)
            for other in others:
                total = total + other.astype(F32)
            out[0] = total

    block = (1, some, feature)
    first = pl.BlockSpec((1,) + block, lambda j, i: (0, j, i, 0))
    others = pl.BlockSpec((ny - 1,) + block, lambda j, i: (0, j, i, 0))
    own = pl.BlockSpec(block, lambda j, i: (j, i, 0))
    rows = lambda w: pl.BlockSpec((n_dw, part, w), lambda j, i: (0, j * parts + i, 0))
    tokens = others_out[0].shape[0] // (experts * parts)
    flat = pl.BlockSpec((tokens, feature), lambda j, i: (j * parts + i, 0))
    handed = [flat, flat, pl.BlockSpec((2, tokens, feature), lambda j, i: (0, j * parts + i, 0))]
    return fused(
        plan,
        body,
        [sums, *dec, *dec_got, *enc, enc_got, *others_out],
        [((n_dw, feature, 3 * feature), F32), ((n_dw, feature, feature), F32)] + [((experts, span, feature), F32)] * 4
        + [(a.shape, a.dtype) for a in others_out],
        "finish",
        grid=(experts, parts),
        in_specs=[
            rows(width),
            first,
            first,
            others,
            others,
            own,
            own,
            pl.BlockSpec((ny - 1, 1, 2, some, feature), lambda j, i: (0, j, 0, i, 0)),
            *handed,
        ],
        out_specs=[rows(3 * feature), rows(feature)] + [own] * 4 + handed,
        us=10,
    )[0]


def local(
    plan,
    source,
    target,
    attention_in,
    attention_out,
    gains,
    encoder_up,
    encoder_down,
    decoder_up,
    decoder_down,
    encoder_route,
    encoder_slot,
    decoder_route,
    decoder_slot,
    output_grad,
):
    _, rows, feature = source.shape
    cap = 2 * rows // EXPERTS
    zr = plan.zr
    za, zb, zc = zr[0::3], zr[1::3], zr[2::3]
    weights = (attention_in, attention_out)

    cols = jnp.stack([encoder_route * cap + encoder_slot, decoder_route * cap + decoder_slot]).reshape(4, rows)
    own_cols = cols.reshape(2, 2, rows, 1)
    out_grad = output_grad.reshape(2, rows, feature)
    og = out_grad.astype(BF16)

    counts = jnp.sum(
        (
            jnp.stack([encoder_route, decoder_route]).reshape(4, rows, 1) == jnp.arange(EXPERTS, dtype=jnp.int32)
        ).astype(F32),
        axis=1,
    )

    enc, dec, (u_near, og_near, col_near), (col_far, og_far) = self_forward(
        plan, source, target, cols, og, gains, *weights, [Job(cols, None, z=zr), Job(og, None, z=za + zb)]
    )
    e1, u, *enc_saved = enc
    t1, hc, *dec_saved = dec
    (e2, memory), (col_far,) = expert_forward(
        plan,
        u_near,
        col_near,
        own_cols[0],
        e1,
        gains,
        encoder_up,
        encoder_down,
        [Job(None, col_far, x=zr)],
    )
    (t2, w_near, result, fg, fg_low, fg_near, dt1, cross_dw, dg2, dg4, dg5), (w_far, col_far, u_far, og_far) = middle(
        plan,
        hc,
        t1,
        memory,
        e2,
        col_near,
        own_cols[1],
        out_grad,
        og_near,
        gains,
        *weights,
        decoder_up,
        decoder_down,
        [
            Job(
                og,
                None,
                later=[(2, "z", zb + zc + za), (2, "s", za), (4, "x", zb), (5, "x", zc)],
                by_pass=True,
                local=True,
            ),
            Job(None, col_far, c=zr),
            Job(u, None, z=zr),
            Job(og, og_far, z=zc, s=za, near=og_near, later=[(1, "x", zb), (2, "c", za), (3, "x", zc)]),
        ],
    )
    (de1, dg1), (w_far, og_far, fg_far) = encoder_experts(
        plan,
        u_near,
        fg_near,
        col_near,
        own_cols[0],
        e1,
        fg,
        gains,
        encoder_up,
        encoder_down,
        [Job(None, w_far, c=zr), Job(None, og_far, c=zb + zc), Job(fg_low, None, z=za + zb)],
    )
    dec_g, (fg_far,) = expert_weights(
        plan,
        1,
        8,
        (w_near, w_far),
        (og_near, og_far),
        (col_near, col_far),
        decoder_up,
        decoder_down,
        [Job(fg_low, fg_far, z=zc, x=za + zb)],
    )
    (target_grad, dec_dw, dg3), (fg_far, u_far, up_got) = decoder_backward(
        plan,
        dt1,
        target,
        gains,
        dec_saved,
        *weights,
        [
            Job(None, fg_far, x=zc, c=za + zb, later=[(1, "c", zc)]),
            Job(None, u_far, s=zr, near=u_near, later=[(1, "c", zr)]),
            Swap(dec_g[0]),
        ],
    )
    count_row = jnp.pad(counts.reshape(1, -1), ((0, 1), (0, feature - counts.size)))
    small = jnp.concatenate([jnp.zeros_like(dg1), dg1, dg2, dg3, dg4, dg5, count_row], axis=0)
    (source_grad, sums, small, up_own, down_own, enc_got, decoder_output), (down_got,) = last(
        plan,
        de1,
        source,
        gains,
        enc_saved,
        *weights,
        [cross_dw, dec_dw],
        small,
        (u_near, u_far),
        (fg_near, fg_far),
        (col_near, col_far),
        encoder_up,
        encoder_down,
        (result, own_cols[1], t2),
        [Swap(dec_g[1], paced=True)],
    )
    a_in, a_out, enc_up_g, enc_down_g, dec_up_g, dec_down_g, source_grad, target_grad, decoder_output = finish(
        plan,
        sums,
        dec_g,
        (up_got, down_got),
        (up_own, down_own),
        enc_got,
        (source_grad, target_grad, decoder_output),
    )
    return (
        decoder_output.reshape(2, 1, rows, feature),
        source_grad[None],
        target_grad[None],
        a_in,
        a_out,
        small[:6],
        enc_up_g,
        enc_down_g,
        dec_up_g,
        dec_down_g,
        small[6, : counts.size].reshape(2, 2, EXPERTS).astype(jnp.int32),
    )


def solution(mesh):
    plan = Plan(mesh.shape["dp"], mesh.shape["expert"])
    in_specs = (
        P("dp", "expert", None),
        P("dp", "expert", None),
        P(),
        P(),
        P(),
        P("expert", None, None),
        P("expert", None, None),
        P("expert", None, None),
        P("expert", None, None),
        P(None, "dp", "expert"),
        P(None, "dp", "expert"),
        P(None, "dp", "expert"),
        P(None, "dp", "expert"),
        P(None, "dp", "expert", None),
    )
    out_specs = (
        P(None, "dp", "expert", None),
        P("dp", "expert", None),
        P("dp", "expert", None),
        P(),
        P(),
        P(),
        P("expert", "dp", None),
        P("expert", "dp", None),
        P("expert", "dp", None),
        P("expert", "dp", None),
        P(),
    )
    return jax.shard_map(
        functools.partial(local, plan),
        mesh=mesh,
        in_specs=in_specs,
        out_specs=out_specs,
        check_vma=False,
    )
```
